32 devices in a mesh: group: 2 (over core), tok: 4 (over y, x), head: 4 (over z).
Axes of the slice: x: 2, y: 2, z: 4, core: 2. Of those that a mesh axis runs over, the one named last changes fastest.
Arguments:
- streams: bfloat16 [2, 4096, 2240], P(None, ('group', 'tok'), 'head'), may hold values from -6 to 6
- w_query: bfloat16 [2240, 2240], P(None, 'head'), may hold values from -0.125 to 0.125
- w_key: bfloat16 [2240, 2240], P(None, 'head'), may hold values from -0.125 to 0.125
- w_value: bfloat16 [2240, 2240], P(None, 'head'), may hold values from -0.125 to 0.125
- gain: float32 [2240], P('head'), may hold values from 0.25 to 1.75
Outputs:
- attended: bfloat16 [2, 4096, 2240], P(None, ('group', 'tok'), 'head')
The draws below stay inside these ranges and needn't reach their ends.
All inputs are finite; a program needn't handle non-finite values.
Results may differ from the reference program's by a relative error of at most 0.0053.
Values may be sent and summed in bfloat16 or wider, within the bound.
No kernel may reach another device: no remote copies, remote signals or barrier semaphores. Data moves between devices by JAX's collectives and lax.ppermute only.
A program may use at most 64 MiB of HBM per device.

```python
import jax
import jax.numpy as jnp
from jax import lax

D = 2240
HEADS = 20
HEAD_DIM = 112
TOK_DEV = 512
TOKENS = 4096
N_GROUP = 2
N_TOK = 4


def block_levels(stream_key, extent, shards, least, largest):
    level = 1.0
    for position, blocks in shards:
        heights = jax.random.uniform(jax.random.fold_in(jax.random.fold_in(stream_key, 6), position), (blocks,), jnp.float32, least / len(shards), largest / len(shards))
        level = level * jnp.repeat(jnp.exp(heights), extent[position] // blocks).reshape((-1,) + (1,) * (len(extent) - 1 - position))
    return level


def normal_values(rng, shape, width, limit, split=(), kind=jnp.bfloat16):
    entries = width * jax.random.normal(rng, shape, jnp.float32)
    if split:
        entries = entries * block_levels(rng, shape, split, -0.22, 0.18)
    return jnp.clip(entries, -limit, limit).astype(kind)


def setup_inputs(seed: int = 0) -> dict:
    splits = jax.random.split(jax.random.key(seed), 6)
    return {
        "streams": normal_values(splits[0], (2, TOKENS, D), 1.0, 6.0, ((1, 8), (2, 4))),
        "w_query": normal_values(splits[1], (D, D), D ** -0.5, 0.125, ((1, 4),)),
        "w_key": normal_values(splits[2], (D, D), D ** -0.5, 0.125, ((1, 4),)),
        "w_value": normal_values(splits[3], (D, D), D ** -0.5, 0.125, ((1, 4),)),
        "gain": jnp.clip(1.0 + 0.15 * jax.random.normal(splits[4], (D,), jnp.float32), 0.25, 1.75),
    }


def project(block, matrix):
    return jnp.dot(block, matrix, preferred_element_type=jnp.float32).astype(jnp.bfloat16)

def group_state(key_rows, value_rows):
    key_heads = jnp.maximum(key_rows, 0).astype(jnp.float32).reshape(-1, HEADS, HEAD_DIM)
    value_heads = value_rows.astype(jnp.float32).reshape(-1, HEADS, HEAD_DIM)
    return jnp.einsum('tha,thb->hab', key_heads, value_heads, precision=lax.Precision.HIGHEST)

def read_norm(query_rows, totals, gain):
    query_heads = jnp.maximum(query_rows, 0).astype(jnp.float32).reshape(-1, HEADS, HEAD_DIM)
    reading = jnp.einsum('tha,hab->thb', query_heads, totals, precision=lax.Precision.HIGHEST)
    scale = lax.rsqrt(lax.optimization_barrier(jnp.mean(reading * reading, axis=-1, keepdims=True)) + 1e-06)
    normed = reading * scale * gain.reshape(HEADS, HEAD_DIM)
    return normed.reshape(-1, D).astype(jnp.bfloat16)

def reference(streams, w_query, w_key, w_value, gain):
    group_len = TOK_DEV * N_TOK
    clean_blocks = streams[0].reshape(N_GROUP, group_len, D)
    noisy_blocks = streams[1].reshape(N_GROUP, group_len, D)

    def step(prefix, blocks):
        clean, noisy = blocks
        clean_state = group_state(project(clean, w_key), project(clean, w_value))
        noisy_state = group_state(project(noisy, w_key), project(noisy, w_value))
        clean_out = read_norm(project(clean, w_query), prefix + clean_state, gain)
        noisy_out = read_norm(project(noisy, w_query), prefix + noisy_state, gain)
        return (prefix + clean_state, (clean_out, noisy_out))
    start = jnp.zeros((HEADS, HEAD_DIM, HEAD_DIM), jnp.float32)
    final, outputs = lax.scan(step, start, (clean_blocks, noisy_blocks))
    clean_all = outputs[0].reshape(N_GROUP * group_len, D)
    noisy_all = outputs[1].reshape(N_GROUP * group_len, D)
    return jnp.stack([clean_all, noisy_all], axis=0)
```

```python
import jax
import jax.numpy as jnp
from jax import lax
from jax.sharding import PartitionSpec as P

HEAD_DIM = 112


def gather_blocks(block, axis):
    count, mine = lax.axis_size(axis), lax.axis_index(axis)
    up = [(i, i + 1) for i in range(count - 1)]
    down = [(i + 1, i) for i in range(count - 1)]
    rising, falling = [block], [block]
    for _ in range(count - 1):
        rising.append(lax.ppermute(rising[-1], axis, up))
        falling.append(lax.ppermute(falling[-1], axis, down))
    rows = block.shape[0]
    whole = jnp.zeros((rows * count,) + block.shape[1:], block.dtype)
    whole = lax.dynamic_update_slice_in_dim(whole, block, mine * rows, 0)
    for back in range(1, count):
        piece = jnp.where(mine >= back, rising[back], falling[count - back])
        place = lax.rem(mine - back + count, count)
        whole = lax.dynamic_update_slice_in_dim(whole, piece, place * rows, 0)
    return whole


def sum_over(value, axis):
    count = lax.axis_size(axis)
    half = value.shape[0] // 2
    steps = [1 << b for b in range(count.bit_length() - 1)]
    outs = []
    for part, order in ((value[:half], steps), (value[half:], steps[::-1])):
        for step in order:
            sent = lax.ppermute(part.astype(jnp.bfloat16), axis, [(i, i ^ step) for i in range(count)])
            part = part + sent.astype(jnp.float32)
        outs.append(part)
    return jnp.concatenate(outs, axis=0)


def entering(value, axis):
    count, mine = lax.axis_size(axis), lax.axis_index(axis)
    total = lax.ppermute(value, axis, [(i, i + 1) for i in range(count - 1)])
    reach = 1
    while reach < count - 1:
        total = total + lax.ppermute(total, axis, [(i, i + reach) for i in range(count - reach)])
        reach *= 2
    return total


def project(matrix, block):
    return jnp.dot(matrix, block, preferred_element_type=jnp.float32).astype(jnp.bfloat16)


def local(streams, w_query, w_key, w_value, gain):
    width = w_query.shape[1]
    heads = width // HEAD_DIM
    tokens = streams.shape[1]
    columns = jnp.swapaxes(streams, 1, 2)
    w_query, w_key, w_value = w_query.T, w_key.T, w_value.T
    gain_heads = gain.reshape(heads, HEAD_DIM, 1)
    prefix, results = None, []
    for stream in range(2):
        features = gather_blocks(columns[stream], "head")
        key = jnp.maximum(project(w_key, features), 0).reshape(heads, HEAD_DIM, tokens)
        value = project(w_value, features).reshape(heads, HEAD_DIM, tokens)
        query = jnp.maximum(project(w_query, features), 0).reshape(heads, HEAD_DIM, tokens)
        state = jnp.einsum("hat,hbt->hba", key, value, preferred_element_type=jnp.float32)
        state = sum_over(state.reshape(width, HEAD_DIM), "tok")
        if stream == 0:
            prefix = entering(state, "group")
        total = (prefix + state).reshape(heads, HEAD_DIM, HEAD_DIM).astype(jnp.bfloat16)
        reading = jnp.einsum("hba,hat->hbt", total, query, preferred_element_type=jnp.float32)
        scale = lax.rsqrt(jnp.mean(reading * reading, axis=1, keepdims=True) + 1e-06)
        normed = reading * scale * gain_heads
        results.append(normed.astype(jnp.bfloat16).reshape(width, tokens))
    return jnp.swapaxes(jnp.stack(results), 1, 2)


def solution(mesh):
    return jax.shard_map(
        local,
        mesh=mesh,
        in_specs=(
            P(None, ("group", "tok"), "head"),
            P(None, "head"),
            P(None, "head"),
            P(None, "head"),
            P("head"),
        ),
        out_specs=P(None, ("group", "tok"), "head"),
        check_vma=False,
    )
```

```python
import jax
import jax.numpy as jnp
from jax import lax
from jax.sharding import PartitionSpec as P

HEAD_DIM = 112


def swap(value, axis, pairs):
    ends = dict(pairs) | {j: i for i, j in pairs}
    count = lax.axis_size(axis)
    return lax.ppermute(value, axis, [(i, ends.get(i, i)) for i in range(count)])


def gather_blocks(block, axis):
    count, mine = lax.axis_size(axis), lax.axis_index(axis)
    if count != 4:
        return lax.all_gather(block, axis, axis=0, tiled=True)
    partners, middle = [(0, 1), (2, 3)], [(1, 2)]
    near = swap(block, axis, partners)
    across = swap(block, axis, middle)
    far = swap(near, axis, middle)
    across_end = swap(across, axis, partners)
    far_end = swap(far, axis, partners)
    inner = (mine == 1) | (mine == 2)
    second = jnp.where(inner, far, across_end)
    third = jnp.where(inner, across, far_end)
    rows = block.shape[0]
    whole = jnp.zeros((rows * count,) + block.shape[1:], block.dtype)
    for flip, piece in enumerate((block, near, second, third)):
        whole = lax.dynamic_update_slice_in_dim(whole, piece, (mine ^ flip) * rows, 0)
    return whole


def sum_over(value, axis):
    count = lax.axis_size(axis)
    half = value.shape[0] // 2
    steps = [1 << b for b in range(count.bit_length() - 1)]
    outs = []
    for part, order in ((value[:half], steps), (value[half:], steps[::-1])):
        for step in order:
            sent = lax.ppermute(part.astype(jnp.bfloat16), axis, [(i, i ^ step) for i in range(count)])
            part = part + sent.astype(jnp.float32)
        outs.append(part)
    return jnp.concatenate(outs, axis=0)


def entering(value, axis):
    count, mine = lax.axis_size(axis), lax.axis_index(axis)
    total = lax.ppermute(value, axis, [(i, i + 1) for i in range(count - 1)])
    reach = 1
    while reach < count - 1:
        total = total + lax.ppermute(total, axis, [(i, i + reach) for i in range(count - reach)])
        reach *= 2
    return total


def project(matrix, block):
    return jnp.dot(matrix, block, preferred_element_type=jnp.float32).astype(jnp.bfloat16)


def local(streams, w_query, w_key, w_value, gain):
    width = w_query.shape[1]
    heads = width // HEAD_DIM
    tokens = streams.shape[1]
    columns = jnp.swapaxes(streams, 1, 2)
    w_query, w_key, w_value = w_query.T, w_key.T, w_value.T
    gain_heads = gain.reshape(heads, HEAD_DIM, 1)
    prefix, results = None, []
    for stream in range(2):
        features = gather_blocks(columns[stream], "head")
        key = jnp.maximum(project(w_key, features), 0).reshape(heads, HEAD_DIM, tokens)
        value = project(w_value, features).reshape(heads, HEAD_DIM, tokens)
        query = jnp.maximum(project(w_query, features), 0).reshape(heads, HEAD_DIM, tokens)
        state = jnp.einsum("hat,hbt->hba", key, value, preferred_element_type=jnp.float32)
        state = sum_over(state.reshape(width, HEAD_DIM), "tok")
        if stream == 0:
            prefix = entering(state, "group")
        total = (prefix + state).reshape(heads, HEAD_DIM, HEAD_DIM).astype(jnp.bfloat16)
        reading = jnp.einsum("hba,hat->hbt", total, query, preferred_element_type=jnp.float32)
        scale = lax.rsqrt(jnp.mean(reading * reading, axis=1, keepdims=True) + 1e-06)
        normed = reading * scale * gain_heads
        results.append(normed.astype(jnp.bfloat16).reshape(width, tokens))
    return jnp.swapaxes(jnp.stack(results), 1, 2)


def solution(mesh):
    return jax.shard_map(
        local,
        mesh=mesh,
        in_specs=(
            P(None, ("group", "tok"), "head"),
            P(None, "head"),
            P(None, "head"),
            P(None, "head"),
            P("head"),
        ),
        out_specs=P(None, ("group", "tok"), "head"),
        check_vma=False,
    )
```

```python
import jax
import jax.numpy as jnp
from jax import lax
from jax.sharding import PartitionSpec as P

HEAD_DIM = 112


def partner_swap(value, axis):
    return lax.ppermute(value, axis, [(i, i ^ 1) for i in range(lax.axis_size(axis))])


def middle_swap(value, axis, other):
    wide, count = lax.axis_size(other), lax.axis_size(axis)
    pairs = []
    for j in range(wide):
        for i in range(count):
            if i in (1, 2):
                pairs.append((j * count + i, j * count + 3 - i))
            else:
                pairs.append((j * count + i, (j ^ 1 if j ^ 1 < wide else j) * count + i))
    return lax.ppermute(value, (other, axis), pairs)


def gather_blocks(block, axis, other):
    count, mine = lax.axis_size(axis), lax.axis_index(axis)
    if count != 4:
        return lax.all_gather(block, axis, axis=0, tiled=True)
    near = partner_swap(block, axis)
    across = middle_swap(block, axis, other)
    far = middle_swap(near, axis, other)
    across_end = partner_swap(across, axis)
    far_end = partner_swap(far, axis)
    inner = (mine == 1) | (mine == 2)
    second = jnp.where(inner, far, across_end)
    third = jnp.where(inner, across, far_end)
    rows = block.shape[0]
    whole = jnp.zeros((rows * count,) + block.shape[1:], block.dtype)
    for flip, piece in enumerate((block, near, second, third)):
        whole = lax.dynamic_update_slice_in_dim(whole, piece, (mine ^ flip) * rows, 0)
    return whole


def sum_over(value, axis):
    count = lax.axis_size(axis)
    half = value.shape[0] // 2
    steps = [1 << b for b in range(count.bit_length() - 1)]
    outs = []
    for part, order in ((value[:half], steps), (value[half:], steps[::-1])):
        for step in order:
            sent = lax.ppermute(part.astype(jnp.bfloat16), axis, [(i, i ^ step) for i in range(count)])
            part = part + sent.astype(jnp.float32)
        outs.append(part)
    return jnp.concatenate(outs, axis=0)


def entering(value, axis):
    count, mine = lax.axis_size(axis), lax.axis_index(axis)
    total = lax.ppermute(value, axis, [(i, i + 1) for i in range(count - 1)])
    reach = 1
    while reach < count - 1:
        total = total + lax.ppermute(total, axis, [(i, i + reach) for i in range(count - reach)])
        reach *= 2
    return total


def project(matrix, block):
    return jnp.dot(matrix, block, preferred_element_type=jnp.float32).astype(jnp.bfloat16)


def local(streams, w_query, w_key, w_value, gain):
    width = w_query.shape[1]
    heads = width // HEAD_DIM
    tokens = streams.shape[1]
    columns = jnp.swapaxes(streams, 1, 2)
    w_query, w_key, w_value = w_query.T, w_key.T, w_value.T
    gain_heads = gain.reshape(heads, HEAD_DIM, 1)
    prefix, results = None, []
    for stream in range(2):
        features = gather_blocks(columns[stream], "head", "group")
        key = jnp.maximum(project(w_key, features), 0).reshape(heads, HEAD_DIM, tokens)
        value = project(w_value, features).reshape(heads, HEAD_DIM, tokens)
        query = jnp.maximum(project(w_query, features), 0).reshape(heads, HEAD_DIM, tokens)
        state = jnp.einsum("hat,hbt->hba", key, value, preferred_element_type=jnp.float32)
        state = sum_over(state.reshape(width, HEAD_DIM), "tok")
        if stream == 0:
            prefix = entering(state, "group")
        total = (prefix + state).reshape(heads, HEAD_DIM, HEAD_DIM).astype(jnp.bfloat16)
        reading = jnp.einsum("hba,hat->hbt", total, query, preferred_element_type=jnp.float32)
        scale = lax.rsqrt(jnp.mean(reading * reading, axis=1, keepdims=True) + 1e-06)
        normed = reading * scale * gain_heads
        results.append(normed.astype(jnp.bfloat16).reshape(width, tokens))
    return jnp.swapaxes(jnp.stack(results), 1, 2)


def solution(mesh):
    return jax.shard_map(
        local,
        mesh=mesh,
        in_specs=(
            P(None, ("group", "tok"), "head"),
            P(None, "head"),
            P(None, "head"),
            P(None, "head"),
            P("head"),
        ),
        out_specs=P(None, ("group", "tok"), "head"),
        check_vma=False,
    )
```

```python
import functools

import jax
import jax.numpy as jnp
from jax import lax
from jax.experimental import pallas as pl
from jax.experimental.pallas import tpu as pltpu
from jax.sharding import PartitionSpec as P

HEAD_DIM = 112
LANES = 128
VMEM_LIMIT = 40 * 1024 * 1024
ANYWHERE = pl.BlockSpec(memory_space=pl.ANY)
IN_VMEM = pl.BlockSpec(memory_space=pltpu.VMEM)
IN_SMEM = pl.BlockSpec(memory_space=pltpu.SMEM)


def call(body, outs, out_specs, in_specs, scratch, flops, aliases=None):
    return pl.pallas_call(
        body,
        out_shape=outs,
        in_specs=in_specs,
        out_specs=out_specs,
        scratch_shapes=scratch,
        input_output_aliases=aliases or {},
        compiler_params=pltpu.CompilerParams(vmem_limit_bytes=VMEM_LIMIT),
        cost_estimate=pl.CostEstimate(flops=flops, bytes_accessed=8 << 20, transcendentals=0),
    )


def rounded_dot(matrix, block):
    return jnp.dot(matrix, block, preferred_element_type=jnp.float32)


def token_tiles(tokens):
    width = 256 if tokens % 256 == 0 else tokens
    return width, tokens // width


def add_state(sums, key, value):
    for start in range(0, key.shape[0], HEAD_DIM):
        rows = slice(start, start + HEAD_DIM)
        sums[rows, :] += lax.dot_general(
            value[rows], key[rows], (((1,), (1,)), ((), ())), preferred_element_type=jnp.float32
        )


def load_blocks(place, found, whole, sems):
    mine, inner = place[0], place[1]
    rows = found[0].shape[0]

    def at(flip):
        return whole.at[pl.ds(pl.multiple_of((mine ^ flip) * rows, 16), rows), :]

    for flip, source in enumerate(found):
        if isinstance(source, tuple):
            for want, ref in ((1, source[0]), (0, source[1])):

                @pl.when(inner == want)
                def _(ref=ref, flip=flip):
                    pltpu.make_async_copy(ref, at(flip), sems.at[flip]).start()
        else:
            pltpu.make_async_copy(source, at(flip), sems.at[flip]).start()
    for flip in range(len(found)):
        pltpu.make_async_copy(at(flip), at(flip), sems.at[flip]).wait()


def whole_kernel(place, b0, b1, b2i, b2o, b3i, b3o, wq, wk, wv, query, state, whole, sems):
    load_blocks(place, [b0, b1, (b2i, b2o), (b3i, b3o)], whole, sems)
    state[...] = jnp.zeros_like(state)
    width, tiles = token_tiles(whole.shape[1])

    @pl.loop(0, tiles)
    def _(tile):
        columns = pl.ds(pl.multiple_of(tile * width, width), width)
        block = whole[:, columns]
        key = jnp.maximum(rounded_dot(wk[...], block).astype(jnp.bfloat16), 0)
        value = rounded_dot(wv[...], block).astype(jnp.bfloat16)
        add_state(state, key, value)
        query[:, columns] = jnp.maximum(rounded_dot(wq[...], block).astype(jnp.bfloat16), 0)


def partial_kernel(place, b0, b1, b2i, b2o, wq, wk, wv, tie, sums, whole, sems):
    rows, tokens = b0.shape
    missing = pl.ds(pl.multiple_of((place[0] ^ 3) * rows, 16), rows)
    whole[missing, :] = jnp.zeros((rows, tokens), whole.dtype)
    load_blocks(place, [b0, b1, (b2i, b2o)], whole, sems)
    width, tiles = token_tiles(tokens)

    @pl.loop(0, tiles)
    def _(tile):
        columns = pl.ds(pl.multiple_of(tile * width, width), width)
        block = whole[:, columns]
        for k, matrix in enumerate((wk, wv, wq)):
            sums[k, :, columns] = rounded_dot(matrix[...], block)


def last_block(place, inner_ref, end_ref, last, sems, count, body):
    rows, tokens = inner_ref.shape
    span = last.shape[0]
    for owner in range(count):
        start = owner * rows
        low = start // LANES * LANES
        high = min(count * rows, -(-(start + rows) // LANES) * LANES)
        offset = start - low

        @pl.when((place[0] ^ 3) == owner)
        def _(low=low, high=high, offset=offset):
            target = last.at[pl.ds(offset, rows), :]

            @pl.when(place[1] == 1)
            def _():
                pltpu.make_async_copy(inner_ref, target, sems.at[0]).start()

            @pl.when(place[1] == 0)
            def _():
                pltpu.make_async_copy(end_ref, target, sems.at[0]).start()

            if offset:
                last[0:offset, :] = jnp.zeros((offset, tokens), last.dtype)
            if offset + rows < span:
                last[offset + rows : span, :] = jnp.zeros((span - offset - rows, tokens), last.dtype)
            pltpu.make_async_copy(target, target, sems.at[0]).wait()
            body(slice(low, high))


def state_kernel(count, place, inner_ref, end_ref, wk, wv, sums, state, last, sems):
    state[...] = jnp.zeros_like(state)
    width, tiles = token_tiles(inner_ref.shape[1])

    def body(span):
        depth = span.stop - span.start

        @pl.loop(0, tiles)
        def _(tile):
            columns = pl.ds(pl.multiple_of(tile * width, width), width)
            block = last[0:depth, columns]
            key = (sums[0, :, columns] + rounded_dot(wk[:, span], block)).astype(jnp.bfloat16)
            value = (sums[1, :, columns] + rounded_dot(wv[:, span], block)).astype(jnp.bfloat16)
            add_state(state, jnp.maximum(key, 0), value)

    last_block(place, inner_ref, end_ref, last, sems, count, body)


def query_kernel(count, place, inner_ref, end_ref, wq, sums, tie, query, last, sems):
    width, tiles = token_tiles(inner_ref.shape[1])

    def body(span):
        depth = span.stop - span.start

        @pl.loop(0, tiles)
        def _(tile):
            columns = pl.ds(pl.multiple_of(tile * width, width), width)
            block = last[0:depth, columns]
            row = (sums[2, :, columns] + rounded_dot(wq[:, span], block)).astype(jnp.bfloat16)
            query[:, columns] = jnp.maximum(row, 0)

    last_block(place, inner_ref, end_ref, last, sems, count, body)


def read_kernel(stream, prefix, state, query, gain, *rest):
    out, held, sem = rest[-3:]
    for start in range(0, query.shape[0], HEAD_DIM):
        rows = slice(start, start + HEAD_DIM)
        total = (prefix[rows, :] + state[rows, :]).astype(jnp.bfloat16)
        reading = rounded_dot(total, query[rows, :])
        scale = lax.rsqrt(jnp.mean(reading * reading, axis=0, keepdims=True) + 1e-06)
        held[rows, :] = (reading * scale * gain[rows, :]).astype(jnp.bfloat16)
    copy = pltpu.make_async_copy(held, out.at[stream], sem)
    copy.start()
    copy.wait()


def partner_swap(value, axis):
    return lax.ppermute(value, axis, [(i, i ^ 1) for i in range(lax.axis_size(axis))])


def middle_swap(value, axis, other):
    wide, count = lax.axis_size(other), lax.axis_size(axis)
    pairs = []
    for j in range(wide):
        for i in range(count):
            if i in (1, 2):
                pairs.append((j * count + i, j * count + 3 - i))
            else:
                pairs.append((j * count + i, (j ^ 1 if j ^ 1 < wide else j) * count + i))
    return lax.ppermute(value, (other, axis), pairs)


def sum_over(value, axis):
    count = lax.axis_size(axis)
    heads = value.shape[0] // HEAD_DIM
    half = (heads + 1) // 2 * HEAD_DIM
    steps = [1 << b for b in range(count.bit_length() - 1)]
    outs = []
    for part, order in ((value[:half], steps), (value[half:], steps[::-1])):
        for step in order:
            sent = lax.ppermute(part.astype(jnp.bfloat16), axis, [(i, i ^ step) for i in range(count)])
            part = part + sent.astype(jnp.float32)
        outs.append(part)
    return jnp.concatenate(outs, axis=0)


def entering(value, axis):
    count = lax.axis_size(axis)
    total = lax.ppermute(value, axis, [(i, i + 1) for i in range(count - 1)])
    reach = 1
    while reach < count - 1:
        total = total + lax.ppermute(total, axis, [(i, i + reach) for i in range(count - reach)])
        reach *= 2
    return total


def local(streams, w_query, w_key, w_value, gain):
    count, mine = lax.axis_size("head"), lax.axis_index("head")
    rows, tokens = streams.shape[2], streams.shape[1]
    width = w_query.shape[1]
    depth = rows * count
    columns = jnp.swapaxes(streams, 1, 2)
    matrices = (w_query.T, w_key.T, w_value.T)
    gain_column = gain.reshape(width, 1)
    inner = (mine == 1) | (mine == 2)
    place = jnp.stack([mine.astype(jnp.int32), inner.astype(jnp.int32)])

    own, near, across, far, across_end, far_end = [], [], [], [], [], []
    for stream in range(2):
        own.append(columns[stream])
        near.append(partner_swap(own[stream], "head"))
        across.append(middle_swap(own[stream], "head", "group"))
    for stream in range(2):
        far.append(middle_swap(near[stream], "head", "group"))
        across_end.append(partner_swap(across[stream], "head"))
    for stream in range(2):
        far_end.append(partner_swap(far[stream], "head"))

    whole = pltpu.VMEM((depth, tokens), jnp.bfloat16)
    sems = pltpu.SemaphoreType.DMA((4,))
    last = pltpu.VMEM((-(-(rows + LANES) // LANES) * LANES, tokens), jnp.bfloat16)
    query_type = jax.ShapeDtypeStruct((width, tokens), jnp.bfloat16)
    state_type = jax.ShapeDtypeStruct((width, HEAD_DIM), jnp.float32)
    out_type = jax.ShapeDtypeStruct((2, width, tokens), jnp.bfloat16)
    one = 2 * width * depth * tokens

    query0, state0 = call(
        whole_kernel, (query_type, state_type), (IN_VMEM, IN_VMEM),
        [IN_SMEM] + [ANYWHERE] * 6 + [IN_VMEM] * 3, [whole, sems], 3 * one,
    )(place, own[0], near[0], far[0], across_end[0], across[0], far_end[0], *matrices)
    state0 = sum_over(state0, "tok")
    prefix = entering(state0, "group")

    sums = call(
        partial_kernel, jax.ShapeDtypeStruct((3, width, tokens), jnp.float32), IN_VMEM,
        [IN_SMEM] + [ANYWHERE] * 4 + [IN_VMEM] * 3 + [ANYWHERE], [whole, sems], 3 * one,
    )(place, own[1], near[1], far[1], across_end[1], *matrices, query0)

    read_scratch = [pltpu.VMEM((width, tokens), jnp.bfloat16), pltpu.SemaphoreType.DMA(())]
    out = call(
        functools.partial(read_kernel, 0), out_type, ANYWHERE, [IN_VMEM] * 4, read_scratch, one // 20,
    )(prefix, state0, query0, gain_column)

    state1 = call(
        functools.partial(state_kernel, count), state_type, IN_VMEM,
        [IN_SMEM] + [ANYWHERE] * 2 + [IN_VMEM] * 3, [last, sems], one // 2,
    )(place, across[1], far_end[1], *matrices[1:], sums)
    query1 = call(
        functools.partial(query_kernel, count), query_type, IN_VMEM,
        [IN_SMEM] + [ANYWHERE] * 2 + [IN_VMEM] * 2 + [ANYWHERE], [last, sems], one // 4,
    )(place, across[1], far_end[1], matrices[0], sums, state1)
    state1 = sum_over(state1, "tok")
    out = call(
        functools.partial(read_kernel, 1), out_type, ANYWHERE, [IN_VMEM] * 4 + [ANYWHERE], read_scratch,
        one // 20, {4: 0},
    )(prefix, state1, query1, gain_column, out)
    return jnp.swapaxes(out, 1, 2)


def solution(mesh):
    return jax.shard_map(
        local,
        mesh=mesh,
        in_specs=(
            P(None, ("group", "tok"), "head"),
            P(None, "head"),
            P(None, "head"),
            P(None, "head"),
            P("head"),
        ),
        out_specs=P(None, ("group", "tok"), "head"),
        check_vma=False,
    )
```

```python
import functools

import jax
import jax.numpy as jnp
from jax import lax
from jax.experimental import pallas as pl
from jax.experimental.pallas import tpu as pltpu
from jax.sharding import PartitionSpec as P

HEAD_DIM = 112
LANES = 128
VMEM_LIMIT = 20 * 1024 * 1024
ANYWHERE = pl.BlockSpec(memory_space=pl.ANY)
IN_VMEM = pl.BlockSpec(memory_space=pltpu.VMEM)
IN_SMEM = pl.BlockSpec(memory_space=pltpu.SMEM)


def call(body, outs, out_specs, in_specs, scratch, flops, aliases=None):
    return pl.pallas_call(
        body,
        out_shape=outs,
        in_specs=in_specs,
        out_specs=out_specs,
        scratch_shapes=scratch,
        input_output_aliases=aliases or {},
        compiler_params=pltpu.CompilerParams(vmem_limit_bytes=VMEM_LIMIT),
        cost_estimate=pl.CostEstimate(flops=flops // 64, bytes_accessed=1 << 10, transcendentals=0),
    )


def rounded_dot(matrix, block):
    return jnp.dot(matrix, block, preferred_element_type=jnp.float32)


def token_tiles(tokens):
    width = 256 if tokens % 256 == 0 else tokens
    return width, tokens // width


def add_state(sums, key, value):
    for start in range(0, key.shape[0], HEAD_DIM):
        rows = slice(start, start + HEAD_DIM)
        sums[rows, :] += lax.dot_general(
            value[rows], key[rows], (((1,), (1,)), ((), ())), preferred_element_type=jnp.float32
        )


def load_blocks(place, found, whole, sems):
    mine, inner = place[0], place[1]
    rows = found[0].shape[0]

    def at(flip):
        return whole.at[pl.ds(pl.multiple_of((mine ^ flip) * rows, 16), rows), :]

    for flip, source in enumerate(found):
        if isinstance(source, tuple):
            for want, ref in ((1, source[0]), (0, source[1])):

                @pl.when(inner == want)
                def _(ref=ref, flip=flip):
                    pltpu.make_async_copy(ref, at(flip), sems.at[flip]).start()
        else:
            pltpu.make_async_copy(source, at(flip), sems.at[flip]).start()
    for flip in range(len(found)):
        pltpu.make_async_copy(at(flip), at(flip), sems.at[flip]).wait()


def partial_kernel(place, b0, b1, b2i, b2o, wq, wk, wv, *rest):
    sums, whole, sems = rest[-3:]
    rows, tokens = b0.shape
    missing = pl.ds(pl.multiple_of((place[0] ^ 3) * rows, 16), rows)
    whole[missing, :] = jnp.zeros((rows, tokens), whole.dtype)
    load_blocks(place, [b0, b1, (b2i, b2o)], whole, sems)
    width, tiles = token_tiles(tokens)

    @pl.loop(0, tiles)
    def _(tile):
        columns = pl.ds(pl.multiple_of(tile * width, width), width)
        block = whole[:, columns]
        for k, matrix in enumerate((wk, wv, wq)):
            sums[k, :, columns] = rounded_dot(matrix[...], block)


def last_block(place, inner_ref, end_ref, last, sems, count, body):
    rows, tokens = inner_ref.shape
    span = last.shape[0]
    for owner in range(count):
        start = owner * rows
        low = start // LANES * LANES
        high = min(count * rows, -(-(start + rows) // LANES) * LANES)
        offset = start - low

        @pl.when((place[0] ^ 3) == owner)
        def _(low=low, high=high, offset=offset):
            target = last.at[pl.ds(offset, rows), :]

            @pl.when(place[1] == 1)
            def _():
                pltpu.make_async_copy(inner_ref, target, sems.at[0]).start()

            @pl.when(place[1] == 0)
            def _():
                pltpu.make_async_copy(end_ref, target, sems.at[0]).start()

            if offset:
                last[0:offset, :] = jnp.zeros((offset, tokens), last.dtype)
            if offset + rows < span:
                last[offset + rows : span, :] = jnp.zeros((span - offset - rows, tokens), last.dtype)
            pltpu.make_async_copy(target, target, sems.at[0]).wait()
            body(slice(low, high))


def state_kernel(count, place, inner_ref, end_ref, wk, wv, sums, *rest):
    state, last, sems = rest[-3:]
    state[...] = jnp.zeros_like(state)
    width, tiles = token_tiles(inner_ref.shape[1])

    def body(span):
        depth = span.stop - span.start

        @pl.loop(0, tiles)
        def _(tile):
            columns = pl.ds(pl.multiple_of(tile * width, width), width)
            block = last[0:depth, columns]
            key = (sums[0, :, columns] + rounded_dot(wk[:, span], block)).astype(jnp.bfloat16)
            value = (sums[1, :, columns] + rounded_dot(wv[:, span], block)).astype(jnp.bfloat16)
            add_state(state, jnp.maximum(key, 0), value)

    last_block(place, inner_ref, end_ref, last, sems, count, body)


def query_kernel(count, place, inner_ref, end_ref, wq, sums, tie, query, last, sems):
    width, tiles = token_tiles(inner_ref.shape[1])

    def body(span):
        depth = span.stop - span.start

        @pl.loop(0, tiles)
        def _(tile):
            columns = pl.ds(pl.multiple_of(tile * width, width), width)
            block = last[0:depth, columns]
            row = (sums[2, :, columns] + rounded_dot(wq[:, span], block)).astype(jnp.bfloat16)
            query[:, columns] = jnp.maximum(row, 0)

    last_block(place, inner_ref, end_ref, last, sems, count, body)


def read_kernel(stream, totals, query, gain, *rest):
    out, held, sem = rest[-3:]
    for start in range(0, query.shape[0], HEAD_DIM):
        rows = slice(start, start + HEAD_DIM)
        total = totals[rows, :].astype(jnp.bfloat16)
        reading = rounded_dot(total, query[rows, :])
        scale = lax.rsqrt(jnp.mean(reading * reading, axis=0, keepdims=True) + 1e-06)
        held[rows, :] = (reading * scale * gain[rows, :]).astype(jnp.bfloat16)
    copy = pltpu.make_async_copy(held, out.at[stream], sem)
    copy.start()
    copy.wait()


def partner_swap(value, axis):
    return lax.ppermute(value, axis, [(i, i ^ 1) for i in range(lax.axis_size(axis))])


def middle_swap(value, axis, other):
    wide, count = lax.axis_size(other), lax.axis_size(axis)
    pairs = []
    for j in range(wide):
        for i in range(count):
            if i in (1, 2):
                pairs.append((j * count + i, j * count + 3 - i))
            else:
                pairs.append((j * count + i, (j ^ 1 if j ^ 1 < wide else j) * count + i))
    return lax.ppermute(value, (other, axis), pairs)


def sum_over(value, axis, backwards):
    count = lax.axis_size(axis)
    steps = [1 << b for b in range(count.bit_length() - 1)]
    for step in steps[::-1] if backwards else steps:
        sent = lax.ppermute(value.astype(jnp.bfloat16), axis, [(i, i ^ step) for i in range(count)])
        value = value + sent.astype(jnp.float32)
    return value


def entering(value, axis):
    count = lax.axis_size(axis)
    total = lax.ppermute(value, axis, [(i, i + 1) for i in range(count - 1)])
    reach = 1
    while reach < count - 1:
        total = total + lax.ppermute(total, axis, [(i, i + reach) for i in range(count - reach)])
        reach *= 2
    return total


def local(streams, w_query, w_key, w_value, gain):
    count, mine = lax.axis_size("head"), lax.axis_index("head")
    rows, tokens = streams.shape[2], streams.shape[1]
    width = w_query.shape[1]
    depth = rows * count
    columns = jnp.swapaxes(streams, 1, 2)
    matrices = (w_query.T, w_key.T, w_value.T)
    gain_column = gain.reshape(width, 1)
    inner = (mine == 1) | (mine == 2)
    place = jnp.stack([mine.astype(jnp.int32), inner.astype(jnp.int32)])

    own, near, across, far, across_end, far_end = [], [], [], [], [], []
    for stream in range(2):
        own.append(columns[stream])
        near.append(partner_swap(own[stream], "head"))
        across.append(middle_swap(own[stream], "head", "group"))
    for stream in range(2):
        far.append(middle_swap(near[stream], "head", "group"))
        across_end.append(partner_swap(across[stream], "head"))
    for stream in range(2):
        far_end.append(partner_swap(far[stream], "head"))

    whole = pltpu.VMEM((depth, tokens), jnp.bfloat16)
    sems = pltpu.SemaphoreType.DMA((4,))
    last = pltpu.VMEM((-(-(rows + LANES) // LANES) * LANES, tokens), jnp.bfloat16)
    query_type = jax.ShapeDtypeStruct((width, tokens), jnp.bfloat16)
    state_type = jax.ShapeDtypeStruct((width, HEAD_DIM), jnp.float32)
    out_type = jax.ShapeDtypeStruct((2, width, tokens), jnp.bfloat16)
    one = 2 * width * depth * tokens

    read_scratch = [pltpu.VMEM((width, tokens), jnp.bfloat16), pltpu.SemaphoreType.DMA(())]
    prefix = query = out = None
    for stream in range(2):
        ties = (far[1], across[1]) if stream == 0 else ()
        sums = call(
            partial_kernel, jax.ShapeDtypeStruct((3, width, tokens), jnp.float32), IN_VMEM,
            [IN_SMEM] + [ANYWHERE] * 4 + [IN_VMEM] * 3 + [ANYWHERE] * len(ties), [whole, sems], 3 * one,
        )(place, own[stream], near[stream], far[stream], across_end[stream], *matrices, *ties)
        ties = (across_end[1],) if stream == 0 else (prefix, query)
        state = call(
            functools.partial(state_kernel, count), state_type, IN_VMEM,
            [IN_SMEM] + [ANYWHERE] * 2 + [IN_VMEM] * 3 + [ANYWHERE] * len(ties), [last, sems], one // 2,
        )(place, across[stream], far_end[stream], *matrices[1:], sums, *ties)
        query = call(
            functools.partial(query_kernel, count), query_type, IN_VMEM,
            [IN_SMEM] + [ANYWHERE] * 2 + [IN_VMEM] * 2 + [ANYWHERE], [last, sems], one // 4,
        )(place, across[stream], far_end[stream], matrices[0], sums, state)
        if stream == 0:
            prefix = entering(state, "group")
        total = sum_over(prefix + state, "tok", stream == 1)
        kept = [] if out is None else [out]
        out = call(
            functools.partial(read_kernel, stream), out_type, ANYWHERE, [IN_VMEM] * 3 + [ANYWHERE] * len(kept),
            read_scratch, one // 20, {3: 0} if kept else None,
        )(total, query, gain_column, *kept)
    return jnp.swapaxes(out, 1, 2)


def solution(mesh):
    return jax.shard_map(
        local,
        mesh=mesh,
        in_specs=(
            P(None, ("group", "tok"), "head"),
            P(None, "head"),
            P(None, "head"),
            P(None, "head"),
            P("head"),
        ),
        out_specs=P(None, ("group", "tok"), "head"),
        check_vma=False,
    )
```

```python
import functools

import jax
import jax.numpy as jnp
from jax import lax
from jax.experimental import pallas as pl
from jax.experimental.pallas import tpu as pltpu
from jax.sharding import PartitionSpec as P

HEAD_DIM = 112
LANES = 128
VMEM_LIMIT = 20 * 1024 * 1024
ANYWHERE = pl.BlockSpec(memory_space=pl.ANY)
IN_VMEM = pl.BlockSpec(memory_space=pltpu.VMEM)
IN_SMEM = pl.BlockSpec(memory_space=pltpu.SMEM)


def call(body, outs, out_specs, in_specs, scratch, flops, aliases=None):
    return pl.pallas_call(
        body,
        out_shape=outs,
        in_specs=in_specs,
        out_specs=out_specs,
        scratch_shapes=scratch,
        input_output_aliases=aliases or {},
        compiler_params=pltpu.CompilerParams(vmem_limit_bytes=VMEM_LIMIT),
        cost_estimate=pl.CostEstimate(flops=flops // 64, bytes_accessed=1 << 10, transcendentals=0),
    )


def rounded_dot(matrix, block):
    return jnp.dot(matrix, block, preferred_element_type=jnp.float32)


def token_tiles(tokens):
    width = 256 if tokens % 256 == 0 else tokens
    return width, tokens // width


def add_state(sums, key, value):
    for start in range(0, key.shape[0], HEAD_DIM):
        rows = slice(start, start + HEAD_DIM)
        sums[rows, :] += lax.dot_general(
            value[rows], key[rows], (((1,), (1,)), ((), ())), preferred_element_type=jnp.float32
        )


def load_blocks(place, found, whole, sems):
    mine, inner = place[0], place[1]
    rows = found[0].shape[0]

    def at(flip):
        return whole.at[pl.ds(pl.multiple_of((mine ^ flip) * rows, 16), rows), :]

    for flip, source in enumerate(found):
        if isinstance(source, tuple):
            for want, ref in ((1, source[0]), (0, source[1])):

                @pl.when(inner == want)
                def _(ref=ref, flip=flip):
                    pltpu.make_async_copy(ref, at(flip), sems.at[flip]).start()
        else:
            pltpu.make_async_copy(source, at(flip), sems.at[flip]).start()
    for flip in range(len(found)):
        pltpu.make_async_copy(at(flip), at(flip), sems.at[flip]).wait()


def partial_kernel(place, b0, b1, b2i, b2o, wq, wk, wv, sums, whole, sems):
    rows, tokens = b0.shape
    missing = pl.ds(pl.multiple_of((place[0] ^ 3) * rows, 16), rows)
    whole[missing, :] = jnp.zeros((rows, tokens), whole.dtype)
    load_blocks(place, [b0, b1, (b2i, b2o)], whole, sems)
    width, tiles = token_tiles(tokens)

    @pl.loop(0, tiles)
    def _(tile):
        columns = pl.ds(pl.multiple_of(tile * width, width), width)
        block = whole[:, columns]
        for k, matrix in enumerate((wk, wv, wq)):
            sums[k, :, columns] = rounded_dot(matrix[...], block)


def last_block(place, inner_ref, end_ref, last, sems, count, body):
    rows, tokens = inner_ref.shape
    span = last.shape[0]
    for owner in range(count):
        start = owner * rows
        low = start // LANES * LANES
        high = min(count * rows, -(-(start + rows) // LANES) * LANES)
        offset = start - low

        @pl.when((place[0] ^ 3) == owner)
        def _(low=low, high=high, offset=offset):
            target = last.at[pl.ds(offset, rows), :]

            @pl.when(place[1] == 1)
            def _():
                pltpu.make_async_copy(inner_ref, target, sems.at[0]).start()

            @pl.when(place[1] == 0)
            def _():
                pltpu.make_async_copy(end_ref, target, sems.at[0]).start()

            if offset:
                last[0:offset, :] = jnp.zeros((offset, tokens), last.dtype)
            if offset + rows < span:
                last[offset + rows : span, :] = jnp.zeros((span - offset - rows, tokens), last.dtype)
            pltpu.make_async_copy(target, target, sems.at[0]).wait()
            body(slice(low, high))


def state_kernel(count, place, inner_ref, end_ref, wk, wv, sums, *rest):
    state, last, sems = rest[-3:]
    state[...] = jnp.zeros_like(state)
    width, tiles = token_tiles(inner_ref.shape[1])

    def body(span):
        depth = span.stop - span.start

        @pl.loop(0, tiles)
        def _(tile):
            columns = pl.ds(pl.multiple_of(tile * width, width), width)
            block = last[0:depth, columns]
            key = (sums[0, :, columns] + rounded_dot(wk[:, span], block)).astype(jnp.bfloat16)
            value = (sums[1, :, columns] + rounded_dot(wv[:, span], block)).astype(jnp.bfloat16)
            add_state(state, jnp.maximum(key, 0), value)

    last_block(place, inner_ref, end_ref, last, sems, count, body)


def query_kernel(count, place, inner_ref, end_ref, wq, sums, tie, query, last, sems):
    width, tiles = token_tiles(inner_ref.shape[1])

    def body(span):
        depth = span.stop - span.start

        @pl.loop(0, tiles)
        def _(tile):
            columns = pl.ds(pl.multiple_of(tile * width, width), width)
            block = last[0:depth, columns]
            row = (sums[2, :, columns] + rounded_dot(wq[:, span], block)).astype(jnp.bfloat16)
            query[:, columns] = jnp.maximum(row, 0)

    last_block(place, inner_ref, end_ref, last, sems, count, body)


def read_kernel(stream, totals, query, gain, *rest):
    out, held, sem = rest[-3:]
    for start in range(0, query.shape[0], HEAD_DIM):
        rows = slice(start, start + HEAD_DIM)
        total = totals[rows, :].astype(jnp.bfloat16)
        reading = rounded_dot(total, query[rows, :])
        scale = lax.rsqrt(jnp.mean(reading * reading, axis=0, keepdims=True) + 1e-06)
        held[rows, :] = (reading * scale * gain[rows, :]).astype(jnp.bfloat16)
    copy = pltpu.make_async_copy(held, out.at[stream], sem)
    copy.start()
    copy.wait()


def partner_swap(value, axis):
    return lax.ppermute(value, axis, [(i, i ^ 1) for i in range(lax.axis_size(axis))])


def middle_swap(value, axis, other):
    wide, count = lax.axis_size(other), lax.axis_size(axis)
    pairs = []
    for j in range(wide):
        for i in range(count):
            if i in (1, 2):
                pairs.append((j * count + i, j * count + 3 - i))
            else:
                pairs.append((j * count + i, (j ^ 1 if j ^ 1 < wide else j) * count + i))
    return lax.ppermute(value, (other, axis), pairs)


def sum_over(value, axis, backwards):
    count = lax.axis_size(axis)
    steps = [1 << b for b in range(count.bit_length() - 1)]
    for step in steps[::-1] if backwards else steps:
        sent = lax.ppermute(value.astype(jnp.bfloat16), axis, [(i, i ^ step) for i in range(count)])
        value = value + sent.astype(jnp.float32)
    return value


def entering(value, axis):
    count = lax.axis_size(axis)
    total = lax.ppermute(value, axis, [(i, i + 1) for i in range(count - 1)])
    reach = 1
    while reach < count - 1:
        total = total + lax.ppermute(total, axis, [(i, i + reach) for i in range(count - reach)])
        reach *= 2
    return total


def local(streams, w_query, w_key, w_value, gain):
    count, mine = lax.axis_size("head"), lax.axis_index("head")
    rows, tokens = streams.shape[2], streams.shape[1]
    width = w_query.shape[1]
    depth = rows * count
    columns = jnp.swapaxes(streams, 1, 2)
    matrices = (w_query.T, w_key.T, w_value.T)
    gain_column = gain.reshape(width, 1)
    inner = (mine == 1) | (mine == 2)
    place = jnp.stack([mine.astype(jnp.int32), inner.astype(jnp.int32)])

    own, near, across, far, across_end, far_end = [], [], [], [], [], []
    for stream in range(2):
        own.append(columns[stream])
        near.append(partner_swap(own[stream], "head"))
        across.append(middle_swap(own[stream], "head", "group"))
    for stream in range(2):
        far.append(middle_swap(near[stream], "head", "group"))
        ready, _ = lax.optimization_barrier((across[stream], near[stream]))
        across_end.append(partner_swap(ready, "head"))
    whole = pltpu.VMEM((depth, tokens), jnp.bfloat16)
    sems = pltpu.SemaphoreType.DMA((4,))
    last = pltpu.VMEM((-(-(rows + LANES) // LANES) * LANES, tokens), jnp.bfloat16)
    query_type = jax.ShapeDtypeStruct((width, tokens), jnp.bfloat16)
    state_type = jax.ShapeDtypeStruct((width, HEAD_DIM), jnp.float32)
    out_type = jax.ShapeDtypeStruct((2, width, tokens), jnp.bfloat16)
    one = 2 * width * depth * tokens

    read_scratch = [pltpu.VMEM((width, tokens), jnp.bfloat16), pltpu.SemaphoreType.DMA(())]
    sums = []
    for stream in range(2):
        ready, *_ = lax.optimization_barrier((far[stream], across_end[stream], *sums))
        far_end.append(partner_swap(ready, "head"))
        sums.append(call(
            partial_kernel, jax.ShapeDtypeStruct((3, width, tokens), jnp.float32), IN_VMEM,
            [IN_SMEM] + [ANYWHERE] * 4 + [IN_VMEM] * 3, [whole, sems], 3 * one,
        )(place, own[stream], near[stream], far[stream], across_end[stream], *matrices))
    prefix = query = out = None
    for stream in range(2):
        ties = (sums[1],) if stream == 0 else (prefix, query)
        state = call(
            functools.partial(state_kernel, count), state_type, IN_VMEM,
            [IN_SMEM] + [ANYWHERE] * 2 + [IN_VMEM] * 3 + [ANYWHERE] * len(ties), [last, sems], one // 2,
        )(place, across[stream], far_end[stream], *matrices[1:], sums[stream], *ties)
        query = call(
            functools.partial(query_kernel, count), query_type, IN_VMEM,
            [IN_SMEM] + [ANYWHERE] * 2 + [IN_VMEM] * 2 + [ANYWHERE], [last, sems], one // 4,
        )(place, across[stream], far_end[stream], matrices[0], sums[stream], state)
        if stream == 0:
            prefix = entering(state, "group")
        total = sum_over(prefix + state, "tok", stream == 1)
        kept = [] if out is None else [out]
        out = call(
            functools.partial(read_kernel, stream), out_type, ANYWHERE, [IN_VMEM] * 3 + [ANYWHERE] * len(kept),
            read_scratch, one // 20, {3: 0} if kept else None,
        )(total, query, gain_column, *kept)
    return jnp.swapaxes(out, 1, 2)


def solution(mesh):
    return jax.shard_map(
        local,
        mesh=mesh,
        in_specs=(
            P(None, ("group", "tok"), "head"),
            P(None, "head"),
            P(None, "head"),
            P(None, "head"),
            P("head"),
        ),
        out_specs=P(None, ("group", "tok"), "head"),
        check_vma=False,
    )
```

```python
import functools

import jax
import jax.numpy as jnp
from jax import lax
from jax.experimental import pallas as pl
from jax.experimental.pallas import tpu as pltpu
from jax.sharding import PartitionSpec as P

HEAD_DIM = 112
LANES = 128
VMEM_LIMIT = 20 * 1024 * 1024
ANYWHERE = pl.BlockSpec(memory_space=pl.ANY)
IN_VMEM = pl.BlockSpec(memory_space=pltpu.VMEM)
IN_SMEM = pl.BlockSpec(memory_space=pltpu.SMEM)


def call(body, outs, out_specs, in_specs, scratch, flops, aliases=None):
    return pl.pallas_call(
        body,
        out_shape=outs,
        in_specs=in_specs,
        out_specs=out_specs,
        scratch_shapes=scratch,
        input_output_aliases=aliases or {},
        compiler_params=pltpu.CompilerParams(vmem_limit_bytes=VMEM_LIMIT),
        cost_estimate=pl.CostEstimate(flops=flops // 64, bytes_accessed=1 << 10, transcendentals=0),
    )


def rounded_dot(matrix, block):
    return jnp.dot(matrix, block, preferred_element_type=jnp.float32)


def token_tiles(tokens):
    width = 256 if tokens % 256 == 0 else tokens
    return width, tokens // width


def add_state(sums, key, value):
    for start in range(0, key.shape[0], HEAD_DIM):
        rows = slice(start, start + HEAD_DIM)
        sums[rows, :] += lax.dot_general(
            value[rows], key[rows], (((1,), (1,)), ((), ())), preferred_element_type=jnp.float32
        )


def load_blocks(place, found, whole, sems):
    mine, inner = place[0], place[1]
    rows = found[0].shape[0]

    def at(flip):
        return whole.at[pl.ds(pl.multiple_of((mine ^ flip) * rows, 16), rows), :]

    for flip, source in enumerate(found):
        if isinstance(source, tuple):
            for want, ref in ((1, source[0]), (0, source[1])):

                @pl.when(inner == want)
                def _(ref=ref, flip=flip):
                    pltpu.make_async_copy(ref, at(flip), sems.at[flip]).start()
        else:
            pltpu.make_async_copy(source, at(flip), sems.at[flip]).start()
    for flip in range(len(found)):
        pltpu.make_async_copy(at(flip), at(flip), sems.at[flip]).wait()


def partial_kernel(place, b0, b1, b2i, b2o, wq, wk, wv, sums, whole, sems):
    rows, tokens = b0.shape
    missing = pl.ds(pl.multiple_of((place[0] ^ 3) * rows, 16), rows)
    whole[missing, :] = jnp.zeros((rows, tokens), whole.dtype)
    load_blocks(place, [b0, b1, (b2i, b2o)], whole, sems)
    width, tiles = token_tiles(tokens)

    @pl.loop(0, tiles)
    def _(tile):
        columns = pl.ds(pl.multiple_of(tile * width, width), width)
        block = whole[:, columns]
        for k, matrix in enumerate((wk, wv, wq)):
            sums[k, :, columns] = rounded_dot(matrix[...], block)


def last_block(place, inner_ref, end_ref, last, sems, count, body):
    rows, tokens = inner_ref.shape
    span = last.shape[0]
    for owner in range(count):
        start = owner * rows
        low = start // LANES * LANES
        high = min(count * rows, -(-(start + rows) // LANES) * LANES)
        offset = start - low

        @pl.when((place[0] ^ 3) == owner)
        def _(low=low, high=high, offset=offset):
            target = last.at[pl.ds(offset, rows), :]

            @pl.when(place[1] == 1)
            def _():
                pltpu.make_async_copy(inner_ref, target, sems.at[0]).start()

            @pl.when(place[1] == 0)
            def _():
                pltpu.make_async_copy(end_ref, target, sems.at[0]).start()

            if offset:
                last[0:offset, :] = jnp.zeros((offset, tokens), last.dtype)
            if offset + rows < span:
                last[offset + rows : span, :] = jnp.zeros((span - offset - rows, tokens), last.dtype)
            pltpu.make_async_copy(target, target, sems.at[0]).wait()
            body(slice(low, high))


def state_kernel(count, place, inner_ref, end_ref, wk, wv, sums, *rest):
    state, last, sems = rest[-3:]
    state[...] = jnp.zeros_like(state)
    width, tiles = token_tiles(inner_ref.shape[1])

    def body(span):
        depth = span.stop - span.start

        @pl.loop(0, tiles)
        def _(tile):
            columns = pl.ds(pl.multiple_of(tile * width, width), width)
            block = last[0:depth, columns]
            key = (sums[0, :, columns] + rounded_dot(wk[:, span], block)).astype(jnp.bfloat16)
            value = (sums[1, :, columns] + rounded_dot(wv[:, span], block)).astype(jnp.bfloat16)
            add_state(state, jnp.maximum(key, 0), value)

    last_block(place, inner_ref, end_ref, last, sems, count, body)


def query_kernel(count, place, inner_ref, end_ref, wq, sums, tie, query, last, sems):
    width, tiles = token_tiles(inner_ref.shape[1])

    def body(span):
        depth = span.stop - span.start

        @pl.loop(0, tiles)
        def _(tile):
            columns = pl.ds(pl.multiple_of(tile * width, width), width)
            block = last[0:depth, columns]
            row = (sums[2, :, columns] + rounded_dot(wq[:, span], block)).astype(jnp.bfloat16)
            query[:, columns] = jnp.maximum(row, 0)

    last_block(place, inner_ref, end_ref, last, sems, count, body)


def read_kernel(stream, prefix, states, query, gain, *rest):
    out, held, sem = rest[-3:]
    for start in range(0, query.shape[0], HEAD_DIM):
        rows = slice(start, start + HEAD_DIM)
        total = (prefix[rows, :] + states[rows, :]).astype(jnp.bfloat16)
        reading = rounded_dot(total, query[rows, :])
        scale = lax.rsqrt(jnp.mean(reading * reading, axis=0, keepdims=True) + 1e-06)
        held[rows, :] = (reading * scale * gain[rows, :]).astype(jnp.bfloat16)
    copy = pltpu.make_async_copy(held, out.at[stream], sem)
    copy.start()
    copy.wait()


def partner_swap(value, axis):
    return lax.ppermute(value, axis, [(i, i ^ 1) for i in range(lax.axis_size(axis))])


def middle_swap(value, axis, other):
    wide, count = lax.axis_size(other), lax.axis_size(axis)
    pairs = []
    for j in range(wide):
        for i in range(count):
            if i in (1, 2):
                pairs.append((j * count + i, j * count + 3 - i))
            else:
                pairs.append((j * count + i, (j ^ 1 if j ^ 1 < wide else j) * count + i))
    return lax.ppermute(value, (other, axis), pairs)


def sum_over(value, axis):
    count = lax.axis_size(axis)
    sent = value.astype(jnp.bfloat16)
    for step in range(count - 1, 0, -1):
        pairs = [(i, (i + step) % count) for i in range(count)]
        if count & (count - 1) == 0:
            pairs = [(i, i ^ step) for i in range(count)]
        value = value + lax.ppermute(sent, axis, pairs).astype(jnp.float32)
    return value


def entering(value, axis):
    count = lax.axis_size(axis)
    total = lax.ppermute(value, axis, [(i, i + 1) for i in range(count - 1)])
    reach = 1
    while reach < count - 1:
        total = total + lax.ppermute(total, axis, [(i, i + reach) for i in range(count - reach)])
        reach *= 2
    return total


def local(streams, w_query, w_key, w_value, gain):
    count, mine = lax.axis_size("head"), lax.axis_index("head")
    rows, tokens = streams.shape[2], streams.shape[1]
    width = w_query.shape[1]
    depth = rows * count
    columns = jnp.swapaxes(streams, 1, 2)
    matrices = (w_query.T, w_key.T, w_value.T)
    gain_column = gain.reshape(width, 1)
    inner = (mine == 1) | (mine == 2)
    place = jnp.stack([mine.astype(jnp.int32), inner.astype(jnp.int32)])

    own, near, across, far, across_end, far_end = [], [], [], [], [], []
    for stream in range(2):
        own.append(columns[stream])
        near.append(partner_swap(own[stream], "head"))
        across.append(middle_swap(own[stream], "head", "group"))
    for stream in range(2):
        far.append(middle_swap(near[stream], "head", "group"))
        ready, _ = lax.optimization_barrier((across[stream], near[stream]))
        across_end.append(partner_swap(ready, "head"))
    whole = pltpu.VMEM((depth, tokens), jnp.bfloat16)
    sems = pltpu.SemaphoreType.DMA((4,))
    last = pltpu.VMEM((-(-(rows + LANES) // LANES) * LANES, tokens), jnp.bfloat16)
    query_type = jax.ShapeDtypeStruct((width, tokens), jnp.bfloat16)
    state_type = jax.ShapeDtypeStruct((width, HEAD_DIM), jnp.float32)
    out_type = jax.ShapeDtypeStruct((2, width, tokens), jnp.bfloat16)
    one = 2 * width * depth * tokens

    read_scratch = [pltpu.VMEM((width, tokens), jnp.bfloat16), pltpu.SemaphoreType.DMA(())]
    sums = []
    for stream in range(2):
        ready, *_ = lax.optimization_barrier((far[stream], across_end[stream], *sums))
        far_end.append(partner_swap(ready, "head"))
        sums.append(call(
            partial_kernel, jax.ShapeDtypeStruct((3, width, tokens), jnp.float32), IN_VMEM,
            [IN_SMEM] + [ANYWHERE] * 4 + [IN_VMEM] * 3, [whole, sems], 3 * one,
        )(place, own[stream], near[stream], far[stream], across_end[stream], *matrices))
    prefix = query = out = None
    for stream in range(2):
        ties = (sums[1],) if stream == 0 else (total, query)
        state = call(
            functools.partial(state_kernel, count), state_type, IN_VMEM,
            [IN_SMEM] + [ANYWHERE] * 2 + [IN_VMEM] * 3 + [ANYWHERE] * len(ties), [last, sems], one // 2,
        )(place, across[stream], far_end[stream], *matrices[1:], sums[stream], *ties)
        query = call(
            functools.partial(query_kernel, count), query_type, IN_VMEM,
            [IN_SMEM] + [ANYWHERE] * 2 + [IN_VMEM] * 2 + [ANYWHERE], [last, sems], one // 4,
        )(place, across[stream], far_end[stream], matrices[0], sums[stream], state)
        total = sum_over(state, "tok")
        if stream == 0:
            prefix = entering(total, "group")
        kept = [] if out is None else [out]
        out = call(
            functools.partial(read_kernel, stream), out_type, ANYWHERE, [IN_VMEM] * 4 + [ANYWHERE] * len(kept),
            read_scratch, one // 20, {4: 0} if kept else None,
        )(prefix, total, query, gain_column, *kept)
    return jnp.swapaxes(out, 1, 2)


def solution(mesh):
    return jax.shard_map(
        local,
        mesh=mesh,
        in_specs=(
            P(None, ("group", "tok"), "head"),
            P(None, "head"),
            P(None, "head"),
            P(None, "head"),
            P("head"),
        ),
        out_specs=P(None, ("group", "tok"), "head"),
        check_vma=False,
    )
```

```python
import functools

import jax
import jax.numpy as jnp
from jax import lax
from jax.experimental import pallas as pl
from jax.experimental.pallas import tpu as pltpu
from jax.sharding import PartitionSpec as P

HEAD_DIM = 112
VMEM_LIMIT = 20 * 1024 * 1024
ANYWHERE = pl.BlockSpec(memory_space=pl.ANY)
IN_VMEM = pl.BlockSpec(memory_space=pltpu.VMEM)
IN_SMEM = pl.BlockSpec(memory_space=pltpu.SMEM)


def call(body, outs, out_specs, in_specs, scratch, flops, aliases=None):
    return pl.pallas_call(
        body,
        out_shape=outs,
        in_specs=in_specs,
        out_specs=out_specs,
        scratch_shapes=scratch,
        input_output_aliases=aliases or {},
        compiler_params=pltpu.CompilerParams(vmem_limit_bytes=VMEM_LIMIT),
        cost_estimate=pl.CostEstimate(flops=flops // 64, bytes_accessed=1 << 10, transcendentals=0),
    )


def rounded_dot(matrix, block):
    return jnp.dot(matrix, block, preferred_element_type=jnp.float32)


def token_tiles(tokens):
    width = 256 if tokens % 256 == 0 else tokens
    return width, tokens // width


def load_blocks(place, found, whole, sems):
    mine, inner = place[0], place[1]
    rows = found[0].shape[0]

    def at(flip):
        return whole.at[pl.ds(pl.multiple_of((mine ^ flip) * rows, 16), rows), :]

    for flip, source in enumerate(found):
        if isinstance(source, tuple):
            for want, ref in ((1, source[0]), (0, source[1])):

                @pl.when(inner == want)
                def _(ref=ref, flip=flip):
                    pltpu.make_async_copy(ref, at(flip), sems.at[flip]).start()
        else:
            pltpu.make_async_copy(source, at(flip), sems.at[flip]).start()
    for flip in range(len(found)):
        pltpu.make_async_copy(at(flip), at(flip), sems.at[flip]).wait()


def partial_kernel(place, b0, b1, b2i, b2o, wq, wk, wv, tie, sums, whole, sems):
    rows, tokens = b0.shape
    missing = pl.ds(pl.multiple_of((place[0] ^ 3) * rows, 16), rows)
    whole[missing, :] = jnp.zeros((rows, tokens), whole.dtype)
    load_blocks(place, [b0, b1, (b2i, b2o)], whole, sems)
    width, tiles = token_tiles(tokens)

    @pl.loop(0, tiles)
    def _(tile):
        columns = pl.ds(pl.multiple_of(tile * width, width), width)
        block = whole[:, columns]
        for k, matrix in enumerate((wk, wv, wq)):
            sums[k, :, columns] = rounded_dot(matrix[...], block)


def cut_kernel(count, place, *rest):
    matrices, (cut,) = rest[:-1], rest[-1:]
    rows = cut.shape[2]
    for owner in range(count):

        @pl.when((place[0] ^ 3) == owner)
        def _(owner=owner):
            for k, matrix in enumerate(matrices):
                cut[k] = matrix[:, owner * rows : (owner + 1) * rows]


def on_last(place, inner_ref, end_ref, body):
    for want, ref in ((1, inner_ref), (0, end_ref)):

        @pl.when(place[1] == want)
        def _(ref=ref):
            body(ref)


def state_kernel(place, inner_ref, end_ref, cut, sums, *rest):
    state = rest[-1]

    def body(block):
        key = (sums[0] + rounded_dot(cut[0], block[...])).astype(jnp.bfloat16)
        value = (sums[1] + rounded_dot(cut[1], block[...])).astype(jnp.bfloat16)
        key = jnp.maximum(key, 0)
        for start in range(0, key.shape[0], HEAD_DIM):
            rows = slice(start, start + HEAD_DIM)
            state[rows, :] = lax.dot_general(
                value[rows], key[rows], (((1,), (1,)), ((), ())), preferred_element_type=jnp.float32
            )

    on_last(place, inner_ref, end_ref, body)


def query_kernel(place, inner_ref, end_ref, cut, sums, tie, query):
    def body(block):
        row = (sums[2] + rounded_dot(cut[2], block[...])).astype(jnp.bfloat16)
        query[...] = jnp.maximum(row, 0)

    on_last(place, inner_ref, end_ref, body)


def read_kernel(stream, parts, query, gain, *rest):
    out, held, sem = rest[-3:]
    for start in range(0, query.shape[0], HEAD_DIM):
        rows = slice(start, start + HEAD_DIM)
        total = sum(part[rows, :].astype(jnp.float32) for part in rest[:parts])
        reading = rounded_dot(total.astype(jnp.bfloat16), query[rows, :])
        scale = lax.rsqrt(jnp.mean(reading * reading, axis=0, keepdims=True) + 1e-06)
        held[rows, :] = (reading * scale * gain[rows, :]).astype(jnp.bfloat16)
    copy = pltpu.make_async_copy(held, out.at[stream], sem)
    copy.start()
    copy.wait()


def partner_swap(value, axis):
    return lax.ppermute(value, axis, [(i, i ^ 1) for i in range(lax.axis_size(axis))])


def middle_swap(value, axis, other):
    wide, count = lax.axis_size(other), lax.axis_size(axis)
    pairs = []
    for j in range(wide):
        for i in range(count):
            if i in (1, 2):
                pairs.append((j * count + i, j * count + 3 - i))
            else:
                pairs.append((j * count + i, (j ^ 1 if j ^ 1 < wide else j) * count + i))
    return lax.ppermute(value, (other, axis), pairs)


def from_others(value, axis):
    count = lax.axis_size(axis)
    sent = value.astype(jnp.bfloat16)
    got = []
    for step in range(count - 1, 0, -1):
        pairs = [(i, (i + step) % count) for i in range(count)]
        if count & (count - 1) == 0:
            pairs = [(i, i ^ step) for i in range(count)]
        got.append(lax.ppermute(sent, axis, pairs))
    return got


def entering(value, axis):
    count = lax.axis_size(axis)
    total = lax.ppermute(value, axis, [(i, i + 1) for i in range(count - 1)])
    reach = 1
    while reach < count - 1:
        total = total + lax.ppermute(total, axis, [(i, i + reach) for i in range(count - reach)])
        reach *= 2
    return total


def local(streams, w_query, w_key, w_value, gain):
    count, mine = lax.axis_size("head"), lax.axis_index("head")
    rows, tokens = streams.shape[2], streams.shape[1]
    width = w_query.shape[1]
    depth = rows * count
    columns = jnp.swapaxes(streams, 1, 2)
    matrices = (w_query.T, w_key.T, w_value.T)
    gain_column = gain.reshape(width, 1)
    inner = (mine == 1) | (mine == 2)
    place = jnp.stack([mine.astype(jnp.int32), inner.astype(jnp.int32)])

    one = 2 * width * depth * tokens
    cut = call(
        functools.partial(cut_kernel, count), jax.ShapeDtypeStruct((3, width, rows), jnp.bfloat16), IN_VMEM,
        [IN_SMEM] + [IN_VMEM] * 3, [], one // 4,
    )(place, matrices[1], matrices[2], matrices[0])
    own, near, across, far, across_end, far_end = [], [], [], [], [], []
    for stream in range(2):
        if own:
            columns, own[0] = lax.optimization_barrier((columns, own[0]))
        own.append(columns[stream])
        near.append(partner_swap(own[stream], "head"))
        across.append(middle_swap(own[stream], "head", "group"))
    for stream in range(2):
        far.append(middle_swap(near[stream], "head", "group"))
        ready, *_ = lax.optimization_barrier((across[stream], near[stream], *([cut] if stream else [])))
        across_end.append(partner_swap(ready, "head"))
    whole = pltpu.VMEM((depth, tokens), jnp.bfloat16)
    sems = pltpu.SemaphoreType.DMA((4,))
    query_type = jax.ShapeDtypeStruct((width, tokens), jnp.bfloat16)
    state_type = jax.ShapeDtypeStruct((width, HEAD_DIM), jnp.float32)
    out_type = jax.ShapeDtypeStruct((2, width, tokens), jnp.bfloat16)

    read_scratch = [pltpu.VMEM((width, tokens), jnp.bfloat16), pltpu.SemaphoreType.DMA(())]
    sums = []
    for stream in range(2):
        ready, *_ = lax.optimization_barrier((far[stream], across_end[stream], *sums))
        far_end.append(partner_swap(ready, "head"))
        sums.append(call(
            partial_kernel, jax.ShapeDtypeStruct((3, width, tokens), jnp.float32), IN_VMEM,
            [IN_SMEM] + [ANYWHERE] * 4 + [IN_VMEM] * 3 + [ANYWHERE], [whole, sems], 3 * one,
        )(place, own[stream], near[stream], far[stream], across_end[stream], *matrices, cut))
    prefix = parts = query = out = None
    for stream in range(2):
        ties = (sums[1],) if stream == 0 else (parts[0], query)
        state = call(
            state_kernel, state_type, IN_VMEM,
            [IN_SMEM] + [IN_VMEM] * 4 + [ANYWHERE] * len(ties), [], one // 2,
        )(place, across[stream], far_end[stream], cut, sums[stream], *ties)
        query = call(
            query_kernel, query_type, IN_VMEM, [IN_SMEM] + [IN_VMEM] * 4 + [ANYWHERE], [], one // 4,
        )(place, across[stream], far_end[stream], cut, sums[stream], state)
        parts = [state, *from_others(state, "tok")]
        if stream == 0:
            parts = [sum(part.astype(jnp.float32) for part in parts)]
            prefix = entering(parts[0], "group")
        kept = [] if out is None else [out]
        out = call(
            functools.partial(read_kernel, stream, len(parts) + 1), out_type, ANYWHERE,
            [IN_VMEM] * (3 + len(parts)) + [ANYWHERE] * len(kept),
            read_scratch, one // 20, {3 + len(parts): 0} if kept else None,
        )(query, gain_column, prefix, *parts, *kept)
    return jnp.swapaxes(out, 1, 2)


def solution(mesh):
    return jax.shard_map(
        local,
        mesh=mesh,
        in_specs=(
            P(None, ("group", "tok"), "head"),
            P(None, "head"),
            P(None, "head"),
            P(None, "head"),
            P("head"),
        ),
        out_specs=P(None, ("group", "tok"), "head"),
        check_vma=False,
    )
```

```python
import functools

import jax
import jax.numpy as jnp
from jax import lax
from jax.experimental import pallas as pl
from jax.experimental.pallas import tpu as pltpu
from jax.sharding import PartitionSpec as P

HEAD_DIM = 112
VMEM_LIMIT = 20 * 1024 * 1024
ANYWHERE = pl.BlockSpec(memory_space=pl.ANY)
IN_VMEM = pl.BlockSpec(memory_space=pltpu.VMEM)
IN_SMEM = pl.BlockSpec(memory_space=pltpu.SMEM)


def call(body, outs, out_specs, in_specs, scratch, flops, aliases=None):
    return pl.pallas_call(
        body,
        out_shape=outs,
        in_specs=in_specs,
        out_specs=out_specs,
        scratch_shapes=scratch,
        input_output_aliases=aliases or {},
        compiler_params=pltpu.CompilerParams(vmem_limit_bytes=VMEM_LIMIT),
        cost_estimate=pl.CostEstimate(flops=flops // 64, bytes_accessed=1 << 10, transcendentals=0),
    )


def rounded_dot(matrix, block):
    return jnp.dot(matrix, block, preferred_element_type=jnp.float32)


def token_tiles(tokens):
    width = 256 if tokens % 256 == 0 else tokens
    return width, tokens // width


def load_blocks(place, found, whole, sems):
    mine, inner = place[0], place[1]
    rows = found[0].shape[0]

    def at(flip):
        return whole.at[pl.ds(pl.multiple_of((mine ^ flip) * rows, 16), rows), :]

    for flip, source in enumerate(found):
        if isinstance(source, tuple):
            for want, ref in ((1, source[0]), (0, source[1])):

                @pl.when(inner == want)
                def _(ref=ref, flip=flip):
                    pltpu.make_async_copy(ref, at(flip), sems.at[flip]).start()
        else:
            pltpu.make_async_copy(source, at(flip), sems.at[flip]).start()
    for flip in range(len(found)):
        pltpu.make_async_copy(at(flip), at(flip), sems.at[flip]).wait()


def partial_kernel(stream, place, own, near, b2i, b2o, wq, wk, wv, tie, sums, whole, sems):
    rows, tokens = b2i.shape
    missing = pl.ds(pl.multiple_of((place[0] ^ 3) * rows, 16), rows)
    whole[missing, :] = jnp.zeros((rows, tokens), whole.dtype)
    load_blocks(place, [own.at[stream], near.at[stream], (b2i, b2o)], whole, sems)
    width, tiles = token_tiles(tokens)

    @pl.loop(0, tiles)
    def _(tile):
        columns = pl.ds(pl.multiple_of(tile * width, width), width)
        block = whole[:, columns]
        for k, matrix in enumerate((wk, wv, wq)):
            sums[k, :, columns] = rounded_dot(matrix[...], block)


def cut_kernel(count, place, *rest):
    matrices, (cut,) = rest[:-1], rest[-1:]
    rows = cut.shape[2]
    for owner in range(count):

        @pl.when((place[0] ^ 3) == owner)
        def _(owner=owner):
            for k, matrix in enumerate(matrices):
                cut[k] = matrix[:, owner * rows : (owner + 1) * rows]


def on_last(place, inner_ref, end_ref, body):
    for want, ref in ((1, inner_ref), (0, end_ref)):

        @pl.when(place[1] == want)
        def _(ref=ref):
            body(ref)


def state_kernel(place, inner_ref, end_ref, cut, sums, *rest):
    state = rest[-1]

    def body(block):
        key = (sums[0] + rounded_dot(cut[0], block[...])).astype(jnp.bfloat16)
        value = (sums[1] + rounded_dot(cut[1], block[...])).astype(jnp.bfloat16)
        key = jnp.maximum(key, 0)
        for start in range(0, key.shape[0], HEAD_DIM):
            rows = slice(start, start + HEAD_DIM)
            state[rows, :] = lax.dot_general(
                value[rows], key[rows], (((1,), (1,)), ((), ())), preferred_element_type=jnp.float32
            )

    on_last(place, inner_ref, end_ref, body)


def query_kernel(place, inner_ref, end_ref, cut, sums, tie, query):
    def body(block):
        row = (sums[2] + rounded_dot(cut[2], block[...])).astype(jnp.bfloat16)
        query[...] = jnp.maximum(row, 0)

    on_last(place, inner_ref, end_ref, body)


def read_kernel(stream, parts, query, gain, *rest):
    out, held, sem = rest[-3:]
    for start in range(0, query.shape[0], HEAD_DIM):
        rows = slice(start, start + HEAD_DIM)
        total = sum(part[rows, :].astype(jnp.float32) for part in rest[:parts])
        reading = rounded_dot(total.astype(jnp.bfloat16), query[rows, :])
        scale = lax.rsqrt(jnp.mean(reading * reading, axis=0, keepdims=True) + 1e-06)
        held[rows, :] = (reading * scale * gain[rows, :]).astype(jnp.bfloat16)
    copy = pltpu.make_async_copy(held, out.at[stream], sem)
    copy.start()
    copy.wait()


def partner_swap(value, axis):
    return lax.ppermute(value, axis, [(i, i ^ 1) for i in range(lax.axis_size(axis))])


def middle_swap(value, axis, other):
    wide, count = lax.axis_size(other), lax.axis_size(axis)
    pairs = []
    for j in range(wide):
        for i in range(count):
            if i in (1, 2):
                pairs.append((j * count + i, j * count + 3 - i))
            else:
                pairs.append((j * count + i, (j ^ 1 if j ^ 1 < wide else j) * count + i))
    return lax.ppermute(value, (other, axis), pairs)


def from_others(value, axis):
    count = lax.axis_size(axis)
    sent = value.astype(jnp.bfloat16)
    got = []
    for step in range(count - 1, 0, -1):
        pairs = [(i, (i + step) % count) for i in range(count)]
        if count & (count - 1) == 0:
            pairs = [(i, i ^ step) for i in range(count)]
        got.append(lax.ppermute(sent, axis, pairs))
    return got


def entering(value, axis):
    count = lax.axis_size(axis)
    total = lax.ppermute(value, axis, [(i, i + 1) for i in range(count - 1)])
    reach = 1
    while reach < count - 1:
        total = total + lax.ppermute(total, axis, [(i, i + reach) for i in range(count - reach)])
        reach *= 2
    return total


def local(streams, w_query, w_key, w_value, gain):
    count, mine = lax.axis_size("head"), lax.axis_index("head")
    rows, tokens = streams.shape[2], streams.shape[1]
    width = w_query.shape[1]
    depth = rows * count
    columns = jnp.swapaxes(streams, 1, 2)
    matrices = (w_query.T, w_key.T, w_value.T)
    gain_column = gain.reshape(width, 1)
    inner = (mine == 1) | (mine == 2)
    place = jnp.stack([mine.astype(jnp.int32), inner.astype(jnp.int32)])

    one = 2 * width * depth * tokens
    cut = call(
        functools.partial(cut_kernel, count), jax.ShapeDtypeStruct((3, width, rows), jnp.bfloat16), IN_VMEM,
        [IN_SMEM] + [IN_VMEM] * 3, [], one // 4,
    )(place, matrices[1], matrices[2], matrices[0])
    across, far, across_end, far_end = [], [], [], []
    near = partner_swap(columns, "head")
    for stream in range(2):
        across.append(middle_swap(columns[stream], "head", "group"))
    for stream in range(2):
        far.append(middle_swap(near[stream], "head", "group"))
        ready, *_ = lax.optimization_barrier((across[stream], *([cut] if stream else [])))
        across_end.append(partner_swap(ready, "head"))
    whole = pltpu.VMEM((depth, tokens), jnp.bfloat16)
    sems = pltpu.SemaphoreType.DMA((4,))
    query_type = jax.ShapeDtypeStruct((width, tokens), jnp.bfloat16)
    state_type = jax.ShapeDtypeStruct((width, HEAD_DIM), jnp.float32)
    out_type = jax.ShapeDtypeStruct((2, width, tokens), jnp.bfloat16)

    read_scratch = [pltpu.VMEM((width, tokens), jnp.bfloat16), pltpu.SemaphoreType.DMA(())]
    sums = []
    for stream in range(2):
        ready, *_ = lax.optimization_barrier((far[stream], across_end[stream], *sums))
        far_end.append(partner_swap(ready, "head"))
        sums.append(call(
            functools.partial(partial_kernel, stream), jax.ShapeDtypeStruct((3, width, tokens), jnp.float32), IN_VMEM,
            [IN_SMEM] + [ANYWHERE] * 4 + [IN_VMEM] * 3 + [ANYWHERE], [whole, sems], 3 * one,
        )(place, columns, near, far[stream], across_end[stream], *matrices, cut))
    prefix = parts = query = out = None
    for stream in range(2):
        ties = (sums[1],) if stream == 0 else (parts[0], query)
        state = call(
            state_kernel, state_type, IN_VMEM,
            [IN_SMEM] + [IN_VMEM] * 4 + [ANYWHERE] * len(ties), [], one // 2,
        )(place, across[stream], far_end[stream], cut, sums[stream], *ties)
        query = call(
            query_kernel, query_type, IN_VMEM, [IN_SMEM] + [IN_VMEM] * 4 + [ANYWHERE], [], one // 4,
        )(place, across[stream], far_end[stream], cut, sums[stream], state)
        parts = [state, *from_others(state, "tok")]
        if stream == 0:
            query, *parts = lax.optimization_barrier((query, *parts))
            parts = [sum(part.astype(jnp.float32) for part in parts)]
            prefix = entering(parts[0], "group")
        kept = [] if out is None else [out]
        out = call(
            functools.partial(read_kernel, stream, len(parts) + 1), out_type, ANYWHERE,
            [IN_VMEM] * (3 + len(parts)) + [ANYWHERE] * len(kept),
            read_scratch, one // 20, {3 + len(parts): 0} if kept else None,
        )(query, gain_column, prefix, *parts, *kept)
    return jnp.swapaxes(out, 1, 2)


def solution(mesh):
    return jax.shard_map(
        local,
        mesh=mesh,
        in_specs=(
            P(None, ("group", "tok"), "head"),
            P(None, "head"),
            P(None, "head"),
            P(None, "head"),
            P("head"),
        ),
        out_specs=P(None, ("group", "tok"), "head"),
        check_vma=False,
    )
```

```python
import functools

import jax
import jax.numpy as jnp
from jax import lax
from jax.experimental import pallas as pl
from jax.experimental.pallas import tpu as pltpu
from jax.sharding import PartitionSpec as P

HEAD_DIM = 112
VMEM_LIMIT = 20 * 1024 * 1024
ANYWHERE = pl.BlockSpec(memory_space=pl.ANY)
IN_VMEM = pl.BlockSpec(memory_space=pltpu.VMEM)
IN_SMEM = pl.BlockSpec(memory_space=pltpu.SMEM)


def call(body, outs, out_specs, in_specs, scratch, flops, aliases=None):
    return pl.pallas_call(
        body,
        out_shape=outs,
        in_specs=in_specs,
        out_specs=out_specs,
        scratch_shapes=scratch,
        input_output_aliases=aliases or {},
        compiler_params=pltpu.CompilerParams(vmem_limit_bytes=VMEM_LIMIT),
        cost_estimate=pl.CostEstimate(flops=flops // 64, bytes_accessed=1 << 10, transcendentals=0),
    )


def rounded_dot(matrix, block):
    return jnp.dot(matrix, block, preferred_element_type=jnp.float32)


def token_tiles(tokens):
    width = 256 if tokens % 256 == 0 else tokens
    return width, tokens // width


def load_blocks(place, found, whole, sems):
    mine, inner = place[0], place[1]
    rows = found[0].shape[0]

    def at(flip):
        return whole.at[pl.ds(pl.multiple_of((mine ^ flip) * rows, 16), rows), :]

    for flip, source in enumerate(found):
        if isinstance(source, tuple):
            for want, ref in ((1, source[0]), (0, source[1])):

                @pl.when(inner == want)
                def _(ref=ref, flip=flip):
                    pltpu.make_async_copy(ref, at(flip), sems.at[flip]).start()
        else:
            pltpu.make_async_copy(source, at(flip), sems.at[flip]).start()
    for flip in range(len(found)):
        pltpu.make_async_copy(at(flip), at(flip), sems.at[flip]).wait()


def partial_kernel(stream, place, own, near, b2i, b2o, wq, wk, wv, tie, sums, whole, sems):
    rows, tokens = b2i.shape
    missing = pl.ds(pl.multiple_of((place[0] ^ 3) * rows, 16), rows)
    whole[missing, :] = jnp.zeros((rows, tokens), whole.dtype)
    load_blocks(place, [own.at[stream], near.at[stream], (b2i, b2o)], whole, sems)
    width, tiles = token_tiles(tokens)

    @pl.loop(0, tiles)
    def _(tile):
        columns = pl.ds(pl.multiple_of(tile * width, width), width)
        block = whole[:, columns]
        for k, matrix in enumerate((wk, wv, wq)):
            sums[k, :, columns] = rounded_dot(matrix[...], block)


def cut_kernel(count, place, *rest):
    matrices, (cut,) = rest[:-1], rest[-1:]
    rows = cut.shape[2]
    for owner in range(count):

        @pl.when((place[0] ^ 3) == owner)
        def _(owner=owner):
            for k, matrix in enumerate(matrices):
                cut[k] = matrix[:, owner * rows : (owner + 1) * rows]


def on_last(place, inner_ref, end_ref, body):
    for want, ref in ((1, inner_ref), (0, end_ref)):

        @pl.when(place[1] == want)
        def _(ref=ref):
            body(ref)


def state_kernel(place, inner_ref, end_ref, cut, sums, *rest):
    state = rest[-1]

    def body(block):
        key = (sums[0] + rounded_dot(cut[0], block[...])).astype(jnp.bfloat16)
        value = (sums[1] + rounded_dot(cut[1], block[...])).astype(jnp.bfloat16)
        key = jnp.maximum(key, 0)
        for start in range(0, key.shape[0], HEAD_DIM):
            rows = slice(start, start + HEAD_DIM)
            state[rows, :] = lax.dot_general(
                value[rows], key[rows], (((1,), (1,)), ((), ())), preferred_element_type=jnp.float32
            )

    on_last(place, inner_ref, end_ref, body)


def query_kernel(place, inner_ref, end_ref, cut, sums, tie, query):
    def body(block):
        row = (sums[2] + rounded_dot(cut[2], block[...])).astype(jnp.bfloat16)
        query[...] = jnp.maximum(row, 0)

    on_last(place, inner_ref, end_ref, body)


def read_kernel(stream, parts, query, gain, *rest):
    out, held, sems = rest[-3:]
    copies = []
    for start in range(0, query.shape[0], HEAD_DIM):
        rows = slice(start, start + HEAD_DIM)
        total = sum(part[rows, :].astype(jnp.float32) for part in rest[:parts])
        reading = rounded_dot(total.astype(jnp.bfloat16), query[rows, :])
        scale = lax.rsqrt(jnp.mean(reading * reading, axis=0, keepdims=True) + 1e-06)
        held[rows, :] = (reading * scale * gain[rows, :]).astype(jnp.bfloat16)
        copies.append(pltpu.make_async_copy(held.at[rows, :], out.at[stream, rows, :], sems.at[len(copies)]))
        copies[-1].start()
    for copy in copies:
        copy.wait()


def partner_swap(value, axis):
    return lax.ppermute(value, axis, [(i, i ^ 1) for i in range(lax.axis_size(axis))])


def middle_swap(value, axis, other):
    wide, count = lax.axis_size(other), lax.axis_size(axis)
    pairs = []
    for j in range(wide):
        for i in range(count):
            if i in (1, 2):
                pairs.append((j * count + i, j * count + 3 - i))
            else:
                pairs.append((j * count + i, (j ^ 1 if j ^ 1 < wide else j) * count + i))
    return lax.ppermute(value, (other, axis), pairs)


def from_others(value, axis):
    count = lax.axis_size(axis)
    sent = value.astype(jnp.bfloat16)
    got = []
    for step in range(count - 1, 0, -1):
        pairs = [(i, (i + step) % count) for i in range(count)]
        if count & (count - 1) == 0:
            pairs = [(i, i ^ step) for i in range(count)]
        got.append(lax.ppermute(sent, axis, pairs))
    return got


def pairwise_sum(value, axis, other):
    count, wide = lax.axis_size(axis), lax.axis_size(other)
    if count & (count - 1):
        return [value, *from_others(value, axis)]
    steps = [1 << b for b in range(count.bit_length() - 1)]
    terms = [value]
    for k in range(len(steps)):
        value = sum(term.astype(jnp.float32) for term in terms)
        pairs = []
        for j in range(wide):
            step = steps[-1 - k] if j % 2 else steps[k]
            pairs += [(j * count + i, j * count + (i ^ step)) for i in range(count)]
        terms = [value, lax.ppermute(value.astype(jnp.bfloat16), (other, axis), pairs)]
    return terms


def entering(value, axis):
    count = lax.axis_size(axis)
    total = lax.ppermute(value, axis, [(i, i + 1) for i in range(count - 1)])
    reach = 1
    while reach < count - 1:
        total = total + lax.ppermute(total, axis, [(i, i + reach) for i in range(count - reach)])
        reach *= 2
    return total


def local(streams, w_query, w_key, w_value, gain):
    count, mine = lax.axis_size("head"), lax.axis_index("head")
    rows, tokens = streams.shape[2], streams.shape[1]
    width = w_query.shape[1]
    depth = rows * count
    columns = jnp.swapaxes(streams, 1, 2)
    matrices = (w_query.T, w_key.T, w_value.T)
    gain_column = gain.reshape(width, 1)
    inner = (mine == 1) | (mine == 2)
    place = jnp.stack([mine.astype(jnp.int32), inner.astype(jnp.int32)])

    one = 2 * width * depth * tokens
    cut = call(
        functools.partial(cut_kernel, count), jax.ShapeDtypeStruct((3, width, rows), jnp.bfloat16), IN_VMEM,
        [IN_SMEM] + [IN_VMEM] * 3, [], one // 4,
    )(place, matrices[1], matrices[2], matrices[0])
    across, far, across_end, far_end = [], [], [], []
    near = partner_swap(columns, "head")
    for stream in range(2):
        across.append(middle_swap(columns[stream], "head", "group"))
    for stream in range(2):
        far.append(middle_swap(near[stream], "head", "group"))
        ready, *_ = lax.optimization_barrier((across[stream], *([cut] if stream else [])))
        across_end.append(partner_swap(ready, "head"))
    whole = pltpu.VMEM((depth, tokens), jnp.bfloat16)
    sems = pltpu.SemaphoreType.DMA((4,))
    query_type = jax.ShapeDtypeStruct((width, tokens), jnp.bfloat16)
    state_type = jax.ShapeDtypeStruct((width, HEAD_DIM), jnp.float32)
    out_type = jax.ShapeDtypeStruct((2, width, tokens), jnp.bfloat16)

    read_scratch = [pltpu.VMEM((width, tokens), jnp.bfloat16), pltpu.SemaphoreType.DMA((width // HEAD_DIM,))]
    sums = []
    for stream in range(2):
        ready, *_ = lax.optimization_barrier((far[stream], across_end[stream], *sums))
        far_end.append(partner_swap(ready, "head"))
        sums.append(call(
            functools.partial(partial_kernel, stream), jax.ShapeDtypeStruct((3, width, tokens), jnp.float32), IN_VMEM,
            [IN_SMEM] + [ANYWHERE] * 4 + [IN_VMEM] * 3 + [ANYWHERE], [whole, sems], 3 * one,
        )(place, columns, near, far[stream], across_end[stream], *matrices, cut))
    queries, query, clean = [], None, None
    for stream in range(2):
        ties = (sums[1],) if stream == 0 else (clean, query)
        state = call(
            state_kernel, state_type, IN_VMEM,
            [IN_SMEM] + [IN_VMEM] * 4 + [ANYWHERE] * len(ties), [], one // 2,
        )(place, across[stream], far_end[stream], cut, sums[stream], *ties)
        query = call(
            query_kernel, query_type, IN_VMEM, [IN_SMEM] + [IN_VMEM] * 4 + [ANYWHERE], [], one // 4,
        )(place, across[stream], far_end[stream], cut, sums[stream], state)
        queries.append(query)
        if stream == 0:
            query, *got = lax.optimization_barrier((query, *from_others(state, "tok")))
            clean = state + sum(part.astype(jnp.float32) for part in got)
    clean, state = lax.optimization_barrier((clean, state))
    prefix = entering(clean, "group")
    out = None
    for stream, parts in enumerate(([clean], pairwise_sum(state, "tok", "group"))):
        kept = [] if out is None else [out]
        out = call(
            functools.partial(read_kernel, stream, len(parts) + 1), out_type, ANYWHERE,
            [IN_VMEM] * (3 + len(parts)) + [ANYWHERE] * len(kept),
            read_scratch, one // 20, {3 + len(parts): 0} if kept else None,
        )(queries[stream], gain_column, prefix, *parts, *kept)
    return jnp.swapaxes(out, 1, 2)


def solution(mesh):
    return jax.shard_map(
        local,
        mesh=mesh,
        in_specs=(
            P(None, ("group", "tok"), "head"),
            P(None, "head"),
            P(None, "head"),
            P(None, "head"),
            P("head"),
        ),
        out_specs=P(None, ("group", "tok"), "head"),
        check_vma=False,
    )
```

```python
import functools

import jax
import jax.numpy as jnp
from jax import lax
from jax.experimental import pallas as pl
from jax.experimental.pallas import tpu as pltpu
from jax.sharding import PartitionSpec as P

HEAD_DIM = 112
VMEM_LIMIT = 20 * 1024 * 1024
ANYWHERE = pl.BlockSpec(memory_space=pl.ANY)
IN_VMEM = pl.BlockSpec(memory_space=pltpu.VMEM)
IN_SMEM = pl.BlockSpec(memory_space=pltpu.SMEM)


def call(body, outs, out_specs, in_specs, scratch, flops, aliases=None):
    return pl.pallas_call(
        body,
        out_shape=outs,
        in_specs=in_specs,
        out_specs=out_specs,
        scratch_shapes=scratch,
        input_output_aliases=aliases or {},
        compiler_params=pltpu.CompilerParams(vmem_limit_bytes=VMEM_LIMIT),
        cost_estimate=pl.CostEstimate(flops=flops // 64, bytes_accessed=1 << 10, transcendentals=0),
    )


def rounded_dot(matrix, block):
    return jnp.dot(matrix, block, preferred_element_type=jnp.float32)


def token_tiles(tokens):
    width = 256 if tokens % 256 == 0 else tokens
    return width, tokens // width


def load_blocks(place, found, whole, sems):
    mine, inner = place[0], place[1]
    rows = found[0].shape[0]

    def at(flip):
        return whole.at[pl.ds(pl.multiple_of((mine ^ flip) * rows, 16), rows), :]

    for flip, source in enumerate(found):
        if isinstance(source, tuple):
            for want, ref in ((1, source[0]), (0, source[1])):

                @pl.when(inner == want)
                def _(ref=ref, flip=flip):
                    pltpu.make_async_copy(ref, at(flip), sems.at[flip]).start()
        else:
            pltpu.make_async_copy(source, at(flip), sems.at[flip]).start()
    for flip in range(len(found)):
        pltpu.make_async_copy(at(flip), at(flip), sems.at[flip]).wait()


def partial_kernel(stream, place, own, near, b2i, b2o, wq, wk, wv, tie, sums, whole, sems):
    rows, tokens = b2i.shape
    missing = pl.ds(pl.multiple_of((place[0] ^ 3) * rows, 16), rows)
    whole[missing, :] = jnp.zeros((rows, tokens), whole.dtype)
    load_blocks(place, [own.at[stream], near.at[stream], (b2i, b2o)], whole, sems)
    width, tiles = token_tiles(tokens)

    @pl.loop(0, tiles)
    def _(tile):
        columns = pl.ds(pl.multiple_of(tile * width, width), width)
        block = whole[:, columns]
        for k, matrix in enumerate((wk, wv, wq)):
            sums[k, :, columns] = rounded_dot(matrix[...], block)


def cut_kernel(count, place, *rest):
    matrices, (cut,) = rest[:-1], rest[-1:]
    rows = cut.shape[2]
    for owner in range(count):

        @pl.when((place[0] ^ 3) == owner)
        def _(owner=owner):
            for k, matrix in enumerate(matrices):
                cut[k] = matrix[:, owner * rows : (owner + 1) * rows]


def on_last(place, inner_ref, end_ref, body):
    for want, ref in ((1, inner_ref), (0, end_ref)):

        @pl.when(place[1] == want)
        def _(ref=ref):
            body(ref)


def state_kernel(place, inner_ref, end_ref, cut, sums, *rest):
    state = rest[-1]

    def body(block):
        key = (sums[0] + rounded_dot(cut[0], block[...])).astype(jnp.bfloat16)
        value = (sums[1] + rounded_dot(cut[1], block[...])).astype(jnp.bfloat16)
        key = jnp.maximum(key, 0)
        for start in range(0, key.shape[0], HEAD_DIM):
            rows = slice(start, start + HEAD_DIM)
            state[rows, :] = lax.dot_general(
                value[rows], key[rows], (((1,), (1,)), ((), ())), preferred_element_type=jnp.float32
            )

    on_last(place, inner_ref, end_ref, body)


def query_kernel(place, inner_ref, end_ref, cut, sums, tie, query):
    def body(block):
        row = (sums[2] + rounded_dot(cut[2], block[...])).astype(jnp.bfloat16)
        query[...] = jnp.maximum(row, 0)

    on_last(place, inner_ref, end_ref, body)


def read_kernel(stream, parts, query, gain, *rest):
    out, held, sems = rest[-3:]
    copies = []
    for start in range(0, query.shape[0], HEAD_DIM):
        rows = slice(start, start + HEAD_DIM)
        total = sum(part[rows, :].astype(jnp.float32) for part in rest[:parts])
        reading = rounded_dot(total.astype(jnp.bfloat16), query[rows, :])
        scale = lax.rsqrt(jnp.mean(reading * reading, axis=0, keepdims=True) + 1e-06)
        held[rows, :] = (reading * scale * gain[rows, :]).astype(jnp.bfloat16)
        copies.append(pltpu.make_async_copy(held.at[rows, :], out.at[stream, rows, :], sems.at[len(copies)]))
        copies[-1].start()
    for copy in copies:
        copy.wait()


def partner_swap(value, axis):
    return lax.ppermute(value, axis, [(i, i ^ 1) for i in range(lax.axis_size(axis))])


def middle_swap(value, axis, other):
    wide, count = lax.axis_size(other), lax.axis_size(axis)
    pairs = []
    for j in range(wide):
        for i in range(count):
            if i in (1, 2):
                pairs.append((j * count + i, j * count + 3 - i))
            else:
                pairs.append((j * count + i, (j ^ 1 if j ^ 1 < wide else j) * count + i))
    return lax.ppermute(value, (other, axis), pairs)


def from_others(value, axis):
    count = lax.axis_size(axis)
    sent = value.astype(jnp.bfloat16)
    got = []
    for step in range(count - 1, 0, -1):
        pairs = [(i, (i + step) % count) for i in range(count)]
        if count & (count - 1) == 0:
            pairs = [(i, i ^ step) for i in range(count)]
        got.append(lax.ppermute(sent, axis, pairs))
    return got


def entering(value, axis):
    count, mine = lax.axis_size(axis), lax.axis_index(axis)

    def earlier(value, reach):
        sent = lax.ppermute(value.astype(jnp.bfloat16), axis, [(i, (i + reach) % count) for i in range(count)])
        return jnp.where(mine >= reach, sent.astype(jnp.float32), 0.0)

    total, reach = earlier(value, 1), 1
    while reach < count - 1:
        total, reach = total + earlier(total, reach), 2 * reach
    return total


def local(streams, w_query, w_key, w_value, gain):
    count, mine = lax.axis_size("head"), lax.axis_index("head")
    rows, tokens = streams.shape[2], streams.shape[1]
    width = w_query.shape[1]
    depth = rows * count
    columns = jnp.swapaxes(streams, 1, 2)
    matrices = (w_query.T, w_key.T, w_value.T)
    gain_column = gain.reshape(width, 1)
    inner = (mine == 1) | (mine == 2)
    place = jnp.stack([mine.astype(jnp.int32), inner.astype(jnp.int32)])

    one = 2 * width * depth * tokens
    cut = call(
        functools.partial(cut_kernel, count), jax.ShapeDtypeStruct((3, width, rows), jnp.bfloat16), IN_VMEM,
        [IN_SMEM] + [IN_VMEM] * 3, [], one // 4,
    )(place, matrices[1], matrices[2], matrices[0])
    across, far, across_end, far_end = [], [], [], []
    near = partner_swap(columns, "head")
    for stream in range(2):
        across.append(middle_swap(columns[stream], "head", "group"))
    for stream in range(2):
        far.append(middle_swap(near[stream], "head", "group"))
        ready, *_ = lax.optimization_barrier((across[stream], *([cut] if stream else [])))
        across_end.append(partner_swap(ready, "head"))
    whole = pltpu.VMEM((depth, tokens), jnp.bfloat16)
    sems = pltpu.SemaphoreType.DMA((4,))
    query_type = jax.ShapeDtypeStruct((width, tokens), jnp.bfloat16)
    state_type = jax.ShapeDtypeStruct((width, HEAD_DIM), jnp.float32)
    out_type = jax.ShapeDtypeStruct((2, width, tokens), jnp.bfloat16)

    read_scratch = [pltpu.VMEM((width, tokens), jnp.bfloat16), pltpu.SemaphoreType.DMA((width // HEAD_DIM,))]
    sums = []
    for stream in range(2):
        ready, *_ = lax.optimization_barrier((far[stream], across_end[stream], *sums))
        far_end.append(partner_swap(ready, "head"))
        sums.append(call(
            functools.partial(partial_kernel, stream), jax.ShapeDtypeStruct((3, width, tokens), jnp.float32), IN_VMEM,
            [IN_SMEM] + [ANYWHERE] * 4 + [IN_VMEM] * 3 + [ANYWHERE], [whole, sems], 3 * one,
        )(place, columns, near, far[stream], across_end[stream], *matrices, cut))
    queries, query, clean = [], None, None
    for stream in range(2):
        ties = (sums[1],) if stream == 0 else (clean, query)
        state = call(
            state_kernel, state_type, IN_VMEM,
            [IN_SMEM] + [IN_VMEM] * 4 + [ANYWHERE] * len(ties), [], one // 2,
        )(place, across[stream], far_end[stream], cut, sums[stream], *ties)
        query = call(
            query_kernel, query_type, IN_VMEM, [IN_SMEM] + [IN_VMEM] * 4 + [ANYWHERE], [], one // 4,
        )(place, across[stream], far_end[stream], cut, sums[stream], state)
        queries.append(query)
        if stream == 0:
            query, *got = lax.optimization_barrier((query, *from_others(state, "tok")))
            clean = state + sum(part.astype(jnp.float32) for part in got)
            prefix = entering(clean, "group")
    out = None
    for stream, parts in enumerate(([clean], [state, *from_others(state, "tok")])):
        kept = [] if out is None else [out]
        out = call(
            functools.partial(read_kernel, stream, len(parts) + 1), out_type, ANYWHERE,
            [IN_VMEM] * (3 + len(parts)) + [ANYWHERE] * len(kept),
            read_scratch, one // 20, {3 + len(parts): 0} if kept else None,
        )(queries[stream], gain_column, prefix, *parts, *kept)
    return jnp.swapaxes(out, 1, 2)


def solution(mesh):
    return jax.shard_map(
        local,
        mesh=mesh,
        in_specs=(
            P(None, ("group", "tok"), "head"),
            P(None, "head"),
            P(None, "head"),
            P(None, "head"),
            P("head"),
        ),
        out_specs=P(None, ("group", "tok"), "head"),
        check_vma=False,
    )
```

```python
import functools

import jax
import jax.numpy as jnp
from jax import lax
from jax.experimental import pallas as pl
from jax.experimental.pallas import tpu as pltpu
from jax.sharding import PartitionSpec as P

HEAD_DIM = 112
VMEM_LIMIT = 8 * 1024 * 1024
ANYWHERE = pl.BlockSpec(memory_space=pl.ANY)
IN_VMEM = pl.BlockSpec(memory_space=pltpu.VMEM)
IN_SMEM = pl.BlockSpec(memory_space=pltpu.SMEM)


def call(body, outs, out_specs, in_specs, scratch, flops, aliases=None):
    return pl.pallas_call(
        body,
        out_shape=outs,
        in_specs=in_specs,
        out_specs=out_specs,
        scratch_shapes=scratch,
        input_output_aliases=aliases or {},
        compiler_params=pltpu.CompilerParams(vmem_limit_bytes=VMEM_LIMIT),
        cost_estimate=pl.CostEstimate(flops=flops // 64, bytes_accessed=1 << 10, transcendentals=0),
    )


def rounded_dot(matrix, block):
    return jnp.dot(matrix, block, preferred_element_type=jnp.float32)


def token_tiles(tokens):
    width = 256 if tokens % 256 == 0 else tokens
    return width, tokens // width


def load_blocks(place, found, whole, sems):
    mine, inner = place[0], place[1]
    rows = found[0].shape[0]

    def at(flip):
        return whole.at[pl.ds(pl.multiple_of((mine ^ flip) * rows, 16), rows), :]

    for flip, source in enumerate(found):
        if isinstance(source, tuple):
            for want, ref in ((1, source[0]), (0, source[1])):

                @pl.when(inner == want)
                def _(ref=ref, flip=flip):
                    pltpu.make_async_copy(ref, at(flip), sems.at[flip]).start()
        else:
            pltpu.make_async_copy(source, at(flip), sems.at[flip]).start()
    for flip in range(len(found)):
        pltpu.make_async_copy(at(flip), at(flip), sems.at[flip]).wait()


def partial_kernel(stream, place, own, near, b2i, b2o, wq, wk, wv, tie, sums, whole, sems):
    rows, tokens = b2i.shape
    missing = pl.ds(pl.multiple_of((place[0] ^ 3) * rows, 16), rows)
    whole[missing, :] = jnp.zeros((rows, tokens), whole.dtype)
    load_blocks(place, [own.at[stream], near.at[stream], (b2i, b2o)], whole, sems)
    width, tiles = token_tiles(tokens)

    @pl.loop(0, tiles)
    def _(tile):
        columns = pl.ds(pl.multiple_of(tile * width, width), width)
        block = whole[:, columns]
        for k, matrix in enumerate((wk, wv, wq)):
            sums[k, :, columns] = rounded_dot(matrix[...], block)


def cut_kernel(count, place, *rest):
    matrices, (cut,) = rest[:-1], rest[-1:]
    rows = cut.shape[2]
    for owner in range(count):

        @pl.when((place[0] ^ 3) == owner)
        def _(owner=owner):
            for k, matrix in enumerate(matrices):
                cut[k] = matrix[:, owner * rows : (owner + 1) * rows]


def on_last(place, inner_ref, end_ref, body):
    for want, ref in ((1, inner_ref), (0, end_ref)):

        @pl.when(place[1] == want)
        def _(ref=ref):
            body(ref)


def state_kernel(place, inner_ref, end_ref, cut, sums, *rest):
    state = rest[-1]

    def body(block):
        key = (sums[0] + rounded_dot(cut[0], block[...])).astype(jnp.bfloat16)
        value = (sums[1] + rounded_dot(cut[1], block[...])).astype(jnp.bfloat16)
        key = jnp.maximum(key, 0)
        for start in range(0, key.shape[0], HEAD_DIM):
            rows = slice(start, start + HEAD_DIM)
            state[rows, :] = lax.dot_general(
                value[rows], key[rows], (((1,), (1,)), ((), ())), preferred_element_type=jnp.float32
            )

    on_last(place, inner_ref, end_ref, body)


def query_kernel(place, inner_ref, end_ref, cut, sums, tie, query):
    def body(block):
        row = (sums[2] + rounded_dot(cut[2], block[...])).astype(jnp.bfloat16)
        query[...] = jnp.maximum(row, 0)

    on_last(place, inner_ref, end_ref, body)


def read_kernel(stream, parts, query, gain, *rest):
    out, held, sems = rest[-3:]
    copies = []
    for start in range(0, query.shape[0], HEAD_DIM):
        rows = slice(start, start + HEAD_DIM)
        total = sum(part[rows, :].astype(jnp.float32) for part in rest[:parts])
        reading = rounded_dot(total.astype(jnp.bfloat16), query[rows, :])
        scale = lax.rsqrt(jnp.mean(reading * reading, axis=0, keepdims=True) + 1e-06)
        held[rows, :] = (reading * scale * gain[rows, :]).astype(jnp.bfloat16)
        copies.append(pltpu.make_async_copy(held.at[rows, :], out.at[stream, rows, :], sems.at[len(copies)]))
        copies[-1].start()
    for copy in copies:
        copy.wait()


def partner_swap(value, axis):
    return lax.ppermute(value, axis, [(i, i ^ 1) for i in range(lax.axis_size(axis))])


def middle_swap(value, axis, other):
    wide, count = lax.axis_size(other), lax.axis_size(axis)
    pairs = []
    for j in range(wide):
        for i in range(count):
            if i in (1, 2):
                pairs.append((j * count + i, j * count + 3 - i))
            else:
                pairs.append((j * count + i, (j ^ 1 if j ^ 1 < wide else j) * count + i))
    return lax.ppermute(value, (other, axis), pairs)


def from_others(value, axis):
    count = lax.axis_size(axis)
    sent = value.astype(jnp.bfloat16)
    got = []
    for step in range(count - 1, 0, -1):
        pairs = [(i, (i + step) % count) for i in range(count)]
        if count & (count - 1) == 0:
            pairs = [(i, i ^ step) for i in range(count)]
        got.append(lax.ppermute(sent, axis, pairs))
    return got


def entering(value, axis):
    count, mine = lax.axis_size(axis), lax.axis_index(axis)

    def earlier(value, reach):
        sent = lax.ppermute(value.astype(jnp.bfloat16), axis, [(i, (i + reach) % count) for i in range(count)])
        return jnp.where(mine >= reach, sent.astype(jnp.float32), 0.0)

    total, reach = earlier(value, 1), 1
    while reach < count - 1:
        total, reach = total + earlier(total, reach), 2 * reach
    return total


def local(streams, w_query, w_key, w_value, gain):
    count, mine = lax.axis_size("head"), lax.axis_index("head")
    rows, tokens = streams.shape[2], streams.shape[1]
    width = w_query.shape[1]
    depth = rows * count
    columns = jnp.swapaxes(streams, 1, 2)
    matrices = (w_query.T, w_key.T, w_value.T)
    gain_column = gain.reshape(width, 1)
    inner = (mine == 1) | (mine == 2)
    place = jnp.stack([mine.astype(jnp.int32), inner.astype(jnp.int32)])

    one = 2 * width * depth * tokens
    cut = call(
        functools.partial(cut_kernel, count), jax.ShapeDtypeStruct((3, width, rows), jnp.bfloat16), IN_VMEM,
        [IN_SMEM] + [IN_VMEM] * 3, [], one // 4,
    )(place, matrices[1], matrices[2], matrices[0])
    across, far, across_end, far_end = [], [], [], []
    near = partner_swap(columns, "head")
    for stream in range(2):
        across.append(middle_swap(columns[stream], "head", "group"))
    for stream in range(2):
        far.append(middle_swap(near[stream], "head", "group"))
        ready, *_ = lax.optimization_barrier((across[stream], *([cut] if stream else [])))
        across_end.append(partner_swap(ready, "head"))
    whole = pltpu.VMEM((depth, tokens), jnp.bfloat16)
    sems = pltpu.SemaphoreType.DMA((4,))
    query_type = jax.ShapeDtypeStruct((width, tokens), jnp.bfloat16)
    state_type = jax.ShapeDtypeStruct((width, HEAD_DIM), jnp.float32)
    out_type = jax.ShapeDtypeStruct((2, width, tokens), jnp.bfloat16)

    read_scratch = [pltpu.VMEM((width, tokens), jnp.bfloat16), pltpu.SemaphoreType.DMA((width // HEAD_DIM,))]
    sums = []
    for stream in range(2):
        ready, *_ = lax.optimization_barrier((far[stream], across_end[stream], *sums))
        far_end.append(partner_swap(ready, "head"))
        sums.append(call(
            functools.partial(partial_kernel, stream), jax.ShapeDtypeStruct((3, width, tokens), jnp.float32), IN_VMEM,
            [IN_SMEM] + [ANYWHERE] * 4 + [IN_VMEM] * 3 + [ANYWHERE], [whole, sems], 3 * one,
        )(place, columns, near, far[stream], across_end[stream], *matrices, cut))
    queries, query, clean = [], None, None
    for stream in range(2):
        ties = (sums[1],) if stream == 0 else (clean, query)
        state = call(
            state_kernel, state_type, IN_VMEM,
            [IN_SMEM] + [IN_VMEM] * 4 + [ANYWHERE] * len(ties), [], one // 2,
        )(place, across[stream], far_end[stream], cut, sums[stream], *ties)
        query = call(
            query_kernel, query_type, IN_VMEM, [IN_SMEM] + [IN_VMEM] * 4 + [ANYWHERE], [], one // 4,
        )(place, across[stream], far_end[stream], cut, sums[stream], state)
        queries.append(query)
        if stream == 0:
            query, *got = lax.optimization_barrier((query, *from_others(state, "tok")))
            clean = state + sum(part.astype(jnp.float32) for part in got)
            prefix = entering(clean, "group")
    out = None
    for stream, parts in enumerate(([clean], [state, *from_others(state, "tok")])):
        kept = [] if out is None else [out]
        out = call(
            functools.partial(read_kernel, stream, len(parts) + 1), out_type, ANYWHERE,
            [IN_VMEM] * (3 + len(parts)) + [ANYWHERE] * len(kept),
            read_scratch, one // 20, {3 + len(parts): 0} if kept else None,
        )(queries[stream], gain_column, prefix, *parts, *kept)
    return jnp.swapaxes(out, 1, 2)


def solution(mesh):
    return jax.shard_map(
        local,
        mesh=mesh,
        in_specs=(
            P(None, ("group", "tok"), "head"),
            P(None, "head"),
            P(None, "head"),
            P(None, "head"),
            P("head"),
        ),
        out_specs=P(None, ("group", "tok"), "head"),
        check_vma=False,
    )
```

```python
import functools

import jax
import jax.numpy as jnp
from jax import lax
from jax.experimental import pallas as pl
from jax.experimental.pallas import tpu as pltpu
from jax.sharding import PartitionSpec as P

HEAD_DIM = 112
VMEM_LIMIT = 20 * 1024 * 1024
ANYWHERE = pl.BlockSpec(memory_space=pl.ANY)
IN_VMEM = pl.BlockSpec(memory_space=pltpu.VMEM)
IN_SMEM = pl.BlockSpec(memory_space=pltpu.SMEM)


def call(body, outs, out_specs, in_specs, scratch, flops, aliases=None):
    return pl.pallas_call(
        body,
        out_shape=outs,
        in_specs=in_specs,
        out_specs=out_specs,
        scratch_shapes=scratch,
        input_output_aliases=aliases or {},
        compiler_params=pltpu.CompilerParams(vmem_limit_bytes=VMEM_LIMIT),
        cost_estimate=pl.CostEstimate(flops=flops // 64, bytes_accessed=1 << 10, transcendentals=0),
    )


def rounded_dot(matrix, block):
    return jnp.dot(matrix, block, preferred_element_type=jnp.float32)


def token_tiles(tokens):
    width = 256 if tokens % 256 == 0 else tokens
    return width, tokens // width


def load_blocks(place, found, whole, sems):
    mine, inner = place[0], place[1]
    rows = found[0].shape[0]

    def at(flip):
        return whole.at[pl.ds(pl.multiple_of((mine ^ flip) * rows, 16), rows), :]

    for flip, source in enumerate(found):
        if isinstance(source, tuple):
            for want, ref in ((1, source[0]), (0, source[1])):

                @pl.when(inner == want)
                def _(ref=ref, flip=flip):
                    pltpu.make_async_copy(ref, at(flip), sems.at[flip]).start()
        else:
            pltpu.make_async_copy(source, at(flip), sems.at[flip]).start()
    for flip in range(len(found)):
        pltpu.make_async_copy(at(flip), at(flip), sems.at[flip]).wait()


def partial_kernel(stream, place, own, near, b2i, b2o, wq, wk, wv, sums, query_sums, token, whole, sems):
    token[...] = jnp.zeros_like(token)
    rows, tokens = b2i.shape
    missing = pl.ds(pl.multiple_of((place[0] ^ 3) * rows, 16), rows)
    whole[missing, :] = jnp.zeros((rows, tokens), whole.dtype)
    load_blocks(place, [own.at[stream], near.at[stream], (b2i, b2o)], whole, sems)
    width, tiles = token_tiles(tokens)

    @pl.loop(0, tiles)
    def _(tile):
        columns = pl.ds(pl.multiple_of(tile * width, width), width)
        block = whole[:, columns]
        for k, matrix in enumerate((wk, wv)):
            sums[k, :, columns] = rounded_dot(matrix[...], block)
        query_sums[:, columns] = rounded_dot(wq[...], block)


def cut_kernel(count, place, *rest):
    matrices, (cut,) = rest[:-1], rest[-1:]
    rows = cut.shape[2]
    for owner in range(count):

        @pl.when((place[0] ^ 3) == owner)
        def _(owner=owner):
            for k, matrix in enumerate(matrices):
                cut[k] = matrix[:, owner * rows : (owner + 1) * rows]


def on_last(place, inner_ref, end_ref, body):
    for want, ref in ((1, inner_ref), (0, end_ref)):

        @pl.when(place[1] == want)
        def _(ref=ref):
            body(ref)


def state_kernel(place, inner_ref, end_ref, cut, sums, *rest):
    state = rest[-1]

    def body(block):
        key = (sums[0] + rounded_dot(cut[0], block[...])).astype(jnp.bfloat16)
        value = (sums[1] + rounded_dot(cut[1], block[...])).astype(jnp.bfloat16)
        key = jnp.maximum(key, 0)
        for start in range(0, key.shape[0], HEAD_DIM):
            rows = slice(start, start + HEAD_DIM)
            state[rows, :] = lax.dot_general(
                value[rows], key[rows], (((1,), (1,)), ((), ())), preferred_element_type=jnp.float32
            )

    on_last(place, inner_ref, end_ref, body)


def query_kernel(place, inner_ref, end_ref, cut, sums, tie, query):
    def body(block):
        row = (sums[...] + rounded_dot(cut[2], block[...])).astype(jnp.bfloat16)
        query[...] = jnp.maximum(row, 0)

    on_last(place, inner_ref, end_ref, body)


def read_kernel(stream, parts, query, gain, *rest):
    out, held, sems = rest[-3:]
    copies = []
    for start in range(0, query.shape[0], HEAD_DIM):
        rows = slice(start, start + HEAD_DIM)
        total = sum(part[rows, :].astype(jnp.float32) for part in rest[:parts])
        reading = rounded_dot(total.astype(jnp.bfloat16), query[rows, :])
        scale = lax.rsqrt(jnp.mean(reading * reading, axis=0, keepdims=True) + 1e-06)
        held[rows, :] = (reading * scale * gain[rows, :]).astype(jnp.bfloat16)
        copies.append(pltpu.make_async_copy(held.at[rows, :], out.at[stream, rows, :], sems.at[len(copies)]))
        copies[-1].start()
    for copy in copies:
        copy.wait()


def partner_swap(value, axis):
    return lax.ppermute(value, axis, [(i, i ^ 1) for i in range(lax.axis_size(axis))])


def middle_swap(value, axis, other):
    wide, count = lax.axis_size(other), lax.axis_size(axis)
    pairs = []
    for j in range(wide):
        for i in range(count):
            if i in (1, 2):
                pairs.append((j * count + i, j * count + 3 - i))
            else:
                pairs.append((j * count + i, (j ^ 1 if j ^ 1 < wide else j) * count + i))
    return lax.ppermute(value, (other, axis), pairs)


def from_others(value, axis):
    count = lax.axis_size(axis)
    sent = value.astype(jnp.bfloat16)
    got = []
    for step in range(count - 1, 0, -1):
        pairs = [(i, (i + step) % count) for i in range(count)]
        if count & (count - 1) == 0:
            pairs = [(i, i ^ step) for i in range(count)]
        got.append(lax.ppermute(sent, axis, pairs))
    return got


def entering(value, axis):
    count, mine = lax.axis_size(axis), lax.axis_index(axis)

    def earlier(value, reach):
        sent = lax.ppermute(value.astype(jnp.bfloat16), axis, [(i, (i + reach) % count) for i in range(count)])
        return jnp.where(mine >= reach, sent.astype(jnp.float32), 0.0)

    total, reach = earlier(value, 1), 1
    while reach < count - 1:
        total, reach = total + earlier(total, reach), 2 * reach
    return total


def local(streams, w_query, w_key, w_value, gain):
    count, mine = lax.axis_size("head"), lax.axis_index("head")
    rows, tokens = streams.shape[2], streams.shape[1]
    width = w_query.shape[1]
    depth = rows * count
    columns = jnp.swapaxes(streams, 1, 2)
    matrices = (w_query.T, w_key.T, w_value.T)
    gain_column = gain.reshape(width, 1)
    inner = (mine == 1) | (mine == 2)
    place = jnp.stack([mine.astype(jnp.int32), inner.astype(jnp.int32)])

    one = 2 * width * depth * tokens
    cut = call(
        functools.partial(cut_kernel, count), jax.ShapeDtypeStruct((3, width, rows), jnp.bfloat16), IN_VMEM,
        [IN_SMEM] + [IN_VMEM] * 3, [], one // 4,
    )(place, matrices[1], matrices[2], matrices[0])
    across, far, across_end, far_end = [], [], [], []
    near = partner_swap(columns, "head")
    for stream in range(2):
        across.append(middle_swap(columns[stream], "head", "group"))
    for stream in range(2):
        far.append(middle_swap(near[stream], "head", "group"))
        ready, *_ = lax.optimization_barrier((across[stream], *([cut] if stream else [])))
        across_end.append(partner_swap(ready, "head"))
    whole = pltpu.VMEM((depth, tokens), jnp.bfloat16)
    sems = pltpu.SemaphoreType.DMA((4,))
    query_type = jax.ShapeDtypeStruct((width, tokens), jnp.bfloat16)
    state_type = jax.ShapeDtypeStruct((width, HEAD_DIM), jnp.float32)
    out_type = jax.ShapeDtypeStruct((2, width, tokens), jnp.bfloat16)

    read_scratch = [pltpu.VMEM((width, tokens), jnp.bfloat16), pltpu.SemaphoreType.DMA((width // HEAD_DIM,))]
    partial_types = (
        jax.ShapeDtypeStruct((2, width, tokens), jnp.float32),
        jax.ShapeDtypeStruct((width, tokens), jnp.float32),
        jax.ShapeDtypeStruct((8, 128), jnp.float32),
    )
    sums, query_sums, done = [], [], []
    for stream in range(2):
        ready, *_ = lax.optimization_barrier((far[stream], across_end[stream], *done))
        far_end.append(partner_swap(ready, "head"))
        key_value, query, token = call(
            functools.partial(partial_kernel, stream), partial_types, (IN_VMEM,) * 3,
            [IN_SMEM] + [ANYWHERE] * 4 + [IN_VMEM] * 3, [whole, sems], 3 * one,
        )(place, columns, near, far[stream], across_end[stream], *matrices)
        sums.append(key_value)
        query_sums.append(query)
        done.append(token)
    queries, query, clean = [], None, None
    for stream in range(2):
        ties = (done[1],) if stream == 0 else (clean, query)
        state = call(
            state_kernel, state_type, IN_VMEM,
            [IN_SMEM] + [IN_VMEM] * 4 + [ANYWHERE] * len(ties), [], one // 2,
        )(place, across[stream], far_end[stream], cut, sums[stream], *ties)
        query = call(
            query_kernel, query_type, IN_VMEM, [IN_SMEM] + [IN_VMEM] * 4 + [ANYWHERE], [], one // 4,
        )(place, across[stream], far_end[stream], cut, query_sums[stream], state)
        queries.append(query)
        if stream == 0:
            query, *got = lax.optimization_barrier((query, *from_others(state, "tok")))
            clean = state + sum(part.astype(jnp.float32) for part in got)
            prefix = entering(clean, "group")
    out = None
    for stream, parts in enumerate(([clean], [state, *from_others(state, "tok")])):
        kept = [] if out is None else [out]
        out = call(
            functools.partial(read_kernel, stream, len(parts) + 1), out_type, ANYWHERE,
            [IN_VMEM] * (3 + len(parts)) + [ANYWHERE] * len(kept),
            read_scratch, one // 20, {3 + len(parts): 0} if kept else None,
        )(queries[stream], gain_column, prefix, *parts, *kept)
    return jnp.swapaxes(out, 1, 2)


def solution(mesh):
    return jax.shard_map(
        local,
        mesh=mesh,
        in_specs=(
            P(None, ("group", "tok"), "head"),
            P(None, "head"),
            P(None, "head"),
            P(None, "head"),
            P("head"),
        ),
        out_specs=P(None, ("group", "tok"), "head"),
        check_vma=False,
    )
```

```python
import functools

import jax
import jax.numpy as jnp
from jax import lax
from jax.experimental import pallas as pl
from jax.experimental.pallas import tpu as pltpu
from jax.sharding import PartitionSpec as P

HEAD_DIM = 112
VMEM_LIMIT = 20 * 1024 * 1024
ANYWHERE = pl.BlockSpec(memory_space=pl.ANY)
IN_VMEM = pl.BlockSpec(memory_space=pltpu.VMEM)
IN_SMEM = pl.BlockSpec(memory_space=pltpu.SMEM)


def call(body, outs, out_specs, in_specs, scratch, flops, aliases=None):
    return pl.pallas_call(
        body,
        out_shape=outs,
        in_specs=in_specs,
        out_specs=out_specs,
        scratch_shapes=scratch,
        input_output_aliases=aliases or {},
        compiler_params=pltpu.CompilerParams(vmem_limit_bytes=VMEM_LIMIT),
        cost_estimate=pl.CostEstimate(flops=flops // 64, bytes_accessed=1 << 10, transcendentals=0),
    )


def rounded_dot(matrix, block):
    return jnp.dot(matrix, block, preferred_element_type=jnp.float32)


def token_tiles(tokens):
    width = 256 if tokens % 256 == 0 else tokens
    return width, tokens // width


def load_blocks(place, found, whole, sems):
    mine, inner = place[0], place[1]
    rows = found[0].shape[0]

    def at(flip):
        return whole.at[pl.ds(pl.multiple_of((mine ^ flip) * rows, 16), rows), :]

    for flip, source in enumerate(found):
        if isinstance(source, tuple):
            for want, ref in ((1, source[0]), (0, source[1])):

                @pl.when(inner == want)
                def _(ref=ref, flip=flip):
                    pltpu.make_async_copy(ref, at(flip), sems.at[flip]).start()
        else:
            pltpu.make_async_copy(source, at(flip), sems.at[flip]).start()
    for flip in range(len(found)):
        pltpu.make_async_copy(at(flip), at(flip), sems.at[flip]).wait()


def partial_kernel(stream, place, own, near, b2i, b2o, wq, wk, wv, tie, sums, whole, sems):
    rows, tokens = b2i.shape
    missing = pl.ds(pl.multiple_of((place[0] ^ 3) * rows, 16), rows)
    whole[missing, :] = jnp.zeros((rows, tokens), whole.dtype)
    load_blocks(place, [own.at[stream], near.at[stream], (b2i, b2o)], whole, sems)
    width, tiles = token_tiles(tokens)

    @pl.loop(0, tiles)
    def _(tile):
        columns = pl.ds(pl.multiple_of(tile * width, width), width)
        block = whole[:, columns]
        for k, matrix in enumerate((wk, wv, wq)):
            sums[k, :, columns] = rounded_dot(matrix[...], block)


def cut_kernel(count, place, *rest):
    matrices, (cut,) = rest[:-1], rest[-1:]
    rows = cut.shape[2]
    for owner in range(count):

        @pl.when((place[0] ^ 3) == owner)
        def _(owner=owner):
            for k, matrix in enumerate(matrices):
                cut[k] = matrix[:, owner * rows : (owner + 1) * rows]


def on_last(place, inner_ref, end_ref, body):
    for want, ref in ((1, inner_ref), (0, end_ref)):

        @pl.when(place[1] == want)
        def _(ref=ref):
            body(ref)


def state_kernel(place, inner_ref, end_ref, cut, sums, *rest):
    state = rest[-1]

    def body(block):
        key = (sums[0] + rounded_dot(cut[0], block[...])).astype(jnp.bfloat16)
        value = (sums[1] + rounded_dot(cut[1], block[...])).astype(jnp.bfloat16)
        key = jnp.maximum(key, 0)
        for start in range(0, key.shape[0], HEAD_DIM):
            rows = slice(start, start + HEAD_DIM)
            state[rows, :] = lax.dot_general(
                value[rows], key[rows], (((1,), (1,)), ((), ())), preferred_element_type=jnp.float32
            )

    on_last(place, inner_ref, end_ref, body)


def query_kernel(place, inner_ref, end_ref, cut, sums, tie, query):
    def body(block):
        row = (sums[2] + rounded_dot(cut[2], block[...])).astype(jnp.bfloat16)
        query[...] = jnp.maximum(row, 0)

    on_last(place, inner_ref, end_ref, body)


def read_kernel(stream, parts, query, gain, *rest):
    out, held, sems = rest[-3:]
    copies = []
    for start in range(0, query.shape[0], HEAD_DIM):
        rows = slice(start, start + HEAD_DIM)
        total = sum(part[rows, :].astype(jnp.float32) for part in rest[:parts])
        reading = rounded_dot(total.astype(jnp.bfloat16), query[rows, :])
        scale = lax.rsqrt(jnp.mean(reading * reading, axis=0, keepdims=True) + 1e-06)
        held[rows, :] = (reading * scale * gain[rows, :]).astype(jnp.bfloat16)
        copies.append(pltpu.make_async_copy(held.at[rows, :], out.at[stream, rows, :], sems.at[len(copies)]))
        copies[-1].start()
    for copy in copies:
        copy.wait()


def partner_swap(value, axis):
    return lax.ppermute(value, axis, [(i, i ^ 1) for i in range(lax.axis_size(axis))])


def middle_swap(value, axis, other):
    wide, count = lax.axis_size(other), lax.axis_size(axis)
    pairs = []
    for j in range(wide):
        for i in range(count):
            if i in (1, 2):
                pairs.append((j * count + i, j * count + 3 - i))
            else:
                pairs.append((j * count + i, (j ^ 1 if j ^ 1 < wide else j) * count + i))
    return lax.ppermute(value, (other, axis), pairs)


def from_others(value, axis):
    count = lax.axis_size(axis)
    sent = value.astype(jnp.bfloat16)
    got = []
    for step in range(count - 1, 0, -1):
        pairs = [(i, (i + step) % count) for i in range(count)]
        if count & (count - 1) == 0:
            pairs = [(i, i ^ step) for i in range(count)]
        got.append(lax.ppermute(sent, axis, pairs))
    return got


def entering(value, axis):
    count, mine = lax.axis_size(axis), lax.axis_index(axis)

    def earlier(value, reach):
        sent = jnp.where(mine + reach < count, value, 0.0)
        return lax.ppermute(sent, axis, [(i, (i + reach) % count) for i in range(count)])

    total, reach = earlier(value, 1), 1
    while reach < count - 1:
        total, reach = total + earlier(total, reach), 2 * reach
    return total


def local(streams, w_query, w_key, w_value, gain):
    count, mine = lax.axis_size("head"), lax.axis_index("head")
    rows, tokens = streams.shape[2], streams.shape[1]
    width = w_query.shape[1]
    depth = rows * count
    columns = jnp.swapaxes(streams, 1, 2)
    matrices = (w_query.T, w_key.T, w_value.T)
    gain_column = gain.reshape(width, 1)
    inner = (mine == 1) | (mine == 2)
    place = jnp.stack([mine.astype(jnp.int32), inner.astype(jnp.int32)])

    one = 2 * width * depth * tokens
    cut = call(
        functools.partial(cut_kernel, count), jax.ShapeDtypeStruct((3, width, rows), jnp.bfloat16), IN_VMEM,
        [IN_SMEM] + [IN_VMEM] * 3, [], one // 4,
    )(place, matrices[1], matrices[2], matrices[0])
    across, far, across_end, far_end = [], [], [], []
    near = partner_swap(columns, "head")
    for stream in range(2):
        across.append(middle_swap(columns[stream], "head", "group"))
    for stream in range(2):
        far.append(middle_swap(near[stream], "head", "group"))
        ready, *_ = lax.optimization_barrier((across[stream], *([cut] if stream else [])))
        across_end.append(partner_swap(ready, "head"))
    whole = pltpu.VMEM((depth, tokens), jnp.bfloat16)
    sems = pltpu.SemaphoreType.DMA((4,))
    query_type = jax.ShapeDtypeStruct((width, tokens), jnp.bfloat16)
    state_type = jax.ShapeDtypeStruct((width, HEAD_DIM), jnp.float32)
    out_type = jax.ShapeDtypeStruct((2, width, tokens), jnp.bfloat16)

    read_scratch = [pltpu.VMEM((width, tokens), jnp.bfloat16), pltpu.SemaphoreType.DMA((width // HEAD_DIM,))]
    sums = []
    for stream in range(2):
        ready, *_ = lax.optimization_barrier((far[stream], across_end[stream], *sums))
        far_end.append(partner_swap(ready, "head"))
        sums.append(call(
            functools.partial(partial_kernel, stream), jax.ShapeDtypeStruct((3, width, tokens), jnp.float32), IN_VMEM,
            [IN_SMEM] + [ANYWHERE] * 4 + [IN_VMEM] * 3 + [ANYWHERE], [whole, sems], 3 * one,
        )(place, columns, near, far[stream], across_end[stream], *matrices, cut))
    prefix = parts = query = out = None
    for stream in range(2):
        ties = (sums[1],) if stream == 0 else (parts[0], query)
        state = call(
            state_kernel, state_type, IN_VMEM,
            [IN_SMEM] + [IN_VMEM] * 4 + [ANYWHERE] * len(ties), [], one // 2,
        )(place, across[stream], far_end[stream], cut, sums[stream], *ties)
        query = call(
            query_kernel, query_type, IN_VMEM, [IN_SMEM] + [IN_VMEM] * 4 + [ANYWHERE], [], one // 4,
        )(place, across[stream], far_end[stream], cut, sums[stream], state)
        parts = [state, *from_others(state, "tok")]
        if stream == 0:
            query, *parts = lax.optimization_barrier((query, *parts))
            parts = [sum(part.astype(jnp.float32) for part in parts)]
            prefix = entering(parts[0], "group")
        kept = [] if out is None else [out]
        out = call(
            functools.partial(read_kernel, stream, len(parts) + 1), out_type, ANYWHERE,
            [IN_VMEM] * (3 + len(parts)) + [ANYWHERE] * len(kept),
            read_scratch, one // 20, {3 + len(parts): 0} if kept else None,
        )(query, gain_column, prefix, *parts, *kept)
    return jnp.swapaxes(out, 1, 2)


def solution(mesh):
    return jax.shard_map(
        local,
        mesh=mesh,
        in_specs=(
            P(None, ("group", "tok"), "head"),
            P(None, "head"),
            P(None, "head"),
            P(None, "head"),
            P("head"),
        ),
        out_specs=P(None, ("group", "tok"), "head"),
        check_vma=False,
    )
```

```python
import functools

import jax
import jax.numpy as jnp
from jax import lax
from jax.experimental import pallas as pl
from jax.experimental.pallas import tpu as pltpu
from jax.sharding import PartitionSpec as P

HEAD_DIM = 112
VMEM_LIMIT = 20 * 1024 * 1024
ANYWHERE = pl.BlockSpec(memory_space=pl.ANY)
IN_VMEM = pl.BlockSpec(memory_space=pltpu.VMEM)
IN_SMEM = pl.BlockSpec(memory_space=pltpu.SMEM)


def call(body, outs, out_specs, in_specs, scratch, flops, aliases=None):
    return pl.pallas_call(
        body,
        out_shape=outs,
        in_specs=in_specs,
        out_specs=out_specs,
        scratch_shapes=scratch,
        input_output_aliases=aliases or {},
        compiler_params=pltpu.CompilerParams(vmem_limit_bytes=VMEM_LIMIT),
        cost_estimate=pl.CostEstimate(flops=flops // 64, bytes_accessed=1 << 10, transcendentals=0),
    )


def rounded_dot(matrix, block):
    return jnp.dot(matrix, block, preferred_element_type=jnp.float32)


def token_tiles(tokens):
    width = 256 if tokens % 256 == 0 else tokens
    return width, tokens // width


def load_blocks(place, found, whole, sems):
    mine, inner = place[0], place[1]
    rows = found[0].shape[0]

    def at(flip):
        return whole.at[pl.ds(pl.multiple_of((mine ^ flip) * rows, 16), rows), :]

    for flip, source in enumerate(found):
        if isinstance(source, tuple):
            for want, ref in ((1, source[0]), (0, source[1])):

                @pl.when(inner == want)
                def _(ref=ref, flip=flip):
                    pltpu.make_async_copy(ref, at(flip), sems.at[flip]).start()
        else:
            pltpu.make_async_copy(source, at(flip), sems.at[flip]).start()
    for flip in range(len(found)):
        pltpu.make_async_copy(at(flip), at(flip), sems.at[flip]).wait()


def partial_kernel(stream, place, own, near, b2i, b2o, wq, wk, wv, tie, sums, whole, sems):
    rows, tokens = b2i.shape
    missing = pl.ds(pl.multiple_of((place[0] ^ 3) * rows, 16), rows)
    whole[missing, :] = jnp.zeros((rows, tokens), whole.dtype)
    load_blocks(place, [own.at[stream], near.at[stream], (b2i, b2o)], whole, sems)
    width, tiles = token_tiles(tokens)

    @pl.loop(0, tiles)
    def _(tile):
        columns = pl.ds(pl.multiple_of(tile * width, width), width)
        block = whole[:, columns]
        for k, matrix in enumerate((wk, wv, wq)):
            sums[k, :, columns] = rounded_dot(matrix[...], block)


def cut_kernel(count, place, *rest):
    matrices, (cut,) = rest[:-1], rest[-1:]
    rows = cut.shape[2]
    for owner in range(count):

        @pl.when((place[0] ^ 3) == owner)
        def _(owner=owner):
            for k, matrix in enumerate(matrices):
                cut[k] = matrix[:, owner * rows : (owner + 1) * rows]


def on_last(place, inner_ref, end_ref, body):
    for want, ref in ((1, inner_ref), (0, end_ref)):

        @pl.when(place[1] == want)
        def _(ref=ref):
            body(ref)


def state_kernel(place, inner_ref, end_ref, cut, sums, *rest):
    state = rest[-1]

    def body(block):
        key = (sums[0] + rounded_dot(cut[0], block[...])).astype(jnp.bfloat16)
        value = (sums[1] + rounded_dot(cut[1], block[...])).astype(jnp.bfloat16)
        key = jnp.maximum(key, 0)
        for start in range(0, key.shape[0], HEAD_DIM):
            rows = slice(start, start + HEAD_DIM)
            state[rows, :] = lax.dot_general(
                value[rows], key[rows], (((1,), (1,)), ((), ())), preferred_element_type=jnp.float32
            )

    on_last(place, inner_ref, end_ref, body)


def query_kernel(place, inner_ref, end_ref, cut, sums, tie, query):
    def body(block):
        row = (sums[2] + rounded_dot(cut[2], block[...])).astype(jnp.bfloat16)
        query[...] = jnp.maximum(row, 0)

    on_last(place, inner_ref, end_ref, body)


def read_kernel(stream, parts, place, query, gain, prefix, *rest):
    out, held, sems = rest[-3:]
    copies = []
    for start in range(0, query.shape[0], HEAD_DIM):
        rows = slice(start, start + HEAD_DIM)
        total = sum(part[rows, :].astype(jnp.float32) for part in rest[:parts])
        total += jnp.where(place[2] == 1, prefix[rows, :], 0.0)
        reading = rounded_dot(total.astype(jnp.bfloat16), query[rows, :])
        scale = lax.rsqrt(jnp.mean(reading * reading, axis=0, keepdims=True) + 1e-06)
        held[rows, :] = (reading * scale * gain[rows, :]).astype(jnp.bfloat16)
        copies.append(pltpu.make_async_copy(held.at[rows, :], out.at[stream, rows, :], sems.at[len(copies)]))
        copies[-1].start()
    for copy in copies:
        copy.wait()


def partner_swap(value, axis):
    return lax.ppermute(value, axis, [(i, i ^ 1) for i in range(lax.axis_size(axis))])


def middle_swap(value, axis, other):
    wide, count = lax.axis_size(other), lax.axis_size(axis)
    pairs = []
    for j in range(wide):
        for i in range(count):
            if i in (1, 2):
                pairs.append((j * count + i, j * count + 3 - i))
            else:
                pairs.append((j * count + i, (j ^ 1 if j ^ 1 < wide else j) * count + i))
    return lax.ppermute(value, (other, axis), pairs)


def from_others(value, axis):
    count = lax.axis_size(axis)
    sent = value.astype(jnp.bfloat16)
    got = []
    for step in range(count - 1, 0, -1):
        pairs = [(i, (i + step) % count) for i in range(count)]
        if count & (count - 1) == 0:
            pairs = [(i, i ^ step) for i in range(count)]
        got.append(lax.ppermute(sent, axis, pairs))
    return got


def entering(value, axis):
    count, mine = lax.axis_size(axis), lax.axis_index(axis)

    def earlier(value, reach):
        return lax.ppermute(value, axis, [(i, (i + reach) % count) for i in range(count)])

    total, reach = earlier(value, 1), 1
    while reach < count - 1:
        total = jnp.where(mine >= 1, total, 0.0)
        total, reach = total + jnp.where(mine >= reach, earlier(total, reach), 0.0), 2 * reach
    return total


def local(streams, w_query, w_key, w_value, gain):
    count, mine = lax.axis_size("head"), lax.axis_index("head")
    rows, tokens = streams.shape[2], streams.shape[1]
    width = w_query.shape[1]
    depth = rows * count
    columns = jnp.swapaxes(streams, 1, 2)
    matrices = (w_query.T, w_key.T, w_value.T)
    gain_column = gain.reshape(width, 1)
    inner = (mine == 1) | (mine == 2)
    later = lax.axis_index("group") > 0
    place = jnp.stack([value.astype(jnp.int32) for value in (mine, inner, later)])

    one = 2 * width * depth * tokens
    cut = call(
        functools.partial(cut_kernel, count), jax.ShapeDtypeStruct((3, width, rows), jnp.bfloat16), IN_VMEM,
        [IN_SMEM] + [IN_VMEM] * 3, [], one // 4,
    )(place, matrices[1], matrices[2], matrices[0])
    across, far, across_end, far_end = [], [], [], []
    near = partner_swap(columns, "head")
    for stream in range(2):
        across.append(middle_swap(columns[stream], "head", "group"))
    for stream in range(2):
        far.append(middle_swap(near[stream], "head", "group"))
        ready, *_ = lax.optimization_barrier((across[stream], *([cut] if stream else [])))
        across_end.append(partner_swap(ready, "head"))
    whole = pltpu.VMEM((depth, tokens), jnp.bfloat16)
    sems = pltpu.SemaphoreType.DMA((4,))
    query_type = jax.ShapeDtypeStruct((width, tokens), jnp.bfloat16)
    state_type = jax.ShapeDtypeStruct((width, HEAD_DIM), jnp.float32)
    out_type = jax.ShapeDtypeStruct((2, width, tokens), jnp.bfloat16)

    read_scratch = [pltpu.VMEM((width, tokens), jnp.bfloat16), pltpu.SemaphoreType.DMA((width // HEAD_DIM,))]
    sums = []
    for stream in range(2):
        ready, *_ = lax.optimization_barrier((far[stream], across_end[stream], *sums))
        far_end.append(partner_swap(ready, "head"))
        sums.append(call(
            functools.partial(partial_kernel, stream), jax.ShapeDtypeStruct((3, width, tokens), jnp.float32), IN_VMEM,
            [IN_SMEM] + [ANYWHERE] * 4 + [IN_VMEM] * 3 + [ANYWHERE], [whole, sems], 3 * one,
        )(place, columns, near, far[stream], across_end[stream], *matrices, cut))
    prefix = parts = query = out = None
    for stream in range(2):
        ties = (sums[1],) if stream == 0 else (parts[0], query)
        state = call(
            state_kernel, state_type, IN_VMEM,
            [IN_SMEM] + [IN_VMEM] * 4 + [ANYWHERE] * len(ties), [], one // 2,
        )(place, across[stream], far_end[stream], cut, sums[stream], *ties)
        query = call(
            query_kernel, query_type, IN_VMEM, [IN_SMEM] + [IN_VMEM] * 4 + [ANYWHERE], [], one // 4,
        )(place, across[stream], far_end[stream], cut, sums[stream], state)
        parts = [state, *from_others(state, "tok")]
        if stream == 0:
            query, *parts = lax.optimization_barrier((query, *parts))
            parts = [sum(part.astype(jnp.float32) for part in parts)]
            prefix = entering(parts[0], "group")
        kept = [] if out is None else [out]
        out = call(
            functools.partial(read_kernel, stream, len(parts)), out_type, ANYWHERE,
            [IN_SMEM] + [IN_VMEM] * (3 + len(parts)) + [ANYWHERE] * len(kept),
            read_scratch, one // 20, {4 + len(parts): 0} if kept else None,
        )(place, query, gain_column, prefix, *parts, *kept)
    return jnp.swapaxes(out, 1, 2)


def solution(mesh):
    return jax.shard_map(
        local,
        mesh=mesh,
        in_specs=(
            P(None, ("group", "tok"), "head"),
            P(None, "head"),
            P(None, "head"),
            P(None, "head"),
            P("head"),
        ),
        out_specs=P(None, ("group", "tok"), "head"),
        check_vma=False,
    )
```

```python
import functools

import jax
import jax.numpy as jnp
from jax import lax
from jax.experimental import pallas as pl
from jax.experimental.pallas import tpu as pltpu
from jax.sharding import PartitionSpec as P

HEAD_DIM = 112
VMEM_LIMIT = 20 * 1024 * 1024
ANYWHERE = pl.BlockSpec(memory_space=pl.ANY)
IN_VMEM = pl.BlockSpec(memory_space=pltpu.VMEM)


def call(body, outs, out_specs, in_specs, scratch, flops, aliases=None):
    return pl.pallas_call(
        body,
        out_shape=outs,
        in_specs=in_specs,
        out_specs=out_specs,
        scratch_shapes=scratch,
        input_output_aliases=aliases or {},
        compiler_params=pltpu.CompilerParams(vmem_limit_bytes=VMEM_LIMIT),
        cost_estimate=pl.CostEstimate(flops=flops // 64, bytes_accessed=1 << 10, transcendentals=0),
    )


def rounded_dot(matrix, block):
    return jnp.dot(matrix, block, preferred_element_type=jnp.float32)


def token_tiles(tokens):
    width = 256 if tokens % 256 == 0 else tokens
    return width, tokens // width


def is_inner(position):
    return (position == 1) | (position == 2)


def load_blocks(found, whole, sems):
    mine = lax.axis_index("head")
    rows = found[0].shape[0]

    def at(flip):
        return whole.at[pl.ds(pl.multiple_of((mine ^ flip) * rows, 16), rows), :]

    for flip, source in enumerate(found):
        if isinstance(source, tuple):
            for want, ref in ((True, source[0]), (False, source[1])):

                @pl.when(is_inner(mine) == want)
                def _(ref=ref, flip=flip):
                    pltpu.make_async_copy(ref, at(flip), sems.at[flip]).start()
        else:
            pltpu.make_async_copy(source, at(flip), sems.at[flip]).start()
    for flip in range(len(found)):
        pltpu.make_async_copy(at(flip), at(flip), sems.at[flip]).wait()


def partial_kernel(stream, own, near, b2i, b2o, wq, wk, wv, tie, sums, whole, sems):
    rows, tokens = b2i.shape
    missing = pl.ds(pl.multiple_of((lax.axis_index("head") ^ 3) * rows, 16), rows)
    whole[missing, :] = jnp.zeros((rows, tokens), whole.dtype)
    load_blocks([own.at[stream], near.at[stream], (b2i, b2o)], whole, sems)
    width, tiles = token_tiles(tokens)

    @pl.loop(0, tiles)
    def _(tile):
        columns = pl.ds(pl.multiple_of(tile * width, width), width)
        block = whole[:, columns]
        for k, matrix in enumerate((wk, wv, wq)):
            sums[k, :, columns] = rounded_dot(matrix[...], block)


def cut_kernel(count, *rest):
    matrices, (cut,) = rest[:-1], rest[-1:]
    rows = cut.shape[2]
    for owner in range(count):

        @pl.when((lax.axis_index("head") ^ 3) == owner)
        def _(owner=owner):
            for k, matrix in enumerate(matrices):
                cut[k] = matrix[:, owner * rows : (owner + 1) * rows]


def on_last(inner_ref, end_ref, body):
    for want, ref in ((True, inner_ref), (False, end_ref)):

        @pl.when(is_inner(lax.axis_index("head")) == want)
        def _(ref=ref):
            body(ref)


def state_kernel(inner_ref, end_ref, cut, sums, *rest):
    state = rest[-1]

    def body(block):
        key = (sums[0] + rounded_dot(cut[0], block[...])).astype(jnp.bfloat16)
        value = (sums[1] + rounded_dot(cut[1], block[...])).astype(jnp.bfloat16)
        key = jnp.maximum(key, 0)
        for start in range(0, key.shape[0], HEAD_DIM):
            rows = slice(start, start + HEAD_DIM)
            state[rows, :] = lax.dot_general(
                value[rows], key[rows], (((1,), (1,)), ((), ())), preferred_element_type=jnp.float32
            )

    on_last(inner_ref, end_ref, body)


def query_kernel(inner_ref, end_ref, cut, sums, tie, query):
    def body(block):
        row = (sums[2] + rounded_dot(cut[2], block[...])).astype(jnp.bfloat16)
        query[...] = jnp.maximum(row, 0)

    on_last(inner_ref, end_ref, body)


def read_kernel(stream, parts, query, gain, *rest):
    out, held, sems = rest[-3:]
    copies = []
    for start in range(0, query.shape[0], HEAD_DIM):
        rows = slice(start, start + HEAD_DIM)
        total = sum(part[rows, :].astype(jnp.float32) for part in rest[:parts])
        reading = rounded_dot(total.astype(jnp.bfloat16), query[rows, :])
        scale = lax.rsqrt(jnp.mean(reading * reading, axis=0, keepdims=True) + 1e-06)
        held[rows, :] = (reading * scale * gain[rows, :]).astype(jnp.bfloat16)
        copies.append(pltpu.make_async_copy(held.at[rows, :], out.at[stream, rows, :], sems.at[len(copies)]))
        copies[-1].start()
    for copy in copies:
        copy.wait()


def partner_swap(value, axis):
    return lax.ppermute(value, axis, [(i, i ^ 1) for i in range(lax.axis_size(axis))])


def middle_swap(value, axis, other):
    wide, count = lax.axis_size(other), lax.axis_size(axis)
    pairs = []
    for j in range(wide):
        for i in range(count):
            if i in (1, 2):
                pairs.append((j * count + i, j * count + 3 - i))
            else:
                pairs.append((j * count + i, (j ^ 1 if j ^ 1 < wide else j) * count + i))
    return lax.ppermute(value, (other, axis), pairs)


def from_others(value, axis):
    count = lax.axis_size(axis)
    sent = value.astype(jnp.bfloat16)
    got = []
    for step in range(count - 1, 0, -1):
        pairs = [(i, (i + step) % count) for i in range(count)]
        if count & (count - 1) == 0:
            pairs = [(i, i ^ step) for i in range(count)]
        got.append(lax.ppermute(sent, axis, pairs))
    return got


def entering(value, axis):
    count = lax.axis_size(axis)
    total = lax.ppermute(value, axis, [(i, i + 1) for i in range(count - 1)])
    reach = 1
    while reach < count - 1:
        total = total + lax.ppermute(total, axis, [(i, i + reach) for i in range(count - reach)])
        reach *= 2
    return total


def local(streams, w_query, w_key, w_value, gain):
    count = lax.axis_size("head")
    rows, tokens = streams.shape[2], streams.shape[1]
    width = w_query.shape[1]
    depth = rows * count
    columns = jnp.swapaxes(streams, 1, 2)
    matrices = (w_query.T, w_key.T, w_value.T)
    gain_column = gain.reshape(width, 1)

    one = 2 * width * depth * tokens
    cut = call(
        functools.partial(cut_kernel, count), jax.ShapeDtypeStruct((3, width, rows), jnp.bfloat16), IN_VMEM,
        [IN_VMEM] * 3, [], one // 4,
    )(matrices[1], matrices[2], matrices[0])
    across, far, across_end, far_end = [], [], [], []
    near = partner_swap(columns, "head")
    for stream in range(2):
        across.append(middle_swap(columns[stream], "head", "group"))
    for stream in range(2):
        far.append(middle_swap(near[stream], "head", "group"))
        ready, *_ = lax.optimization_barrier((across[stream], *([cut] if stream else [])))
        across_end.append(partner_swap(ready, "head"))
    whole = pltpu.VMEM((depth, tokens), jnp.bfloat16)
    sems = pltpu.SemaphoreType.DMA((4,))
    query_type = jax.ShapeDtypeStruct((width, tokens), jnp.bfloat16)
    state_type = jax.ShapeDtypeStruct((width, HEAD_DIM), jnp.float32)
    out_type = jax.ShapeDtypeStruct((2, width, tokens), jnp.bfloat16)

    read_scratch = [pltpu.VMEM((width, tokens), jnp.bfloat16), pltpu.SemaphoreType.DMA((width // HEAD_DIM,))]
    sums = []
    for stream in range(2):
        ready, *_ = lax.optimization_barrier((far[stream], across_end[stream], *sums))
        far_end.append(partner_swap(ready, "head"))
        sums.append(call(
            functools.partial(partial_kernel, stream), jax.ShapeDtypeStruct((3, width, tokens), jnp.float32), IN_VMEM,
            [ANYWHERE] * 4 + [IN_VMEM] * 3 + [ANYWHERE], [whole, sems], 3 * one,
        )(columns, near, far[stream], across_end[stream], *matrices, cut))
    prefix = parts = query = out = None
    for stream in range(2):
        ties = (sums[1],) if stream == 0 else (parts[0], query)
        state = call(
            state_kernel, state_type, IN_VMEM,
            [IN_VMEM] * 4 + [ANYWHERE] * len(ties), [], one // 2,
        )(across[stream], far_end[stream], cut, sums[stream], *ties)
        query = call(
            query_kernel, query_type, IN_VMEM, [IN_VMEM] * 4 + [ANYWHERE], [], one // 4,
        )(across[stream], far_end[stream], cut, sums[stream], state)
        parts = [state, *from_others(state, "tok")]
        if stream == 0:
            query, *parts = lax.optimization_barrier((query, *parts))
            parts = [sum(part.astype(jnp.float32) for part in parts)]
            prefix = entering(parts[0], "group")
        kept = [] if out is None else [out]
        out = call(
            functools.partial(read_kernel, stream, len(parts) + 1), out_type, ANYWHERE,
            [IN_VMEM] * (3 + len(parts)) + [ANYWHERE] * len(kept),
            read_scratch, one // 20, {3 + len(parts): 0} if kept else None,
        )(query, gain_column, prefix, *parts, *kept)
    return jnp.swapaxes(out, 1, 2)


def solution(mesh):
    return jax.shard_map(
        local,
        mesh=mesh,
        in_specs=(
            P(None, ("group", "tok"), "head"),
            P(None, "head"),
            P(None, "head"),
            P(None, "head"),
            P("head"),
        ),
        out_specs=P(None, ("group", "tok"), "head"),
        check_vma=False,
    )
```

```python
import functools

import jax
import jax.numpy as jnp
from jax import lax
from jax.experimental import pallas as pl
from jax.experimental.pallas import tpu as pltpu
from jax.sharding import PartitionSpec as P

HEAD_DIM = 112
VMEM_LIMIT = 20 * 1024 * 1024
ANYWHERE = pl.BlockSpec(memory_space=pl.ANY)
IN_VMEM = pl.BlockSpec(memory_space=pltpu.VMEM)


def call(body, outs, out_specs, in_specs, scratch, flops, aliases=None):
    return pl.pallas_call(
        body,
        out_shape=outs,
        in_specs=in_specs,
        out_specs=out_specs,
        scratch_shapes=scratch,
        input_output_aliases=aliases or {},
        compiler_params=pltpu.CompilerParams(vmem_limit_bytes=VMEM_LIMIT),
        cost_estimate=pl.CostEstimate(flops=flops // 64, bytes_accessed=1 << 10, transcendentals=0),
    )


def rounded_dot(matrix, block):
    return jnp.dot(matrix, block, preferred_element_type=jnp.float32)


def token_tiles(tokens):
    width = 256 if tokens % 256 == 0 else tokens
    return width, tokens // width


def is_inner(position):
    return (position == 1) | (position == 2)


def load_blocks(found, whole, sems):
    mine = lax.axis_index("head")
    rows = found[0].shape[0]

    def at(flip):
        return whole.at[pl.ds(pl.multiple_of((mine ^ flip) * rows, 16), rows), :]

    for flip, source in enumerate(found):
        if isinstance(source, tuple):
            for want, ref in ((True, source[0]), (False, source[1])):

                @pl.when(is_inner(mine) == want)
                def _(ref=ref, flip=flip):
                    pltpu.make_async_copy(ref, at(flip), sems.at[flip]).start()
        else:
            pltpu.make_async_copy(source, at(flip), sems.at[flip]).start()
    for flip in range(len(found)):
        pltpu.make_async_copy(at(flip), at(flip), sems.at[flip]).wait()


def partial_kernel(stream, own, near, b2i, b2o, wq, wk, wv, tie, sums, whole, sems):
    rows, tokens = b2i.shape
    missing = pl.ds(pl.multiple_of((lax.axis_index("head") ^ 3) * rows, 16), rows)
    whole[missing, :] = jnp.zeros((rows, tokens), whole.dtype)
    load_blocks([own.at[stream], near.at[stream], (b2i, b2o)], whole, sems)
    width, tiles = token_tiles(tokens)

    @pl.loop(0, tiles)
    def _(tile):
        columns = pl.ds(pl.multiple_of(tile * width, width), width)
        block = whole[:, columns]
        for k, matrix in enumerate((wk, wv, wq)):
            sums[k, :, columns] = rounded_dot(matrix[...], block)


def cut_kernel(count, *rest):
    matrices, (cut,) = rest[:-1], rest[-1:]
    rows = cut.shape[2]
    for owner in range(count):

        @pl.when((lax.axis_index("head") ^ 3) == owner)
        def _(owner=owner):
            for k, matrix in enumerate(matrices):
                cut[k] = matrix[:, owner * rows : (owner + 1) * rows]


def on_last(inner_ref, end_ref, body):
    for want, ref in ((True, inner_ref), (False, end_ref)):

        @pl.when(is_inner(lax.axis_index("head")) == want)
        def _(ref=ref):
            body(ref)


def state_kernel(inner_ref, end_ref, cut, sums, *rest):
    state, rounded = rest[-2:]

    def body(block):
        key = (sums[0] + rounded_dot(cut[0], block[...])).astype(jnp.bfloat16)
        value = (sums[1] + rounded_dot(cut[1], block[...])).astype(jnp.bfloat16)
        key = jnp.maximum(key, 0)
        for start in range(0, key.shape[0], HEAD_DIM):
            rows = slice(start, start + HEAD_DIM)
            total = lax.dot_general(
                value[rows], key[rows], (((1,), (1,)), ((), ())), preferred_element_type=jnp.float32
            )
            state[rows, :] = total
            rounded[rows, :] = total.astype(jnp.bfloat16)

    on_last(inner_ref, end_ref, body)


def query_kernel(inner_ref, end_ref, cut, sums, tie, query):
    def body(block):
        row = (sums[2] + rounded_dot(cut[2], block[...])).astype(jnp.bfloat16)
        query[...] = jnp.maximum(row, 0)

    on_last(inner_ref, end_ref, body)


def read_kernel(stream, parts, query, gain, *rest):
    out, held, sems = rest[-3:]
    copies = []
    for start in range(0, query.shape[0], HEAD_DIM):
        rows = slice(start, start + HEAD_DIM)
        total = sum(part[rows, :].astype(jnp.float32) for part in rest[:parts])
        reading = rounded_dot(total.astype(jnp.bfloat16), query[rows, :])
        scale = lax.rsqrt(jnp.mean(reading * reading, axis=0, keepdims=True) + 1e-06)
        held[rows, :] = (reading * scale * gain[rows, :]).astype(jnp.bfloat16)
        copies.append(pltpu.make_async_copy(held.at[rows, :], out.at[stream, rows, :], sems.at[len(copies)]))
        copies[-1].start()
    for copy in copies:
        copy.wait()


def partner_swap(value, axis):
    return lax.ppermute(value, axis, [(i, i ^ 1) for i in range(lax.axis_size(axis))])


def middle_swap(value, axis, other):
    wide, count = lax.axis_size(other), lax.axis_size(axis)
    pairs = []
    for j in range(wide):
        for i in range(count):
            if i in (1, 2):
                pairs.append((j * count + i, j * count + 3 - i))
            else:
                pairs.append((j * count + i, (j ^ 1 if j ^ 1 < wide else j) * count + i))
    return lax.ppermute(value, (other, axis), pairs)


def from_others(sent, axis):
    count = lax.axis_size(axis)
    got = []
    for step in range(count - 1, 0, -1):
        pairs = [(i, (i + step) % count) for i in range(count)]
        if count & (count - 1) == 0:
            pairs = [(i, i ^ step) for i in range(count)]
        got.append(lax.ppermute(sent, axis, pairs))
    return got


def entering(value, axis):
    count = lax.axis_size(axis)

    def earlier(value, reach):
        return lax.ppermute(value.astype(jnp.bfloat16), axis, [(i, i + reach) for i in range(count - reach)])

    total, reach = earlier(value, 1), 1
    while reach < count - 1:
        total = total.astype(jnp.float32)
        total, reach = total + earlier(total, reach).astype(jnp.float32), 2 * reach
    return total


def local(streams, w_query, w_key, w_value, gain):
    count = lax.axis_size("head")
    rows, tokens = streams.shape[2], streams.shape[1]
    width = w_query.shape[1]
    depth = rows * count
    columns = jnp.swapaxes(streams, 1, 2)
    matrices = (w_query.T, w_key.T, w_value.T)
    gain_column = gain.reshape(width, 1)

    one = 2 * width * depth * tokens
    cut = call(
        functools.partial(cut_kernel, count), jax.ShapeDtypeStruct((3, width, rows), jnp.bfloat16), IN_VMEM,
        [IN_VMEM] * 3, [], one // 4,
    )(matrices[1], matrices[2], matrices[0])
    across, far, across_end, far_end = [], [], [], []
    near = partner_swap(columns, "head")
    for stream in range(2):
        across.append(middle_swap(columns[stream], "head", "group"))
    for stream in range(2):
        far.append(middle_swap(near[stream], "head", "group"))
        ready, *_ = lax.optimization_barrier((across[stream], *([cut] if stream else [])))
        across_end.append(partner_swap(ready, "head"))
    whole = pltpu.VMEM((depth, tokens), jnp.bfloat16)
    sems = pltpu.SemaphoreType.DMA((4,))
    query_type = jax.ShapeDtypeStruct((width, tokens), jnp.bfloat16)
    state_types = [jax.ShapeDtypeStruct((width, HEAD_DIM), kind) for kind in (jnp.float32, jnp.bfloat16)]
    out_type = jax.ShapeDtypeStruct((2, width, tokens), jnp.bfloat16)

    read_scratch = [pltpu.VMEM((width, tokens), jnp.bfloat16), pltpu.SemaphoreType.DMA((width // HEAD_DIM,))]
    sums = []
    for stream in range(2):
        ready, *_ = lax.optimization_barrier((far[stream], across_end[stream], *sums))
        far_end.append(partner_swap(ready, "head"))
        sums.append(call(
            functools.partial(partial_kernel, stream), jax.ShapeDtypeStruct((3, width, tokens), jnp.float32), IN_VMEM,
            [ANYWHERE] * 4 + [IN_VMEM] * 3 + [ANYWHERE], [whole, sems], 3 * one,
        )(columns, near, far[stream], across_end[stream], *matrices, cut))
    prefix = parts = query = out = None
    for stream in range(2):
        ties = (sums[1],) if stream == 0 else (parts[0], query)
        state, rounded = call(
            state_kernel, state_types, (IN_VMEM,) * 2,
            [IN_VMEM] * 4 + [ANYWHERE] * len(ties), [], one // 2,
        )(across[stream], far_end[stream], cut, sums[stream], *ties)
        query = call(
            query_kernel, query_type, IN_VMEM, [IN_VMEM] * 4 + [ANYWHERE], [], one // 4,
        )(across[stream], far_end[stream], cut, sums[stream], state)
        parts = [state, *from_others(rounded, "tok")]
        if stream == 0:
            query, *parts = lax.optimization_barrier((query, *parts))
            parts = [sum(part.astype(jnp.float32) for part in parts)]
            prefix = entering(parts[0], "group")
        kept = [] if out is None else [out]
        out = call(
            functools.partial(read_kernel, stream, len(parts) + 1), out_type, ANYWHERE,
            [IN_VMEM] * (3 + len(parts)) + [ANYWHERE] * len(kept),
            read_scratch, one // 20, {3 + len(parts): 0} if kept else None,
        )(query, gain_column, prefix, *parts, *kept)
    return jnp.swapaxes(out, 1, 2)


def solution(mesh):
    return jax.shard_map(
        local,
        mesh=mesh,
        in_specs=(
            P(None, ("group", "tok"), "head"),
            P(None, "head"),
            P(None, "head"),
            P(None, "head"),
            P("head"),
        ),
        out_specs=P(None, ("group", "tok"), "head"),
        check_vma=False,
    )
```

```python
import functools

import jax
import jax.numpy as jnp
from jax import lax
from jax.experimental import pallas as pl
from jax.experimental.pallas import tpu as pltpu
from jax.sharding import PartitionSpec as P

HEAD_DIM = 112
VMEM_LIMIT = 20 * 1024 * 1024
ANYWHERE = pl.BlockSpec(memory_space=pl.ANY)
IN_VMEM = pl.BlockSpec(memory_space=pltpu.VMEM)


def call(body, outs, out_specs, in_specs, scratch, flops, aliases=None):
    return pl.pallas_call(
        body,
        out_shape=outs,
        in_specs=in_specs,
        out_specs=out_specs,
        scratch_shapes=scratch,
        input_output_aliases=aliases or {},
        compiler_params=pltpu.CompilerParams(vmem_limit_bytes=VMEM_LIMIT),
        cost_estimate=pl.CostEstimate(flops=flops // 64, bytes_accessed=1 << 10, transcendentals=0),
    )


def rounded_dot(matrix, block):
    return jnp.dot(matrix, block, preferred_element_type=jnp.float32)


def token_tiles(tokens):
    width = 256 if tokens % 256 == 0 else tokens
    return width, tokens // width


def is_inner(position):
    return (position == 1) | (position == 2)


def load_blocks(found, whole, sems):
    mine = lax.axis_index("head")
    rows = found[0].shape[0]

    def at(flip):
        return whole.at[pl.ds(pl.multiple_of((mine ^ flip) * rows, 16), rows), :]

    for flip, source in enumerate(found):
        if isinstance(source, tuple):
            for want, ref in ((True, source[0]), (False, source[1])):

                @pl.when(is_inner(mine) == want)
                def _(ref=ref, flip=flip):
                    pltpu.make_async_copy(ref, at(flip), sems.at[flip]).start()
        else:
            pltpu.make_async_copy(source, at(flip), sems.at[flip]).start()
    for flip in range(len(found)):
        pltpu.make_async_copy(at(flip), at(flip), sems.at[flip]).wait()


def partial_kernel(stream, own, near, b2i, b2o, wq, wk, wv, tie, sums, whole, sems):
    rows, tokens = b2i.shape
    missing = pl.ds(pl.multiple_of((lax.axis_index("head") ^ 3) * rows, 16), rows)
    whole[missing, :] = jnp.zeros((rows, tokens), whole.dtype)
    load_blocks([own.at[stream], near.at[stream], (b2i, b2o)], whole, sems)
    width, tiles = token_tiles(tokens)

    @pl.loop(0, tiles)
    def _(tile):
        columns = pl.ds(pl.multiple_of(tile * width, width), width)
        block = whole[:, columns]
        for k, matrix in enumerate((wk, wv, wq)):
            sums[k, :, columns] = rounded_dot(matrix[...], block)


def cut_kernel(count, *rest):
    matrices, (cut,) = rest[:-1], rest[-1:]
    rows = cut.shape[2]
    for owner in range(count):

        @pl.when((lax.axis_index("head") ^ 3) == owner)
        def _(owner=owner):
            for k, matrix in enumerate(matrices):
                cut[k] = matrix[:, owner * rows : (owner + 1) * rows]


def on_last(inner_ref, end_ref, body):
    for want, ref in ((True, inner_ref), (False, end_ref)):

        @pl.when(is_inner(lax.axis_index("head")) == want)
        def _(ref=ref):
            body(ref)


def state_kernel(span, inner_ref, end_ref, cut, sums, *rest):
    state = rest[-1]

    def body(block):
        key = (sums[0, span] + rounded_dot(cut[0, span], block[...])).astype(jnp.bfloat16)
        value = (sums[1, span] + rounded_dot(cut[1, span], block[...])).astype(jnp.bfloat16)
        key = jnp.maximum(key, 0)
        for start in range(0, key.shape[0], HEAD_DIM):
            rows = slice(start, start + HEAD_DIM)
            state[rows, :] = lax.dot_general(
                value[rows], key[rows], (((1,), (1,)), ((), ())), preferred_element_type=jnp.float32
            )

    on_last(inner_ref, end_ref, body)


def query_kernel(inner_ref, end_ref, cut, sums, tie, query):
    def body(block):
        row = (sums[2] + rounded_dot(cut[2], block[...])).astype(jnp.bfloat16)
        query[...] = jnp.maximum(row, 0)

    on_last(inner_ref, end_ref, body)


def read_kernel(stream, span, parts, query, gain, prefix, *rest):
    out, held, sems = rest[-3:]
    copies = []
    for start in range(span.start, span.stop, HEAD_DIM):
        rows, within = slice(start, start + HEAD_DIM), slice(start - span.start, start - span.start + HEAD_DIM)
        total = prefix[rows, :] + sum(part[within, :].astype(jnp.float32) for part in rest[:parts])
        reading = rounded_dot(total.astype(jnp.bfloat16), query[rows, :])
        scale = lax.rsqrt(jnp.mean(reading * reading, axis=0, keepdims=True) + 1e-06)
        held[rows, :] = (reading * scale * gain[rows, :]).astype(jnp.bfloat16)
        copies.append(pltpu.make_async_copy(held.at[rows, :], out.at[stream, rows, :], sems.at[len(copies)]))
        copies[-1].start()
    for copy in copies:
        copy.wait()


def partner_swap(value, axis):
    return lax.ppermute(value, axis, [(i, i ^ 1) for i in range(lax.axis_size(axis))])


def middle_swap(value, axis, other):
    wide, count = lax.axis_size(other), lax.axis_size(axis)
    pairs = []
    for j in range(wide):
        for i in range(count):
            if i in (1, 2):
                pairs.append((j * count + i, j * count + 3 - i))
            else:
                pairs.append((j * count + i, (j ^ 1 if j ^ 1 < wide else j) * count + i))
    return lax.ppermute(value, (other, axis), pairs)


def from_others(value, axis):
    count = lax.axis_size(axis)
    sent = value.astype(jnp.bfloat16)
    got = []
    for step in range(count - 1, 0, -1):
        pairs = [(i, (i + step) % count) for i in range(count)]
        if count & (count - 1) == 0:
            pairs = [(i, i ^ step) for i in range(count)]
        got.append(lax.ppermute(sent, axis, pairs))
    return got


def entering(value, axis):
    count = lax.axis_size(axis)
    total = lax.ppermute(value, axis, [(i, i + 1) for i in range(count - 1)])
    reach = 1
    while reach < count - 1:
        total = total + lax.ppermute(total, axis, [(i, i + reach) for i in range(count - reach)])
        reach *= 2
    return total


def local(streams, w_query, w_key, w_value, gain):
    count = lax.axis_size("head")
    rows, tokens = streams.shape[2], streams.shape[1]
    width = w_query.shape[1]
    depth = rows * count
    columns = jnp.swapaxes(streams, 1, 2)
    matrices = (w_query.T, w_key.T, w_value.T)
    gain_column = gain.reshape(width, 1)

    one = 2 * width * depth * tokens
    cut = call(
        functools.partial(cut_kernel, count), jax.ShapeDtypeStruct((3, width, rows), jnp.bfloat16), IN_VMEM,
        [IN_VMEM] * 3, [], one // 4,
    )(matrices[1], matrices[2], matrices[0])
    across, far, across_end, far_end = [], [], [], []
    near = partner_swap(columns, "head")
    for stream in range(2):
        across.append(middle_swap(columns[stream], "head", "group"))
    for stream in range(2):
        far.append(middle_swap(near[stream], "head", "group"))
        ready, *_ = lax.optimization_barrier((across[stream], *([cut] if stream else [])))
        across_end.append(partner_swap(ready, "head"))
    whole = pltpu.VMEM((depth, tokens), jnp.bfloat16)
    sems = pltpu.SemaphoreType.DMA((4,))
    query_type = jax.ShapeDtypeStruct((width, tokens), jnp.bfloat16)
    out_type = jax.ShapeDtypeStruct((2, width, tokens), jnp.bfloat16)

    read_scratch = [pltpu.VMEM((width, tokens), jnp.bfloat16), pltpu.SemaphoreType.DMA((width // HEAD_DIM,))]
    sums = []
    for stream in range(2):
        ready, *_ = lax.optimization_barrier((far[stream], across_end[stream], *sums))
        far_end.append(partner_swap(ready, "head"))
        sums.append(call(
            functools.partial(partial_kernel, stream), jax.ShapeDtypeStruct((3, width, tokens), jnp.float32), IN_VMEM,
            [ANYWHERE] * 4 + [IN_VMEM] * 3 + [ANYWHERE], [whole, sems], 3 * one,
        )(columns, near, far[stream], across_end[stream], *matrices, cut))
    everything = slice(0, width)
    middle = (width // HEAD_DIM + 1) // 2 * HEAD_DIM
    spans = ([everything], [span for span in (slice(0, middle), slice(middle, width)) if span.stop > span.start])
    prefix = clean = query = out = None
    for stream in range(2):
        ties = (sums[1],) if stream == 0 else (clean, query)
        parts = []
        for span in spans[stream]:
            state = call(
                functools.partial(state_kernel, span),
                jax.ShapeDtypeStruct((span.stop - span.start, HEAD_DIM), jnp.float32), IN_VMEM,
                [IN_VMEM] * 4 + [ANYWHERE] * len(ties), [], one // 2,
            )(across[stream], far_end[stream], cut, sums[stream], *ties)
            ties = (state,)
            parts.append([state, *from_others(state, "tok")])
        query = call(
            query_kernel, query_type, IN_VMEM, [IN_VMEM] * 4 + [ANYWHERE], [], one // 4,
        )(across[stream], far_end[stream], cut, sums[stream], state)
        if stream == 0:
            query, *terms = lax.optimization_barrier((query, *parts[0]))
            clean = sum(term.astype(jnp.float32) for term in terms)
            parts = [[clean]]
            prefix = entering(clean, "group")
        for span, terms in zip(spans[stream], parts):
            kept = [] if out is None else [out]
            out = call(
                functools.partial(read_kernel, stream, span, len(terms)), out_type, ANYWHERE,
                [IN_VMEM] * (3 + len(terms)) + [ANYWHERE] * len(kept),
                read_scratch, one // 20, {3 + len(terms): 0} if kept else None,
            )(query, gain_column, prefix, *terms, *kept)
    return jnp.swapaxes(out, 1, 2)


def solution(mesh):
    return jax.shard_map(
        local,
        mesh=mesh,
        in_specs=(
            P(None, ("group", "tok"), "head"),
            P(None, "head"),
            P(None, "head"),
            P(None, "head"),
            P("head"),
        ),
        out_specs=P(None, ("group", "tok"), "head"),
        check_vma=False,
    )
```

```python
import functools

import jax
import jax.numpy as jnp
from jax import lax
from jax.experimental import pallas as pl
from jax.experimental.pallas import tpu as pltpu
from jax.sharding import PartitionSpec as P

HEAD_DIM = 112
VMEM_LIMIT = 20 * 1024 * 1024
ANYWHERE = pl.BlockSpec(memory_space=pl.ANY)
IN_VMEM = pl.BlockSpec(memory_space=pltpu.VMEM)


def call(body, outs, out_specs, in_specs, scratch, flops, aliases=None):
    return pl.pallas_call(
        body,
        out_shape=outs,
        in_specs=in_specs,
        out_specs=out_specs,
        scratch_shapes=scratch,
        input_output_aliases=aliases or {},
        compiler_params=pltpu.CompilerParams(vmem_limit_bytes=VMEM_LIMIT),
        cost_estimate=pl.CostEstimate(flops=flops // 64, bytes_accessed=1 << 10, transcendentals=0),
    )


def rounded_dot(matrix, block):
    return jnp.dot(matrix, block, preferred_element_type=jnp.float32)


def token_tiles(tokens):
    width = 256 if tokens % 256 == 0 else tokens
    return width, tokens // width


def is_inner(position):
    return (position == 1) | (position == 2)


def load_blocks(found, whole, sems):
    mine = lax.axis_index("head")
    rows = found[0].shape[0]

    def at(flip):
        return whole.at[pl.ds(pl.multiple_of((mine ^ flip) * rows, 16), rows), :]

    for flip, source in enumerate(found):
        if isinstance(source, tuple):
            for want, ref in ((True, source[0]), (False, source[1])):

                @pl.when(is_inner(mine) == want)
                def _(ref=ref, flip=flip):
                    pltpu.make_async_copy(ref, at(flip), sems.at[flip]).start()
        else:
            pltpu.make_async_copy(source, at(flip), sems.at[flip]).start()
    for flip in range(len(found)):
        pltpu.make_async_copy(at(flip), at(flip), sems.at[flip]).wait()


def partial_kernel(stream, own, near, b2i, b2o, wq, wk, wv, tie, sums, whole, sems):
    rows, tokens = b2i.shape
    missing = pl.ds(pl.multiple_of((lax.axis_index("head") ^ 3) * rows, 16), rows)
    whole[missing, :] = jnp.zeros((rows, tokens), whole.dtype)
    load_blocks([own.at[stream], near.at[stream], (b2i, b2o)], whole, sems)
    width, tiles = token_tiles(tokens)

    @pl.loop(0, tiles)
    def _(tile):
        columns = pl.ds(pl.multiple_of(tile * width, width), width)
        block = whole[:, columns]
        for k, matrix in enumerate((wk, wv, wq)):
            sums[k, :, columns] = rounded_dot(matrix[...], block)


def cut_kernel(count, *rest):
    matrices, (cut,) = rest[:-1], rest[-1:]
    rows = cut.shape[2]
    for owner in range(count):

        @pl.when((lax.axis_index("head") ^ 3) == owner)
        def _(owner=owner):
            for k, matrix in enumerate(matrices):
                cut[k] = matrix[:, owner * rows : (owner + 1) * rows]


def on_last(inner_ref, end_ref, body):
    for want, ref in ((True, inner_ref), (False, end_ref)):

        @pl.when(is_inner(lax.axis_index("head")) == want)
        def _(ref=ref):
            body(ref)


def state_kernel(inner_ref, end_ref, cut, sums, *rest):
    state = rest[-1]

    def body(block):
        key = (sums[0] + rounded_dot(cut[0], block[...])).astype(jnp.bfloat16)
        value = (sums[1] + rounded_dot(cut[1], block[...])).astype(jnp.bfloat16)
        key = jnp.maximum(key, 0)
        for start in range(0, key.shape[0], HEAD_DIM):
            rows = slice(start, start + HEAD_DIM)
            state[rows, :] = lax.dot_general(
                value[rows], key[rows], (((1,), (1,)), ((), ())), preferred_element_type=jnp.float32
            )

    on_last(inner_ref, end_ref, body)


def query_kernel(inner_ref, end_ref, cut, sums, tie, query):
    def body(block):
        row = (sums[2] + rounded_dot(cut[2], block[...])).astype(jnp.bfloat16)
        query[...] = jnp.maximum(row, 0)

    on_last(inner_ref, end_ref, body)


def read_kernel(stream, parts, query, gain, *rest):
    out, held, sems = rest[-3:]
    copies = []
    for start in range(0, query.shape[0], HEAD_DIM):
        rows = slice(start, start + HEAD_DIM)
        total = sum(part[rows, :].astype(jnp.float32) for part in rest[:parts])
        reading = rounded_dot(total.astype(jnp.bfloat16), query[rows, :])
        scale = lax.rsqrt(jnp.mean(reading * reading, axis=0, keepdims=True) + 1e-06)
        held[rows, :] = (reading * scale * gain[rows, :]).astype(jnp.bfloat16)
        copies.append(pltpu.make_async_copy(held.at[rows, :], out.at[stream, rows, :], sems.at[len(copies)]))
        copies[-1].start()
    for copy in copies:
        copy.wait()


def partner_swap(value, axis):
    return lax.ppermute(value, axis, [(i, i ^ 1) for i in range(lax.axis_size(axis))])


def middle_swap(value, axis, other):
    wide, count = lax.axis_size(other), lax.axis_size(axis)
    pairs = []
    for j in range(wide):
        for i in range(count):
            if i in (1, 2):
                pairs.append((j * count + i, j * count + 3 - i))
            else:
                pairs.append((j * count + i, (j ^ 1 if j ^ 1 < wide else j) * count + i))
    return lax.ppermute(value, (other, axis), pairs)


def from_others(value, axis):
    count = lax.axis_size(axis)
    sent = value.astype(jnp.bfloat16)
    got = []
    for step in sorted(range(1, count), key=lambda step: (step != count // 2, -step)):
        pairs = [(i, (i + step) % count) for i in range(count)]
        if count & (count - 1) == 0:
            pairs = [(i, i ^ step) for i in range(count)]
        got.append(lax.ppermute(sent, axis, pairs))
    return got


def entering(value, axis):
    count = lax.axis_size(axis)
    total = lax.ppermute(value, axis, [(i, i + 1) for i in range(count - 1)])
    reach = 1
    while reach < count - 1:
        total = total + lax.ppermute(total, axis, [(i, i + reach) for i in range(count - reach)])
        reach *= 2
    return total


def local(streams, w_query, w_key, w_value, gain):
    count = lax.axis_size("head")
    rows, tokens = streams.shape[2], streams.shape[1]
    width = w_query.shape[1]
    depth = rows * count
    columns = jnp.swapaxes(streams, 1, 2)
    matrices = (w_query.T, w_key.T, w_value.T)
    gain_column = gain.reshape(width, 1)

    one = 2 * width * depth * tokens
    cut = call(
        functools.partial(cut_kernel, count), jax.ShapeDtypeStruct((3, width, rows), jnp.bfloat16), IN_VMEM,
        [IN_VMEM] * 3, [], one // 4,
    )(matrices[1], matrices[2], matrices[0])
    across, far, across_end, far_end = [], [], [], []
    near = partner_swap(columns, "head")
    for stream in range(2):
        across.append(middle_swap(columns[stream], "head", "group"))
    for stream in range(2):
        far.append(middle_swap(near[stream], "head", "group"))
        ready, *_ = lax.optimization_barrier((across[stream], *([cut] if stream else [])))
        across_end.append(partner_swap(ready, "head"))
    whole = pltpu.VMEM((depth, tokens), jnp.bfloat16)
    sems = pltpu.SemaphoreType.DMA((4,))
    query_type = jax.ShapeDtypeStruct((width, tokens), jnp.bfloat16)
    state_type = jax.ShapeDtypeStruct((width, HEAD_DIM), jnp.float32)
    out_type = jax.ShapeDtypeStruct((2, width, tokens), jnp.bfloat16)

    read_scratch = [pltpu.VMEM((width, tokens), jnp.bfloat16), pltpu.SemaphoreType.DMA((width // HEAD_DIM,))]
    sums = []
    for stream in range(2):
        ready, *_ = lax.optimization_barrier((far[stream], across_end[stream], *sums))
        far_end.append(partner_swap(ready, "head"))
        sums.append(call(
            functools.partial(partial_kernel, stream), jax.ShapeDtypeStruct((3, width, tokens), jnp.float32), IN_VMEM,
            [ANYWHERE] * 4 + [IN_VMEM] * 3 + [ANYWHERE], [whole, sems], 3 * one,
        )(columns, near, far[stream], across_end[stream], *matrices, cut))
    prefix = parts = query = out = None
    for stream in range(2):
        ties = (sums[1],) if stream == 0 else (parts[0], query)
        state = call(
            state_kernel, state_type, IN_VMEM,
            [IN_VMEM] * 4 + [ANYWHERE] * len(ties), [], one // 2,
        )(across[stream], far_end[stream], cut, sums[stream], *ties)
        query = call(
            query_kernel, query_type, IN_VMEM, [IN_VMEM] * 4 + [ANYWHERE], [], one // 4,
        )(across[stream], far_end[stream], cut, sums[stream], state)
        parts = [state, *from_others(state, "tok")]
        if stream == 0:
            query, *parts = lax.optimization_barrier((query, *parts))
            parts = [sum(part.astype(jnp.float32) for part in parts)]
            prefix = entering(parts[0], "group")
        kept = [] if out is None else [out]
        out = call(
            functools.partial(read_kernel, stream, len(parts) + 1), out_type, ANYWHERE,
            [IN_VMEM] * (3 + len(parts)) + [ANYWHERE] * len(kept),
            read_scratch, one // 20, {3 + len(parts): 0} if kept else None,
        )(query, gain_column, prefix, *parts, *kept)
    return jnp.swapaxes(out, 1, 2)


def solution(mesh):
    return jax.shard_map(
        local,
        mesh=mesh,
        in_specs=(
            P(None, ("group", "tok"), "head"),
            P(None, "head"),
            P(None, "head"),
            P(None, "head"),
            P("head"),
        ),
        out_specs=P(None, ("group", "tok"), "head"),
        check_vma=False,
    )
```

```python
import functools

import jax
import jax.numpy as jnp
from jax import lax
from jax.experimental import pallas as pl
from jax.experimental.pallas import tpu as pltpu
from jax.sharding import PartitionSpec as P

HEAD_DIM = 112
VMEM_LIMIT = 20 * 1024 * 1024
ANYWHERE = pl.BlockSpec(memory_space=pl.ANY)
IN_VMEM = pl.BlockSpec(memory_space=pltpu.VMEM)


def call(body, outs, out_specs, in_specs, scratch, flops, aliases=None):
    return pl.pallas_call(
        body,
        out_shape=outs,
        in_specs=in_specs,
        out_specs=out_specs,
        scratch_shapes=scratch,
        input_output_aliases=aliases or {},
        compiler_params=pltpu.CompilerParams(vmem_limit_bytes=VMEM_LIMIT),
        cost_estimate=pl.CostEstimate(flops=flops // 64, bytes_accessed=1 << 10, transcendentals=0),
    )


def rounded_dot(matrix, block):
    return jnp.dot(matrix, block, preferred_element_type=jnp.float32)


def token_tiles(tokens):
    width = 256 if tokens % 256 == 0 else tokens
    return width, tokens // width


def is_inner(position):
    return (position == 1) | (position == 2)


def load_blocks(found, whole, sems):
    mine = lax.axis_index("head")
    rows = found[0].shape[0]

    def at(flip):
        return whole.at[pl.ds(pl.multiple_of((mine ^ flip) * rows, 16), rows), :]

    for flip, source in enumerate(found):
        if isinstance(source, tuple):
            for want, ref in ((True, source[0]), (False, source[1])):

                @pl.when(is_inner(mine) == want)
                def _(ref=ref, flip=flip):
                    pltpu.make_async_copy(ref, at(flip), sems.at[flip]).start()
        else:
            pltpu.make_async_copy(source, at(flip), sems.at[flip]).start()
    for flip in range(len(found)):
        pltpu.make_async_copy(at(flip), at(flip), sems.at[flip]).wait()


def partial_kernel(stream, own, near, b2i, b2o, wq, wk, wv, tie, sums, whole, sems):
    rows, tokens = b2i.shape
    missing = pl.ds(pl.multiple_of((lax.axis_index("head") ^ 3) * rows, 16), rows)
    whole[missing, :] = jnp.zeros((rows, tokens), whole.dtype)
    load_blocks([own.at[stream], near.at[stream], (b2i, b2o)], whole, sems)
    width, tiles = token_tiles(tokens)

    @pl.loop(0, tiles)
    def _(tile):
        columns = pl.ds(pl.multiple_of(tile * width, width), width)
        block = whole[:, columns]
        for k, matrix in enumerate((wk, wv, wq)):
            sums[k, :, columns] = rounded_dot(matrix[...], block)


def cut_kernel(count, *rest):
    matrices, (cut,) = rest[:-1], rest[-1:]
    rows = cut.shape[2]
    for owner in range(count):

        @pl.when((lax.axis_index("head") ^ 3) == owner)
        def _(owner=owner):
            for k, matrix in enumerate(matrices):
                cut[k] = matrix[:, owner * rows : (owner + 1) * rows]


def on_last(columns, inner_ref, end_ref, body):
    @pl.when(is_inner(lax.axis_index("head")))
    def _():
        body(inner_ref[:, columns])

    @pl.when(jnp.logical_not(is_inner(lax.axis_index("head"))))
    def _():
        body(end_ref[...])


def state_kernel(columns, before, inner_ref, end_ref, cut, sums, *rest):
    state = rest[-1]

    def body(block):
        key = (sums[0, :, columns] + rounded_dot(cut[0], block)).astype(jnp.bfloat16)
        value = (sums[1, :, columns] + rounded_dot(cut[1], block)).astype(jnp.bfloat16)
        key = jnp.maximum(key, 0)
        for start in range(0, key.shape[0], HEAD_DIM):
            rows = slice(start, start + HEAD_DIM)
            total = lax.dot_general(
                value[rows], key[rows], (((1,), (1,)), ((), ())), preferred_element_type=jnp.float32
            )
            state[rows, :] = total + rest[0][rows, :] if before else total

    on_last(columns, inner_ref, end_ref, body)


def query_kernel(pieces, inner_ref, *rest):
    cut, sums, _, query = rest[-4:]
    for columns, end_ref in zip(pieces, rest):

        def body(block, columns=columns):
            row = (sums[2, :, columns] + rounded_dot(cut[2], block)).astype(jnp.bfloat16)
            query[:, columns] = jnp.maximum(row, 0)

        on_last(columns, inner_ref, end_ref, body)


def read_kernel(stream, parts, query, gain, *rest):
    out, held, sems = rest[-3:]
    copies = []
    for start in range(0, query.shape[0], HEAD_DIM):
        rows = slice(start, start + HEAD_DIM)
        total = sum(part[rows, :].astype(jnp.float32) for part in rest[:parts])
        reading = rounded_dot(total.astype(jnp.bfloat16), query[rows, :])
        scale = lax.rsqrt(jnp.mean(reading * reading, axis=0, keepdims=True) + 1e-06)
        held[rows, :] = (reading * scale * gain[rows, :]).astype(jnp.bfloat16)
        copies.append(pltpu.make_async_copy(held.at[rows, :], out.at[stream, rows, :], sems.at[len(copies)]))
        copies[-1].start()
    for copy in copies:
        copy.wait()


def partner_swap(value, axis):
    return lax.ppermute(value, axis, [(i, i ^ 1) for i in range(lax.axis_size(axis))])


def middle_swap(value, axis, other):
    wide, count = lax.axis_size(other), lax.axis_size(axis)
    pairs = []
    for j in range(wide):
        for i in range(count):
            if i in (1, 2):
                pairs.append((j * count + i, j * count + 3 - i))
            else:
                pairs.append((j * count + i, (j ^ 1 if j ^ 1 < wide else j) * count + i))
    return lax.ppermute(value, (other, axis), pairs)


def from_others(value, axis):
    count = lax.axis_size(axis)
    sent = value.astype(jnp.bfloat16)
    got = []
    for step in range(count - 1, 0, -1):
        pairs = [(i, (i + step) % count) for i in range(count)]
        if count & (count - 1) == 0:
            pairs = [(i, i ^ step) for i in range(count)]
        got.append(lax.ppermute(sent, axis, pairs))
    return got


def entering(value, axis):
    count = lax.axis_size(axis)
    total = lax.ppermute(value, axis, [(i, i + 1) for i in range(count - 1)])
    reach = 1
    while reach < count - 1:
        total = total + lax.ppermute(total, axis, [(i, i + reach) for i in range(count - reach)])
        reach *= 2
    return total


def local(streams, w_query, w_key, w_value, gain):
    count = lax.axis_size("head")
    rows, tokens = streams.shape[2], streams.shape[1]
    width = w_query.shape[1]
    depth = rows * count
    columns = jnp.swapaxes(streams, 1, 2)
    matrices = (w_query.T, w_key.T, w_value.T)
    gain_column = gain.reshape(width, 1)

    one = 2 * width * depth * tokens
    cut = call(
        functools.partial(cut_kernel, count), jax.ShapeDtypeStruct((3, width, rows), jnp.bfloat16), IN_VMEM,
        [IN_VMEM] * 3, [], one // 4,
    )(matrices[1], matrices[2], matrices[0])
    across, far, across_end, far_end = [], [], [], []
    near = partner_swap(columns, "head")
    for stream in range(2):
        across.append(middle_swap(columns[stream], "head", "group"))
    for stream in range(2):
        far.append(middle_swap(near[stream], "head", "group"))
        ready, *_ = lax.optimization_barrier((across[stream], *([cut] if stream else [])))
        across_end.append(partner_swap(ready, "head"))
    whole = pltpu.VMEM((depth, tokens), jnp.bfloat16)
    sems = pltpu.SemaphoreType.DMA((4,))
    query_type = jax.ShapeDtypeStruct((width, tokens), jnp.bfloat16)
    state_type = jax.ShapeDtypeStruct((width, HEAD_DIM), jnp.float32)
    out_type = jax.ShapeDtypeStruct((2, width, tokens), jnp.bfloat16)

    read_scratch = [pltpu.VMEM((width, tokens), jnp.bfloat16), pltpu.SemaphoreType.DMA((width // HEAD_DIM,))]
    most = tokens - 128 if tokens % 128 == 0 and tokens > 128 else 0
    pieces = ([slice(0, tokens)], [slice(a, b) for a, b in ((0, most), (most, tokens)) if b > a])
    sums = []
    for stream in range(2):
        ready, *_ = lax.optimization_barrier((far[stream], across_end[stream], *sums))
        far_end.append([partner_swap(ready[:, columns], "head") for columns in pieces[stream]])
        sums.append(call(
            functools.partial(partial_kernel, stream), jax.ShapeDtypeStruct((3, width, tokens), jnp.float32), IN_VMEM,
            [ANYWHERE] * 4 + [IN_VMEM] * 3 + [ANYWHERE], [whole, sems], 3 * one,
        )(columns, near, far[stream], across_end[stream], *matrices, cut))
    state_of = lambda stream, piece, before, ties: call(
        functools.partial(state_kernel, pieces[stream][piece], len(before)), state_type, IN_VMEM,
        [IN_VMEM] * (4 + len(before)) + [ANYWHERE] * len(ties), [], one // 2,
    )(across[stream], far_end[stream][piece], cut, sums[stream], *before, *ties)
    prefix = parts = query = out = None
    early = []
    for stream in range(2):
        ties = (sums[1],) if stream == 0 else (parts[0], query)
        state = state_of(stream, len(pieces[stream]) - 1, early, ties)
        query = call(
            functools.partial(query_kernel, pieces[stream]), query_type, IN_VMEM,
            [IN_VMEM] * (3 + len(pieces[stream])) + [ANYWHERE], [], one // 4,
        )(across[stream], *far_end[stream], cut, sums[stream], state)
        parts = [state, *from_others(state, "tok")]
        if stream == 0:
            for piece in range(len(pieces[1]) - 1):
                early = [state_of(1, piece, early, (query,))]
            query, parts, early = lax.optimization_barrier((query, parts, early))
            parts = [sum(part.astype(jnp.float32) for part in parts)]
            prefix = entering(parts[0], "group")
        kept = [] if out is None else [out]
        out = call(
            functools.partial(read_kernel, stream, len(parts) + 1), out_type, ANYWHERE,
            [IN_VMEM] * (3 + len(parts)) + [ANYWHERE] * len(kept),
            read_scratch, one // 20, {3 + len(parts): 0} if kept else None,
        )(query, gain_column, prefix, *parts, *kept)
    return jnp.swapaxes(out, 1, 2)


def solution(mesh):
    return jax.shard_map(
        local,
        mesh=mesh,
        in_specs=(
            P(None, ("group", "tok"), "head"),
            P(None, "head"),
            P(None, "head"),
            P(None, "head"),
            P("head"),
        ),
        out_specs=P(None, ("group", "tok"), "head"),
        check_vma=False,
    )
```

```python
import functools

import jax
import jax.numpy as jnp
from jax import lax
from jax.experimental import pallas as pl
from jax.experimental.pallas import tpu as pltpu
from jax.sharding import PartitionSpec as P

HEAD_DIM = 112
VMEM_LIMIT = 20 * 1024 * 1024
ANYWHERE = pl.BlockSpec(memory_space=pl.ANY)
IN_VMEM = pl.BlockSpec(memory_space=pltpu.VMEM)


def call(body, outs, out_specs, in_specs, scratch, flops, aliases=None):
    return pl.pallas_call(
        body,
        out_shape=outs,
        in_specs=in_specs,
        out_specs=out_specs,
        scratch_shapes=scratch,
        input_output_aliases=aliases or {},
        compiler_params=pltpu.CompilerParams(vmem_limit_bytes=VMEM_LIMIT),
        cost_estimate=pl.CostEstimate(flops=flops // 64, bytes_accessed=1 << 10, transcendentals=0),
    )


def rounded_dot(matrix, block):
    return jnp.dot(matrix, block, preferred_element_type=jnp.float32)


def token_tiles(tokens):
    width = 256 if tokens % 256 == 0 else tokens
    return width, tokens // width


def is_inner(position):
    return (position == 1) | (position == 2)


def load_blocks(found, whole, sems):
    mine = lax.axis_index("head")
    rows = found[0].shape[0]

    def at(flip):
        return whole.at[pl.ds(pl.multiple_of((mine ^ flip) * rows, 16), rows), :]

    for flip, source in enumerate(found):
        if isinstance(source, tuple):
            for want, ref in ((True, source[0]), (False, source[1])):

                @pl.when(is_inner(mine) == want)
                def _(ref=ref, flip=flip):
                    pltpu.make_async_copy(ref, at(flip), sems.at[flip]).start()
        else:
            pltpu.make_async_copy(source, at(flip), sems.at[flip]).start()
    for flip in range(len(found)):
        pltpu.make_async_copy(at(flip), at(flip), sems.at[flip]).wait()


def partial_kernel(stream, own, near, b2i, b2o, wq, wk, wv, tie, sums, whole, sems):
    rows, tokens = b2i.shape
    missing = pl.ds(pl.multiple_of((lax.axis_index("head") ^ 3) * rows, 16), rows)
    whole[missing, :] = jnp.zeros((rows, tokens), whole.dtype)
    load_blocks([own.at[stream], near.at[stream], (b2i, b2o)], whole, sems)
    width, tiles = token_tiles(tokens)

    @pl.loop(0, tiles)
    def _(tile):
        columns = pl.ds(pl.multiple_of(tile * width, width), width)
        block = whole[:, columns]
        for k, matrix in enumerate((wk, wv, wq)):
            sums[k, :, columns] = rounded_dot(matrix[...], block)


def cut_kernel(count, *rest):
    matrices, (cut,) = rest[:-1], rest[-1:]
    rows = cut.shape[2]
    for owner in range(count):

        @pl.when((lax.axis_index("head") ^ 3) == owner)
        def _(owner=owner):
            for k, matrix in enumerate(matrices):
                cut[k] = matrix[:, owner * rows : (owner + 1) * rows]


def on_last(columns, inner_ref, end_ref, body):
    @pl.when(is_inner(lax.axis_index("head")))
    def _():
        body(inner_ref[:, columns])

    @pl.when(jnp.logical_not(is_inner(lax.axis_index("head"))))
    def _():
        body(end_ref[...])


def state_kernel(columns, before, inner_ref, end_ref, cut, sums, *rest):
    state = rest[-1]

    def body(block):
        key = (sums[0, :, columns] + rounded_dot(cut[0], block)).astype(jnp.bfloat16)
        value = (sums[1, :, columns] + rounded_dot(cut[1], block)).astype(jnp.bfloat16)
        key = jnp.maximum(key, 0)
        for start in range(0, key.shape[0], HEAD_DIM):
            rows = slice(start, start + HEAD_DIM)
            total = lax.dot_general(
                value[rows], key[rows], (((1,), (1,)), ((), ())), preferred_element_type=jnp.float32
            )
            state[rows, :] = total + rest[0][rows, :] if before else total

    on_last(columns, inner_ref, end_ref, body)


def query_kernel(pieces, inner_ref, *rest):
    cut, sums, _, query = rest[-4:]
    for columns, end_ref in zip(pieces, rest):

        def body(block, columns=columns):
            row = (sums[2, :, columns] + rounded_dot(cut[2], block)).astype(jnp.bfloat16)
            query[:, columns] = jnp.maximum(row, 0)

        on_last(columns, inner_ref, end_ref, body)


def read_kernel(stream, parts, query, gain, *rest):
    out, held, sems = rest[-3:]
    copies = []
    for start in range(0, query.shape[0], HEAD_DIM):
        rows = slice(start, start + HEAD_DIM)
        total = 0.0
        for part in rest[:parts]:
            terms = [part[rows, :]] if len(part.shape) == 2 else [part[k, rows, :] for k in range(part.shape[0])]
            total += sum(term.astype(jnp.float32) for term in terms)
        reading = rounded_dot(total.astype(jnp.bfloat16), query[rows, :])
        scale = lax.rsqrt(jnp.mean(reading * reading, axis=0, keepdims=True) + 1e-06)
        held[rows, :] = (reading * scale * gain[rows, :]).astype(jnp.bfloat16)
        copies.append(pltpu.make_async_copy(held.at[rows, :], out.at[stream, rows, :], sems.at[len(copies)]))
        copies[-1].start()
    for copy in copies:
        copy.wait()


def partner_swap(value, axis):
    return lax.ppermute(value, axis, [(i, i ^ 1) for i in range(lax.axis_size(axis))])


def middle_swap(value, axis, other):
    wide, count = lax.axis_size(other), lax.axis_size(axis)
    pairs = []
    for j in range(wide):
        for i in range(count):
            if i in (1, 2):
                pairs.append((j * count + i, j * count + 3 - i))
            else:
                pairs.append((j * count + i, (j ^ 1 if j ^ 1 < wide else j) * count + i))
    return lax.ppermute(value, (other, axis), pairs)


def from_others(value, axis):
    count = lax.axis_size(axis)
    sent = value.astype(jnp.bfloat16)
    got = []
    for step in range(count - 1, 0, -1):
        pairs = [(i, (i + step) % count) for i in range(count)]
        if count & (count - 1) == 0:
            pairs = [(i, i ^ step) for i in range(count)]
        got.append(lax.ppermute(sent, axis, pairs))
    return got


def entering(value, axis):
    count = lax.axis_size(axis)
    total = lax.ppermute(value, axis, [(i, i + 1) for i in range(count - 1)])
    reach = 1
    while reach < count - 1:
        total = total + lax.ppermute(total, axis, [(i, i + reach) for i in range(count - reach)])
        reach *= 2
    return total


def local(streams, w_query, w_key, w_value, gain):
    count = lax.axis_size("head")
    rows, tokens = streams.shape[2], streams.shape[1]
    width = w_query.shape[1]
    depth = rows * count
    columns = jnp.swapaxes(streams, 1, 2)
    matrices = (w_query.T, w_key.T, w_value.T)
    gain_column = gain.reshape(width, 1)

    one = 2 * width * depth * tokens
    cut = call(
        functools.partial(cut_kernel, count), jax.ShapeDtypeStruct((3, width, rows), jnp.bfloat16), IN_VMEM,
        [IN_VMEM] * 3, [], one // 4,
    )(matrices[1], matrices[2], matrices[0])
    across, far, across_end, far_end = [], [], [], []
    near = partner_swap(columns, "head")
    for stream in range(2):
        across.append(middle_swap(columns[stream], "head", "group"))
    for stream in range(2):
        far.append(middle_swap(near[stream], "head", "group"))
        ready, *_ = lax.optimization_barrier((across[stream], *([cut] if stream else [])))
        across_end.append(partner_swap(ready, "head"))
    whole = pltpu.VMEM((depth, tokens), jnp.bfloat16)
    sems = pltpu.SemaphoreType.DMA((4,))
    query_type = jax.ShapeDtypeStruct((width, tokens), jnp.bfloat16)
    state_type = jax.ShapeDtypeStruct((width, HEAD_DIM), jnp.float32)
    out_type = jax.ShapeDtypeStruct((2, width, tokens), jnp.bfloat16)

    read_scratch = [pltpu.VMEM((width, tokens), jnp.bfloat16), pltpu.SemaphoreType.DMA((width // HEAD_DIM,))]
    most = tokens - 128 if tokens % 128 == 0 and tokens > 128 else 0
    pieces = ([slice(0, tokens)], [slice(a, b) for a, b in ((0, most), (most, tokens)) if b > a])
    sums = []
    for stream in range(2):
        ready, *_ = lax.optimization_barrier((far[stream], across_end[stream], *sums))
        far_end.append([partner_swap(ready[:, columns], "head") for columns in pieces[stream]])
        sums.append(call(
            functools.partial(partial_kernel, stream), jax.ShapeDtypeStruct((3, width, tokens), jnp.float32), IN_VMEM,
            [ANYWHERE] * 4 + [IN_VMEM] * 3 + [ANYWHERE], [whole, sems], 3 * one,
        )(columns, near, far[stream], across_end[stream], *matrices, cut))
    state_of = lambda stream, piece, before, ties: call(
        functools.partial(state_kernel, pieces[stream][piece], len(before)), state_type, IN_VMEM,
        [IN_VMEM] * (4 + len(before)) + [ANYWHERE] * len(ties), [], one // 2,
    )(across[stream], far_end[stream][piece], cut, sums[stream], *before, *ties)
    prefix = parts = query = out = None
    early = []
    for stream in range(2):
        ties = (sums[1],) if stream == 0 else (parts[0], query)
        state = state_of(stream, len(pieces[stream]) - 1, early, ties)
        query = call(
            functools.partial(query_kernel, pieces[stream]), query_type, IN_VMEM,
            [IN_VMEM] * (3 + len(pieces[stream])) + [ANYWHERE], [], one // 4,
        )(across[stream], *far_end[stream], cut, sums[stream], state)
        if stream == 1:
            parts = [lax.all_gather(state.astype(jnp.bfloat16), "tok")]
        else:
            parts = [state, *from_others(state, "tok")]
            for piece in range(len(pieces[1]) - 1):
                early = [state_of(1, piece, early, (query,))]
            query, parts, early = lax.optimization_barrier((query, parts, early))
            parts = [sum(part.astype(jnp.float32) for part in parts)]
            prefix = entering(parts[0], "group")
        kept = [] if out is None else [out]
        out = call(
            functools.partial(read_kernel, stream, len(parts) + 1), out_type, ANYWHERE,
            [IN_VMEM] * (3 + len(parts)) + [ANYWHERE] * len(kept),
            read_scratch, one // 20, {3 + len(parts): 0} if kept else None,
        )(query, gain_column, prefix, *parts, *kept)
    return jnp.swapaxes(out, 1, 2)


def solution(mesh):
    return jax.shard_map(
        local,
        mesh=mesh,
        in_specs=(
            P(None, ("group", "tok"), "head"),
            P(None, "head"),
            P(None, "head"),
            P(None, "head"),
            P("head"),
        ),
        out_specs=P(None, ("group", "tok"), "head"),
        check_vma=False,
    )
```

```python
import functools

import jax
import jax.numpy as jnp
from jax import lax
from jax.experimental import pallas as pl
from jax.experimental.pallas import tpu as pltpu
from jax.sharding import PartitionSpec as P

HEAD_DIM = 112
VMEM_LIMIT = 20 * 1024 * 1024
ANYWHERE = pl.BlockSpec(memory_space=pl.ANY)
IN_VMEM = pl.BlockSpec(memory_space=pltpu.VMEM)


def call(body, outs, out_specs, in_specs, scratch, flops, aliases=None):
    return pl.pallas_call(
        body,
        out_shape=outs,
        in_specs=in_specs,
        out_specs=out_specs,
        scratch_shapes=scratch,
        input_output_aliases=aliases or {},
        compiler_params=pltpu.CompilerParams(vmem_limit_bytes=VMEM_LIMIT),
        cost_estimate=pl.CostEstimate(flops=flops // 64, bytes_accessed=1 << 10, transcendentals=0),
    )


def rounded_dot(matrix, block):
    return jnp.dot(matrix, block, preferred_element_type=jnp.float32)


def token_tiles(tokens):
    width = 256 if tokens % 256 == 0 else tokens
    return width, tokens // width


def is_inner(position):
    return (position == 1) | (position == 2)


def load_blocks(found, whole, sems):
    mine = lax.axis_index("head")
    rows = found[0].shape[0]

    def at(flip):
        return whole.at[pl.ds(pl.multiple_of((mine ^ flip) * rows, 16), rows), :]

    for flip, source in enumerate(found):
        if isinstance(source, tuple):
            for want, ref in ((True, source[0]), (False, source[1])):

                @pl.when(is_inner(mine) == want)
                def _(ref=ref, flip=flip):
                    pltpu.make_async_copy(ref, at(flip), sems.at[flip]).start()
        else:
            pltpu.make_async_copy(source, at(flip), sems.at[flip]).start()
    for flip in range(len(found)):
        pltpu.make_async_copy(at(flip), at(flip), sems.at[flip]).wait()


def partial_kernel(stream, own, near, b2i, b2o, wq, wk, wv, tie, sums, whole, sems):
    rows, tokens = b2i.shape
    missing = pl.ds(pl.multiple_of((lax.axis_index("head") ^ 3) * rows, 16), rows)
    whole[missing, :] = jnp.zeros((rows, tokens), whole.dtype)
    load_blocks([own.at[stream], near.at[stream], (b2i, b2o)], whole, sems)
    width, tiles = token_tiles(tokens)

    @pl.loop(0, tiles)
    def _(tile):
        columns = pl.ds(pl.multiple_of(tile * width, width), width)
        block = whole[:, columns]
        for k, matrix in enumerate((wk, wv, wq)):
            sums[k, :, columns] = rounded_dot(matrix[...], block)


def cut_kernel(count, *rest):
    matrices, (cut,) = rest[:-1], rest[-1:]
    rows = cut.shape[2]
    for owner in range(count):

        @pl.when((lax.axis_index("head") ^ 3) == owner)
        def _(owner=owner):
            for k, matrix in enumerate(matrices):
                cut[k] = matrix[:, owner * rows : (owner + 1) * rows]


def on_last(columns, inner_ref, end_ref, body):
    @pl.when(is_inner(lax.axis_index("head")))
    def _():
        body(inner_ref[:, columns])

    @pl.when(jnp.logical_not(is_inner(lax.axis_index("head"))))
    def _():
        body(end_ref[...])


def state_kernel(columns, before, inner_ref, end_ref, cut, sums, *rest):
    state = rest[-1]

    def body(block):
        key = (sums[0, :, columns] + rounded_dot(cut[0], block)).astype(jnp.bfloat16)
        value = (sums[1, :, columns] + rounded_dot(cut[1], block)).astype(jnp.bfloat16)
        key = jnp.maximum(key, 0)
        for start in range(0, key.shape[0], HEAD_DIM):
            rows = slice(start, start + HEAD_DIM)
            total = lax.dot_general(
                value[rows], key[rows], (((1,), (1,)), ((), ())), preferred_element_type=jnp.float32
            )
            state[rows, :] = total + rest[0][rows, :] if before else total

    on_last(columns, inner_ref, end_ref, body)


def query_kernel(pieces, inner_ref, *rest):
    cut, sums, _, query = rest[-4:]
    for columns, end_ref in zip(pieces, rest):

        def body(block, columns=columns):
            row = (sums[2, :, columns] + rounded_dot(cut[2], block)).astype(jnp.bfloat16)
            query[:, columns] = jnp.maximum(row, 0)

        on_last(columns, inner_ref, end_ref, body)


def read_kernel(stream, parts, query, gain, *rest):
    out, held, sems = rest[-3:]
    copies = []
    for start in range(0, query.shape[0], HEAD_DIM):
        rows = slice(start, start + HEAD_DIM)
        total = sum(part[rows, :].astype(jnp.float32) for part in rest[:parts])
        reading = rounded_dot(total.astype(jnp.bfloat16), query[rows, :])
        scale = lax.rsqrt(jnp.mean(reading * reading, axis=0, keepdims=True) + 1e-06)
        held[rows, :] = (reading * scale * gain[rows, :]).astype(jnp.bfloat16)
        copies.append(pltpu.make_async_copy(held.at[rows, :], out.at[stream, rows, :], sems.at[len(copies)]))
        copies[-1].start()
    for copy in copies:
        copy.wait()


def partner_swap(value, axis):
    return lax.ppermute(value, axis, [(i, i ^ 1) for i in range(lax.axis_size(axis))])


def middle_swap(value, axis, other):
    wide, count = lax.axis_size(other), lax.axis_size(axis)
    pairs = []
    for j in range(wide):
        for i in range(count):
            if i in (1, 2):
                pairs.append((j * count + i, j * count + 3 - i))
            else:
                pairs.append((j * count + i, (j ^ 1 if j ^ 1 < wide else j) * count + i))
    return lax.ppermute(value, (other, axis), pairs)


def from_others(value, axis):
    count = lax.axis_size(axis)
    sent = value.astype(jnp.bfloat16)
    got = []
    for step in range(count - 1, 0, -1):
        pairs = [(i, (i + step) % count) for i in range(count)]
        if count & (count - 1) == 0:
            pairs = [(i, i ^ step) for i in range(count)]
        got.append(lax.ppermute(sent, axis, pairs))
    return got


def entering(value, axis):
    count = lax.axis_size(axis)
    total = lax.ppermute(value, axis, [(i, i + 1) for i in range(count - 1)])
    reach = 1
    while reach < count - 1:
        total = total + lax.ppermute(total, axis, [(i, i + reach) for i in range(count - reach)])
        reach *= 2
    return total


def local(streams, w_query, w_key, w_value, gain):
    count = lax.axis_size("head")
    rows, tokens = streams.shape[2], streams.shape[1]
    width = w_query.shape[1]
    depth = rows * count
    columns = jnp.swapaxes(streams, 1, 2)
    matrices = (w_query.T, w_key.T, w_value.T)
    gain_column = gain.reshape(width, 1)

    one = 2 * width * depth * tokens
    cut = call(
        functools.partial(cut_kernel, count), jax.ShapeDtypeStruct((3, width, rows), jnp.bfloat16), IN_VMEM,
        [IN_VMEM] * 3, [], one // 4,
    )(matrices[1], matrices[2], matrices[0])
    across, far, across_end, far_end = [], [], [], []
    near = partner_swap(columns, "head")
    for stream in range(2):
        across.append(middle_swap(columns[stream], "head", "group"))
    for stream in range(2):
        far.append(middle_swap(near[stream], "head", "group"))
        ready, *_ = lax.optimization_barrier((across[stream], *([cut] if stream else [])))
        across_end.append(partner_swap(ready, "head"))
    whole = pltpu.VMEM((depth, tokens), jnp.bfloat16)
    sems = pltpu.SemaphoreType.DMA((4,))
    query_type = jax.ShapeDtypeStruct((width, tokens), jnp.bfloat16)
    state_type = jax.ShapeDtypeStruct((width, HEAD_DIM), jnp.float32)
    out_type = jax.ShapeDtypeStruct((2, width, tokens), jnp.bfloat16)

    read_scratch = [pltpu.VMEM((width, tokens), jnp.bfloat16), pltpu.SemaphoreType.DMA((width // HEAD_DIM,))]
    most = tokens // 2 if tokens % 256 == 0 else 0
    pieces = ([slice(0, tokens)], [slice(a, b) for a, b in ((0, most), (most, tokens)) if b > a])
    sums = []
    for stream in range(2):
        ready, *_ = lax.optimization_barrier((far[stream], across_end[stream], *sums))
        far_end.append([partner_swap(ready[:, columns], "head") for columns in pieces[stream]])
        sums.append(call(
            functools.partial(partial_kernel, stream), jax.ShapeDtypeStruct((3, width, tokens), jnp.float32), IN_VMEM,
            [ANYWHERE] * 4 + [IN_VMEM] * 3 + [ANYWHERE], [whole, sems], 3 * one,
        )(columns, near, far[stream], across_end[stream], *matrices, cut))
    state_of = lambda stream, piece, before, ties: call(
        functools.partial(state_kernel, pieces[stream][piece], len(before)), state_type, IN_VMEM,
        [IN_VMEM] * (4 + len(before)) + [ANYWHERE] * len(ties), [], one // 2,
    )(across[stream], far_end[stream][piece], cut, sums[stream], *before, *ties)
    prefix = parts = query = out = None
    early = []
    for stream in range(2):
        ties = (sums[1],) if stream == 0 else (parts[0], query)
        state = state_of(stream, len(pieces[stream]) - 1, early, ties)
        query = call(
            functools.partial(query_kernel, pieces[stream]), query_type, IN_VMEM,
            [IN_VMEM] * (3 + len(pieces[stream])) + [ANYWHERE], [], one // 4,
        )(across[stream], *far_end[stream], cut, sums[stream], state)
        parts = [state, *from_others(state, "tok")]
        if stream == 0:
            for piece in range(len(pieces[1]) - 1):
                early = [state_of(1, piece, early, (query,))]
            query, parts, early = lax.optimization_barrier((query, parts, early))
            parts = [sum(part.astype(jnp.float32) for part in parts)]
            prefix = entering(parts[0], "group")
        kept = [] if out is None else [out]
        out = call(
            functools.partial(read_kernel, stream, len(parts) + 1), out_type, ANYWHERE,
            [IN_VMEM] * (3 + len(parts)) + [ANYWHERE] * len(kept),
            read_scratch, one // 20, {3 + len(parts): 0} if kept else None,
        )(query, gain_column, prefix, *parts, *kept)
    return jnp.swapaxes(out, 1, 2)


def solution(mesh):
    return jax.shard_map(
        local,
        mesh=mesh,
        in_specs=(
            P(None, ("group", "tok"), "head"),
            P(None, "head"),
            P(None, "head"),
            P(None, "head"),
            P("head"),
        ),
        out_specs=P(None, ("group", "tok"), "head"),
        check_vma=False,
    )
```

```python
import functools

import jax
import jax.numpy as jnp
from jax import lax
from jax.experimental import pallas as pl
from jax.experimental.pallas import tpu as pltpu
from jax.sharding import PartitionSpec as P

HEAD_DIM = 112
VMEM_LIMIT = 20 * 1024 * 1024
ANYWHERE = pl.BlockSpec(memory_space=pl.ANY)
IN_VMEM = pl.BlockSpec(memory_space=pltpu.VMEM)


def call(body, outs, out_specs, in_specs, scratch, flops, aliases=None):
    return pl.pallas_call(
        body,
        out_shape=outs,
        in_specs=in_specs,
        out_specs=out_specs,
        scratch_shapes=scratch,
        input_output_aliases=aliases or {},
        compiler_params=pltpu.CompilerParams(vmem_limit_bytes=VMEM_LIMIT),
        cost_estimate=pl.CostEstimate(flops=flops // 64, bytes_accessed=1 << 10, transcendentals=0),
    )


def rounded_dot(matrix, block):
    return jnp.dot(matrix, block, preferred_element_type=jnp.float32)


def token_tiles(tokens):
    width = 256 if tokens % 256 == 0 else tokens
    return width, tokens // width


def is_inner(position):
    return (position == 1) | (position == 2)


def load_blocks(found, whole, sems):
    mine = lax.axis_index("head")
    rows = found[0].shape[0]

    def at(flip):
        return whole.at[pl.ds(pl.multiple_of((mine ^ flip) * rows, 16), rows), :]

    for flip, source in enumerate(found):
        if isinstance(source, tuple):
            for want, ref in ((True, source[0]), (False, source[1])):

                @pl.when(is_inner(mine) == want)
                def _(ref=ref, flip=flip):
                    pltpu.make_async_copy(ref, at(flip), sems.at[flip]).start()
        else:
            pltpu.make_async_copy(source, at(flip), sems.at[flip]).start()
    for flip in range(len(found)):
        pltpu.make_async_copy(at(flip), at(flip), sems.at[flip]).wait()


def partial_kernel(stream, own, near, b2i, b2o, wq, wk, wv, tie, sums, whole, sems):
    rows, tokens = b2i.shape
    missing = pl.ds(pl.multiple_of((lax.axis_index("head") ^ 3) * rows, 16), rows)
    whole[missing, :] = jnp.zeros((rows, tokens), whole.dtype)
    load_blocks([own.at[stream], near.at[stream], (b2i, b2o)], whole, sems)
    width, tiles = token_tiles(tokens)

    @pl.loop(0, tiles)
    def _(tile):
        columns = pl.ds(pl.multiple_of(tile * width, width), width)
        block = whole[:, columns]
        for k, matrix in enumerate((wk, wv, wq)):
            sums[k, :, columns] = rounded_dot(matrix[...], block)


def cut_kernel(count, *rest):
    matrices, (cut,) = rest[:-1], rest[-1:]
    rows = cut.shape[2]
    for owner in range(count):

        @pl.when((lax.axis_index("head") ^ 3) == owner)
        def _(owner=owner):
            for k, matrix in enumerate(matrices):
                cut[k] = matrix[:, owner * rows : (owner + 1) * rows]


def on_last(columns, inner_ref, end_ref, body):
    @pl.when(is_inner(lax.axis_index("head")))
    def _():
        body(inner_ref[:, columns])

    @pl.when(jnp.logical_not(is_inner(lax.axis_index("head"))))
    def _():
        body(end_ref[...])


def state_kernel(columns, before, inner_ref, end_ref, cut, sums, *rest):
    state = rest[-1]

    def body(block):
        key = (sums[0, :, columns] + rounded_dot(cut[0], block)).astype(jnp.bfloat16)
        value = (sums[1, :, columns] + rounded_dot(cut[1], block)).astype(jnp.bfloat16)
        key = jnp.maximum(key, 0)
        for start in range(0, key.shape[0], HEAD_DIM):
            rows = slice(start, start + HEAD_DIM)
            total = lax.dot_general(
                value[rows], key[rows], (((1,), (1,)), ((), ())), preferred_element_type=jnp.float32
            )
            state[rows, :] = total + rest[0][rows, :] if before else total

    on_last(columns, inner_ref, end_ref, body)


def query_kernel(pieces, inner_ref, *rest):
    cut, sums, _, query = rest[-4:]
    for columns, end_ref in zip(pieces, rest):

        def body(block, columns=columns):
            row = (sums[2, :, columns] + rounded_dot(cut[2], block)).astype(jnp.bfloat16)
            query[:, columns] = jnp.maximum(row, 0)

        on_last(columns, inner_ref, end_ref, body)


def read_kernel(stream, parts, query, gain, *rest):
    out, held, sems = rest[-3:]
    copies = []
    for start in range(0, query.shape[0], HEAD_DIM):
        rows = slice(start, start + HEAD_DIM)
        total = sum(part[rows, :].astype(jnp.float32) for part in rest[:parts])
        reading = rounded_dot(total.astype(jnp.bfloat16), query[rows, :])
        scale = lax.rsqrt(jnp.mean(reading * reading, axis=0, keepdims=True) + 1e-06)
        held[rows, :] = (reading * scale * gain[rows, :]).astype(jnp.bfloat16)
        copies.append(pltpu.make_async_copy(held.at[rows, :], out.at[stream, rows, :], sems.at[len(copies)]))
        copies[-1].start()
    for copy in copies:
        copy.wait()


def partner_swap(value, axis):
    return lax.ppermute(value, axis, [(i, i ^ 1) for i in range(lax.axis_size(axis))])


def middle_swap(value, axis, other):
    wide, count = lax.axis_size(other), lax.axis_size(axis)
    pairs = []
    for j in range(wide):
        for i in range(count):
            if i in (1, 2):
                pairs.append((j * count + i, j * count + 3 - i))
            else:
                pairs.append((j * count + i, (j ^ 1 if j ^ 1 < wide else j) * count + i))
    return lax.ppermute(value, (other, axis), pairs)


def from_others(value, axis):
    count = lax.axis_size(axis)
    sent = value.astype(jnp.bfloat16)
    got = []
    for step in range(count - 1, 0, -1):
        pairs = [(i, (i + step) % count) for i in range(count)]
        if count & (count - 1) == 0:
            pairs = [(i, i ^ step) for i in range(count)]
        got.append(lax.ppermute(sent, axis, pairs))
    return got


def entering(value, axis):
    count = lax.axis_size(axis)
    total = lax.ppermute(value, axis, [(i, i + 1) for i in range(count - 1)])
    reach = 1
    while reach < count - 1:
        total = total + lax.ppermute(total, axis, [(i, i + reach) for i in range(count - reach)])
        reach *= 2
    return total


def local(streams, w_query, w_key, w_value, gain):
    count = lax.axis_size("head")
    rows, tokens = streams.shape[2], streams.shape[1]
    width = w_query.shape[1]
    depth = rows * count
    columns = jnp.swapaxes(streams, 1, 2)
    matrices = (w_query.T, w_key.T, w_value.T)
    gain_column = gain.reshape(width, 1)

    one = 2 * width * depth * tokens
    cut = call(
        functools.partial(cut_kernel, count), jax.ShapeDtypeStruct((3, width, rows), jnp.bfloat16), IN_VMEM,
        [IN_VMEM] * 3, [], one // 4,
    )(matrices[1], matrices[2], matrices[0])
    across, far, across_end, far_end = [], [], [], []
    near = partner_swap(columns, "head")
    for stream in range(2):
        across.append(middle_swap(columns[stream], "head", "group"))
    for stream in range(2):
        far.append(middle_swap(near[stream], "head", "group"))
        ready, *_ = lax.optimization_barrier((across[stream], *([cut] if stream else [])))
        across_end.append(partner_swap(ready, "head"))
    whole = pltpu.VMEM((depth, tokens), jnp.bfloat16)
    sems = pltpu.SemaphoreType.DMA((4,))
    query_type = jax.ShapeDtypeStruct((width, tokens), jnp.bfloat16)
    state_type = jax.ShapeDtypeStruct((width, HEAD_DIM), jnp.float32)
    out_type = jax.ShapeDtypeStruct((2, width, tokens), jnp.bfloat16)

    read_scratch = [pltpu.VMEM((width, tokens), jnp.bfloat16), pltpu.SemaphoreType.DMA((width // HEAD_DIM,))]
    most = tokens // 2 if tokens % 256 == 0 else 0
    pieces = [[slice(a, b) for a, b in ((0, most), (most, tokens)) if b > a]] * 2
    sums = []
    for stream in range(2):
        ready, *_ = lax.optimization_barrier((far[stream], across_end[stream], *sums))
        far_end.append([partner_swap(ready[:, columns], "head") for columns in pieces[stream]])
        sums.append(call(
            functools.partial(partial_kernel, stream), jax.ShapeDtypeStruct((3, width, tokens), jnp.float32), IN_VMEM,
            [ANYWHERE] * 4 + [IN_VMEM] * 3 + [ANYWHERE], [whole, sems], 3 * one,
        )(columns, near, far[stream], across_end[stream], *matrices, cut))
    state_of = lambda stream, piece, before, ties: call(
        functools.partial(state_kernel, pieces[stream][piece], len(before)), state_type, IN_VMEM,
        [IN_VMEM] * (4 + len(before)) + [ANYWHERE] * len(ties), [], one // 2,
    )(across[stream], far_end[stream][piece], cut, sums[stream], *before, *ties)
    prefix = parts = query = out = None
    early = []
    for piece in range(len(pieces[0]) - 1):
        early = [state_of(0, piece, early, (sums[1],))]
    for stream in range(2):
        ties = (sums[1],) if stream == 0 else (parts[0], query)
        state = state_of(stream, len(pieces[stream]) - 1, early, ties)
        query = call(
            functools.partial(query_kernel, pieces[stream]), query_type, IN_VMEM,
            [IN_VMEM] * (3 + len(pieces[stream])) + [ANYWHERE], [], one // 4,
        )(across[stream], *far_end[stream], cut, sums[stream], state)
        parts = [state, *from_others(state, "tok")]
        if stream == 0:
            early = []
            for piece in range(len(pieces[1]) - 1):
                early = [state_of(1, piece, early, (query,))]
            query, parts, early = lax.optimization_barrier((query, parts, early))
            parts = [sum(part.astype(jnp.float32) for part in parts)]
            prefix = entering(parts[0], "group")
        kept = [] if out is None else [out]
        out = call(
            functools.partial(read_kernel, stream, len(parts) + 1), out_type, ANYWHERE,
            [IN_VMEM] * (3 + len(parts)) + [ANYWHERE] * len(kept),
            read_scratch, one // 20, {3 + len(parts): 0} if kept else None,
        )(query, gain_column, prefix, *parts, *kept)
    return jnp.swapaxes(out, 1, 2)


def solution(mesh):
    return jax.shard_map(
        local,
        mesh=mesh,
        in_specs=(
            P(None, ("group", "tok"), "head"),
            P(None, "head"),
            P(None, "head"),
            P(None, "head"),
            P("head"),
        ),
        out_specs=P(None, ("group", "tok"), "head"),
        check_vma=False,
    )
```

```python
import functools

import jax
import jax.numpy as jnp
from jax import lax
from jax.experimental import pallas as pl
from jax.experimental.pallas import tpu as pltpu
from jax.sharding import PartitionSpec as P

HEAD_DIM = 112
VMEM_LIMIT = 20 * 1024 * 1024
ANYWHERE = pl.BlockSpec(memory_space=pl.ANY)
IN_VMEM = pl.BlockSpec(memory_space=pltpu.VMEM)


def call(body, outs, out_specs, in_specs, scratch, flops, aliases=None):
    return pl.pallas_call(
        body,
        out_shape=outs,
        in_specs=in_specs,
        out_specs=out_specs,
        scratch_shapes=scratch,
        input_output_aliases=aliases or {},
        compiler_params=pltpu.CompilerParams(vmem_limit_bytes=VMEM_LIMIT),
        cost_estimate=pl.CostEstimate(flops=flops // 64, bytes_accessed=1 << 10, transcendentals=0),
    )


def rounded_dot(matrix, block):
    return jnp.dot(matrix, block, preferred_element_type=jnp.float32)


def token_tiles(tokens):
    width = 256 if tokens % 256 == 0 else tokens
    return width, tokens // width


def is_inner(position):
    return (position == 1) | (position == 2)


def load_blocks(found, whole, sems):
    mine = lax.axis_index("head")
    rows = found[0].shape[0]

    def at(flip):
        return whole.at[pl.ds(pl.multiple_of((mine ^ flip) * rows, 16), rows), :]

    for flip, source in enumerate(found):
        if isinstance(source, tuple):
            for want, ref in ((True, source[0]), (False, source[1])):

                @pl.when(is_inner(mine) == want)
                def _(ref=ref, flip=flip):
                    pltpu.make_async_copy(ref, at(flip), sems.at[flip]).start()
        else:
            pltpu.make_async_copy(source, at(flip), sems.at[flip]).start()
    for flip in range(len(found)):
        pltpu.make_async_copy(at(flip), at(flip), sems.at[flip]).wait()


def partial_kernel(stream, own, near, b2i, b2o, wq, wk, wv, tie, sums, whole, sems):
    rows, tokens = b2i.shape
    missing = pl.ds(pl.multiple_of((lax.axis_index("head") ^ 3) * rows, 16), rows)
    whole[missing, :] = jnp.zeros((rows, tokens), whole.dtype)
    load_blocks([own.at[stream], near.at[stream], (b2i, b2o)], whole, sems)
    width, tiles = token_tiles(tokens)

    @pl.loop(0, tiles)
    def _(tile):
        columns = pl.ds(pl.multiple_of(tile * width, width), width)
        block = whole[:, columns]
        for k, matrix in enumerate((wk, wv, wq)):
            sums[k, :, columns] = rounded_dot(matrix[...], block)


def cut_kernel(count, *rest):
    matrices, (cut,) = rest[:-1], rest[-1:]
    rows = cut.shape[2]
    for owner in range(count):

        @pl.when((lax.axis_index("head") ^ 3) == owner)
        def _(owner=owner):
            for k, matrix in enumerate(matrices):
                cut[k] = matrix[:, owner * rows : (owner + 1) * rows]


def on_last(columns, inner_ref, end_ref, body):
    @pl.when(is_inner(lax.axis_index("head")))
    def _():
        body(inner_ref[:, columns])

    @pl.when(jnp.logical_not(is_inner(lax.axis_index("head"))))
    def _():
        body(end_ref[...])


def state_kernel(columns, before, inner_ref, end_ref, cut, sums, *rest):
    state = rest[-1]

    def body(block):
        key = (sums[0, :, columns] + rounded_dot(cut[0], block)).astype(jnp.bfloat16)
        value = (sums[1, :, columns] + rounded_dot(cut[1], block)).astype(jnp.bfloat16)
        key = jnp.maximum(key, 0)
        for start in range(0, key.shape[0], HEAD_DIM):
            rows = slice(start, start + HEAD_DIM)
            total = lax.dot_general(
                value[rows], key[rows], (((1,), (1,)), ((), ())), preferred_element_type=jnp.float32
            )
            state[rows, :] = total + rest[0][rows, :] if before else total

    on_last(columns, inner_ref, end_ref, body)


def query_kernel(pieces, inner_ref, *rest):
    cut, sums, _, query = rest[-4:]
    for columns, end_ref in zip(pieces, rest):

        def body(block, columns=columns):
            row = (sums[2, :, columns] + rounded_dot(cut[2], block)).astype(jnp.bfloat16)
            query[:, columns] = jnp.maximum(row, 0)

        on_last(columns, inner_ref, end_ref, body)


def read_kernel(stream, parts, query, gain, *rest):
    out, held, sems = rest[-3:]
    copies = []
    for start in range(0, query.shape[0], HEAD_DIM):
        rows = slice(start, start + HEAD_DIM)
        total = sum(part[rows, :].astype(jnp.float32) for part in rest[:parts])
        reading = rounded_dot(total.astype(jnp.bfloat16), query[rows, :])
        scale = lax.rsqrt(jnp.mean(reading * reading, axis=0, keepdims=True) + 1e-06)
        held[rows, :] = (reading * scale * gain[rows, :]).astype(jnp.bfloat16)
        copies.append(pltpu.make_async_copy(held.at[rows, :], out.at[stream, rows, :], sems.at[len(copies)]))
        copies[-1].start()
    for copy in copies:
        copy.wait()


def partner_swap(value, axis):
    return lax.ppermute(value, axis, [(i, i ^ 1) for i in range(lax.axis_size(axis))])


def middle_swap(value, axis, other):
    wide, count = lax.axis_size(other), lax.axis_size(axis)
    pairs = []
    for j in range(wide):
        for i in range(count):
            if i in (1, 2):
                pairs.append((j * count + i, j * count + 3 - i))
            else:
                pairs.append((j * count + i, (j ^ 1 if j ^ 1 < wide else j) * count + i))
    return lax.ppermute(value, (other, axis), pairs)


def from_others(value, axis):
    count = lax.axis_size(axis)
    sent = value.astype(jnp.bfloat16)
    got = []
    for step in (count - 1, *range(1, count - 1)):
        pairs = [(i, (i + step) % count) for i in range(count)]
        if count & (count - 1) == 0:
            pairs = [(i, i ^ step) for i in range(count)]
        got.append(lax.ppermute(sent, axis, pairs))
    return got


def entering(value, axis):
    count = lax.axis_size(axis)
    total = lax.ppermute(value, axis, [(i, i + 1) for i in range(count - 1)])
    reach = 1
    while reach < count - 1:
        total = total + lax.ppermute(total, axis, [(i, i + reach) for i in range(count - reach)])
        reach *= 2
    return total


def local(streams, w_query, w_key, w_value, gain):
    count = lax.axis_size("head")
    rows, tokens = streams.shape[2], streams.shape[1]
    width = w_query.shape[1]
    depth = rows * count
    columns = jnp.swapaxes(streams, 1, 2)
    matrices = (w_query.T, w_key.T, w_value.T)
    gain_column = gain.reshape(width, 1)

    one = 2 * width * depth * tokens
    cut = call(
        functools.partial(cut_kernel, count), jax.ShapeDtypeStruct((3, width, rows), jnp.bfloat16), IN_VMEM,
        [IN_VMEM] * 3, [], one // 4,
    )(matrices[1], matrices[2], matrices[0])
    across, far, across_end, far_end = [], [], [], []
    near = partner_swap(columns, "head")
    for stream in range(2):
        across.append(middle_swap(columns[stream], "head", "group"))
    for stream in range(2):
        far.append(middle_swap(near[stream], "head", "group"))
        ready, *_ = lax.optimization_barrier((across[stream], *([cut] if stream else [])))
        across_end.append(partner_swap(ready, "head"))
    whole = pltpu.VMEM((depth, tokens), jnp.bfloat16)
    sems = pltpu.SemaphoreType.DMA((4,))
    query_type = jax.ShapeDtypeStruct((width, tokens), jnp.bfloat16)
    state_type = jax.ShapeDtypeStruct((width, HEAD_DIM), jnp.float32)
    out_type = jax.ShapeDtypeStruct((2, width, tokens), jnp.bfloat16)

    read_scratch = [pltpu.VMEM((width, tokens), jnp.bfloat16), pltpu.SemaphoreType.DMA((width // HEAD_DIM,))]
    most = tokens // 2 if tokens % 256 == 0 else 0
    pieces = [[slice(a, b) for a, b in ((0, most), (most, tokens)) if b > a]] * 2
    sums = []
    for stream in range(2):
        ready, *_ = lax.optimization_barrier((far[stream], across_end[stream], *sums))
        far_end.append([partner_swap(ready[:, columns], "head") for columns in pieces[stream]])
        sums.append(call(
            functools.partial(partial_kernel, stream), jax.ShapeDtypeStruct((3, width, tokens), jnp.float32), IN_VMEM,
            [ANYWHERE] * 4 + [IN_VMEM] * 3 + [ANYWHERE], [whole, sems], 3 * one,
        )(columns, near, far[stream], across_end[stream], *matrices, cut))
    state_of = lambda stream, piece, before, ties: call(
        functools.partial(state_kernel, pieces[stream][piece], len(before)), state_type, IN_VMEM,
        [IN_VMEM] * (4 + len(before)) + [ANYWHERE] * len(ties), [], one // 2,
    )(across[stream], far_end[stream][piece], cut, sums[stream], *before, *ties)
    prefix = parts = query = out = None
    early = []
    for piece in range(len(pieces[0]) - 1):
        early = [state_of(0, piece, early, (sums[1],))]
    for stream in range(2):
        ties = (sums[1],) if stream == 0 else (parts[0], query)
        state = state_of(stream, len(pieces[stream]) - 1, early, ties)
        query = call(
            functools.partial(query_kernel, pieces[stream]), query_type, IN_VMEM,
            [IN_VMEM] * (3 + len(pieces[stream])) + [ANYWHERE], [], one // 4,
        )(across[stream], *far_end[stream], cut, sums[stream], state)
        parts = [state, *from_others(state, "tok")]
        if stream == 0:
            early = []
            for piece in range(len(pieces[1]) - 1):
                early = [state_of(1, piece, early, (query,))]
            query, parts, early = lax.optimization_barrier((query, parts, early))
            parts = [sum(part.astype(jnp.float32) for part in parts)]
            prefix = entering(parts[0], "group")
        kept = [] if out is None else [out]
        out = call(
            functools.partial(read_kernel, stream, len(parts) + 1), out_type, ANYWHERE,
            [IN_VMEM] * (3 + len(parts)) + [ANYWHERE] * len(kept),
            read_scratch, one // 20, {3 + len(parts): 0} if kept else None,
        )(query, gain_column, prefix, *parts, *kept)
    return jnp.swapaxes(out, 1, 2)


def solution(mesh):
    return jax.shard_map(
        local,
        mesh=mesh,
        in_specs=(
            P(None, ("group", "tok"), "head"),
            P(None, "head"),
            P(None, "head"),
            P(None, "head"),
            P("head"),
        ),
        out_specs=P(None, ("group", "tok"), "head"),
        check_vma=False,
    )
```
